128 devices in a mesh: seq: 16 (over y, z), exp: 8 (over x, core).
Axes of the slice: x: 4, y: 4, z: 4, core: 2. Of those that a mesh axis runs over, the one named last changes fastest.
Arguments:
- grad_out: bfloat16 [16384, 8192], P(('seq', 'exp')), may hold values from -6 to 6
- hidden: bfloat16 [16384, 8192], P(('seq', 'exp')), may hold values from -6 to 6
- norm_gain: float32 [8192], replicated, may hold values from 0.5 to 1.5
- router_logits: float32 [16384, 16], P(('seq', 'exp')), may hold values from -15 to 410
- router_weight: float32 [16, 8192], replicated, may hold values from -3 to 3
- expert_ids: int32 [16384, 2], P(('seq', 'exp')), may hold values from 0 to 15, as said below
- expert_grad: bfloat16 [16, 16, 192, 8192], P('seq', 'exp'), may hold values from -6 to 6
- expert_out: bfloat16 [16, 16, 192, 8192], P('seq', 'exp'), may hold values from -0.0625 to 0.0625
Outputs:
- grad_hidden: bfloat16 [16384, 8192], P(('seq', 'exp'))
- router_grad: float32 [16, 8192], replicated
The draws below stay inside these ranges and needn't reach their ends.
Inputs may be any that keep to these rules, and one draw needn't show every extreme that they name: `expert_ids`: among the rows of one device, no expert is named by more than 24 entries, and some expert is named by exactly 24; the 2 experts of a row differ; every expert is named somewhere. Slots that no token uses hold values that no output reads.
All inputs are finite; a program needn't handle non-finite values.
Results may differ from the reference program's by a relative error of at most 0.0027.
Values may be sent and summed in bfloat16 or wider, within the bound.
No kernel may reach another device: no remote copies, remote signals or barrier semaphores. Data moves between devices by JAX's collectives and lax.ppermute only.
A program may use at most 128 MiB of HBM per device.

```python
import math
import jax
import jax.numpy as jnp
from jax import lax

D = 8192
EXPERTS = 16
TOP = 2
TOK_DEV = 128
TOKENS = 16384
CAP = 24
SLOTS = 192
SEQ_GROUPS = 16
N_SEQ = 16
N_EXP = 8


def draw_router_logits(key, part):
    key_base = jax.random.fold_in(key, 0)
    values = jnp.clip(3.0 * jax.random.normal(key_base, (TOKENS, EXPERTS), jnp.float32), -15.0, 15.0)
    return values


def draw_expert_ids(key, part):
    key = jax.random.fold_in(key, 7)
    blocks = TOKENS // TOK_DEV
    unit_rows = TOK_DEV // 32
    profile = jnp.array([2, 2, 3, 3, 3, 4, 4, 4, 4, 4, 4, 5, 5, 5, 6, 6], jnp.int32)
    key_rank, key_blocks = jax.random.split(key)
    ranking = jax.random.permutation(key_rank, EXPERTS).astype(jnp.int32)

    def one_block(block):
        block_key = jax.random.fold_in(key_blocks, block)
        key_off, key_flip, key_rows = jax.random.split(block_key, 3)
        offset = jax.random.randint(key_off, (), 0, 4, jnp.int32)
        by_rank = profile[(jnp.arange(EXPERTS, dtype=jnp.int32) + offset) % EXPERTS] * unit_rows
        by_expert = jnp.zeros((EXPERTS,), jnp.int32).at[ranking].set(by_rank)
        entries = jnp.repeat(jnp.arange(EXPERTS, dtype=jnp.int32), by_expert, total_repeat_length=2 * TOK_DEV)
        paired = jnp.stack([entries[:TOK_DEV], entries[TOK_DEV:]], axis=1)
        flips = jax.random.randint(key_flip, (TOK_DEV, 1), 0, 2, jnp.int32)
        paired = jnp.where(flips == 1, paired[:, ::-1], paired)
        order = jax.random.permutation(key_rows, TOK_DEV)
        return paired[order]
    chosen = jax.lax.map(one_block, jnp.arange(blocks, dtype=jnp.int32))
    return chosen.reshape(TOKENS, TOP).astype(jnp.int32)


def shard_levels(rng, dims, cuts, least, top_value):
    factor_of, own = 1.0, jax.random.fold_in(rng, 6)
    for axis_at, shards_of in cuts:
        steps = jnp.exp(jax.random.uniform(jax.random.fold_in(own, axis_at), (shards_of,), jnp.float32, least / len(cuts), top_value / len(cuts)))
        factor_of = factor_of * jnp.repeat(steps, dims[axis_at] // shards_of).reshape([-1 if axis == axis_at else 1 for axis in range(len(dims))])
    return factor_of


def gaussian(stream_key, shape, width, limit, cuts=(), kind=jnp.bfloat16):
    values = width * jax.random.normal(stream_key, shape, jnp.float32)
    if cuts:
        values = values * shard_levels(stream_key, shape, cuts, -0.22, 0.18)
    return jnp.clip(values, -limit, limit).astype(kind)


def setup_inputs(seed: int = 0) -> dict:
    arg_keys = jax.random.split(jax.random.key(seed), 9)
    return {
        "grad_out": gaussian(arg_keys[0], (TOKENS, D), 1.0, 6.0, ((0, 128),)),
        "hidden": gaussian(arg_keys[1], (TOKENS, D), 1.0, 6.0, ((0, 128),)),
        "norm_gain": jnp.clip(1.0 + 0.1 * jax.random.normal(arg_keys[2], (D,), jnp.float32), 0.5, 1.5),
        "router_logits": draw_router_logits(jax.random.fold_in(arg_keys[8], 71), 0),
        "router_weight": gaussian(arg_keys[4], (EXPERTS, D), 0.5, 3.0, (), jnp.float32),
        "expert_ids": draw_expert_ids(jax.random.fold_in(arg_keys[8], 71), 0),
        "expert_grad": gaussian(arg_keys[6], (SEQ_GROUPS, EXPERTS, SLOTS, D), 1.0, 6.0, ((0, 16), (1, 8))),
        "expert_out": gaussian(arg_keys[7], (SEQ_GROUPS, EXPERTS, SLOTS, D), D ** -0.5, 0.0625, ((0, 16), (1, 8))),
    }


def reference(grad_out, hidden, norm_gain, router_logits, router_weight, expert_ids, expert_grad, expert_out):
    labels = jnp.arange(EXPERTS, dtype=jnp.int32)
    counts = lax.optimization_barrier(jnp.sum((expert_ids[:, :, None] == labels).astype(jnp.int32), axis=(0, 1)))
    expert_load = EXPERTS * counts.astype(jnp.float32) / (TOP * TOKENS)
    flat_grad = expert_grad.reshape(N_SEQ * EXPERTS * SLOTS, D)
    flat_out = expert_out.reshape(N_SEQ * EXPERTS * SLOTS, D)

    def one_device(device):
        start = (device * TOK_DEV).astype(jnp.int32)
        upstream = lax.dynamic_slice_in_dim(grad_out, start, TOK_DEV, 0)
        resid = lax.dynamic_slice_in_dim(hidden, start, TOK_DEV, 0)
        logits = lax.dynamic_slice_in_dim(router_logits, start, TOK_DEV, 0)
        chosen_ids = lax.dynamic_slice_in_dim(expert_ids, start, TOK_DEV, 0)
        onehot = (chosen_ids[:, :, None] == labels).astype(jnp.int32).reshape(TOK_DEV * TOP, EXPERTS)
        ranks = jnp.cumsum(onehot, axis=0) - onehot
        slot_index = lax.optimization_barrier(jnp.sum(onehot * ranks, axis=1)).reshape(TOK_DEV, TOP)
        seq_index = device // N_EXP
        peer = device % N_EXP
        row_index = ((seq_index * EXPERTS + chosen_ids) * SLOTS + peer * CAP + slot_index).reshape(-1).astype(jnp.int32)
        picked_grad = jnp.take(flat_grad, row_index, axis=0).reshape(TOK_DEV, TOP, D)
        picked_out = jnp.take(flat_out, row_index, axis=0).reshape(TOK_DEV, TOP, D)
        dots_full = jnp.einsum('td,tkd->tk', upstream.astype(jnp.float32), picked_out.astype(jnp.float32))
        gate_dots = lax.optimization_barrier(dots_full.astype(jnp.bfloat16)).astype(jnp.float32)
        chosen = jnp.take_along_axis(logits, chosen_ids, axis=1)
        gate_weights = jax.nn.softmax(chosen, axis=-1)
        combined = jnp.zeros((TOK_DEV, D), jnp.float32)
        for k in range(TOP):
            combined = combined + gate_weights[:, k:k + 1] * picked_grad[:, k].astype(jnp.float32)
        chosen_grad = gate_weights * (gate_dots - lax.optimization_barrier(jnp.sum(gate_weights * gate_dots, axis=1, keepdims=True)))
        direct_grad = lax.optimization_barrier(jnp.sum(chosen_grad[:, :, None] * (chosen_ids[:, :, None] == labels).astype(jnp.float32), axis=1))
        router_probs = jax.nn.softmax(logits, axis=-1)
        aux_grad = router_probs * (expert_load - lax.optimization_barrier(jnp.sum(router_probs * expert_load, axis=1, keepdims=True)))
        logit_grad = direct_grad + aux_grad
        normed_grad = combined + jnp.dot(logit_grad, router_weight, precision=lax.Precision.HIGHEST)
        resid_f = resid.astype(jnp.float32)
        inv_rms = lax.rsqrt(lax.optimization_barrier(jnp.mean(resid_f * resid_f, axis=1, keepdims=True)) + 1e-05)
        normed = resid_f * inv_rms
        scaled = norm_gain * normed_grad
        back = inv_rms * (scaled - normed * lax.optimization_barrier(jnp.mean(normed * scaled, axis=1, keepdims=True)))
        routed_in = norm_gain * normed
        partial_router = lax.dot_general(logit_grad, routed_in, (((0,), (0,)), ((), ())), precision=lax.Precision.HIGHEST)
        return ((upstream.astype(jnp.float32) + back).astype(jnp.bfloat16), partial_router)
    blocks, partials = lax.map(one_device, jnp.arange(N_SEQ * N_EXP, dtype=jnp.int32))
    grad_hidden = blocks.reshape(TOKENS, D)
    router_grad = lax.optimization_barrier(jnp.sum(partials, axis=0)) / math.sqrt(TOKENS)
    return (grad_hidden, router_grad)
```

```python
import jax
import jax.numpy as jnp
from jax import lax
from jax.experimental import pallas as pl
from jax.experimental.pallas import tpu as pltpu
from jax.sharding import PartitionSpec as P

D = 8192
EXPERTS = 16
TOK = 128
CAP = 24
ROWS = 2 * CAP
TOKENS = 16384
AXES = ("seq", "exp")
WINDOW = 4
CHUNK = 1024
F32 = jnp.float32
BF16 = jnp.bfloat16
VMEM = pl.BlockSpec(memory_space=pltpu.VMEM)

ROUTES = ((0, 0), (1, 0), (3, 0), (2, 0), (1, 1), (3, 1), (2, 1), (0, 1))


def coords():
    s, e = lax.axis_index("seq"), lax.axis_index("exp")
    return {"y": s >> 2, "z": s & 3, "x": e >> 1, "c": e & 1}


STRIDE = {"y": 32, "z": 8, "x": 2, "c": 1}
SIZE = {"y": 4, "z": 4, "x": 4, "c": 2}


def shift_perm(axis, d):
    out = []
    for i in range(128):
        a = (i // STRIDE[axis]) % SIZE[axis]
        out.append((i, i + ((a + d) % SIZE[axis] - a) * STRIDE[axis]))
    return out


def xor_perm(axis, d):
    return [(i, i ^ (d * STRIDE[axis])) for i in range(128)]


def after(x, *deps):
    out = lax.optimization_barrier((x,) + deps)
    return out[0], out[1:]


def split3(v):
    a = v.astype(BF16)
    r = v - a.astype(F32)
    b = r.astype(BF16)
    c = (r - b.astype(F32)).astype(BF16)
    return a, b, c


def pre_kernel(ids_ref, logits_ref, hidden_ref, pack_ref, probs_ref, counts_ref):
    ids = ids_ref[...]
    logits = logits_ref[...]
    labels = lax.broadcasted_iota(jnp.int32, (TOK, EXPERTS), 1)
    oh = [(ids[:, k : k + 1] == labels).astype(F32) for k in range(2)]
    both = oh[0] + oh[1]
    row = lax.broadcasted_iota(jnp.int32, (TOK, TOK), 0)
    col = lax.broadcasted_iota(jnp.int32, (TOK, TOK), 1)
    before = (row > col).astype(F32).astype(BF16)
    ranks = jnp.dot(before, both.astype(BF16), preferred_element_type=F32)
    counts_ref[...] = jnp.broadcast_to(jnp.sum(both, axis=0, keepdims=True), (8, EXPERTS))
    index = [
        jnp.sum(oh[k] * (ranks + (CAP * labels).astype(F32)), axis=1, keepdims=True)
        for k in range(2)
    ]
    chosen = [jnp.sum(oh[k] * logits, axis=1, keepdims=True) for k in range(2)]
    top = jnp.maximum(chosen[0], chosen[1])
    w = [jnp.exp(c - top) for c in chosen]
    total = w[0] + w[1]
    e = jnp.exp(logits - jnp.max(logits, axis=1, keepdims=True))
    probs_ref[...] = e / jnp.sum(e, axis=1, keepdims=True)
    square = jnp.zeros((TOK, 128), F32)
    for c in range(D // CHUNK):
        h = hidden_ref[:, c * CHUNK : (c + 1) * CHUNK].astype(F32)
        h = h * h
        for j in range(CHUNK // 128):
            square = square + h[:, j * 128 : (j + 1) * 128]
    inv = lax.rsqrt(jnp.sum(square, axis=1, keepdims=True) / D + 1e-05)
    lane = lax.broadcasted_iota(jnp.int32, (TOK, 8), 1)
    pack = jnp.zeros((TOK, 8), F32)
    for i, v in enumerate((w[0] / total, w[1] / total, index[0], index[1], inv)):
        pack = jnp.where(lane == i, v, pack)
    pack_ref[...] = pack


def mid_kernel(
    slots_ref, pack_ref, ids_ref, probs_ref, counts_ref, gain_ref, hidden_ref, grad_ref, *refs
):
    blocks, (logit_ref, partial_ref) = refs[:8], refs[8:]
    pack = pack_ref[...]
    gate = [pack[:, 0:1], pack[:, 1:2]]
    inv = pack[:, 4:5]
    dots = jnp.zeros((TOK, 8 * ROWS), F32)
    for c in range(D // CHUNK):
        cols = slice(c * CHUNK, (c + 1) * CHUNK)
        picked = jnp.concatenate([b[:, cols] for b in blocks], axis=0)
        dots = dots + lax.dot_general(
            grad_ref[:, cols], picked, (((1,), (1,)), ((), ())), preferred_element_type=F32
        )
    slots = slots_ref[...]
    gate_dot = [
        jnp.sum(jnp.where(slots == pack[:, 2 + k : 3 + k], dots, 0.0), axis=1, keepdims=True)
        .astype(BF16)
        .astype(F32)
        for k in range(2)
    ]
    mean = gate[0] * gate_dot[0] + gate[1] * gate_dot[1]
    ids = ids_ref[...]
    labels = lax.broadcasted_iota(jnp.int32, (TOK, EXPERTS), 1)
    direct = jnp.zeros((TOK, EXPERTS), F32)
    for k in range(2):
        chosen = gate[k] * (gate_dot[k] - mean)
        direct = direct + jnp.where(ids[:, k : k + 1] == labels, chosen, 0.0)
    probs = probs_ref[...]
    load = counts_ref[0:1, :] * (EXPERTS / (2 * TOKENS))
    aux = probs * (load - jnp.sum(probs * load, axis=1, keepdims=True))
    logit = direct + aux
    logit_ref[...] = logit
    left = jnp.concatenate(split3(logit * inv), axis=1)
    for c in range(D // CHUNK):
        cols = slice(c * CHUNK, (c + 1) * CHUNK)
        p = lax.dot_general(
            left, hidden_ref[:, cols], (((0,), (0,)), ((), ())), preferred_element_type=F32
        )
        p = p[0:16] + p[16:32] + p[32:48]
        partial_ref[:, cols] = p * (gain_ref[:, cols] * (1.0 / 128.0))


def last_kernel(
    slots_ref, pack_ref, logit_ref, weight_ref, gain_ref, hidden_ref, grad_ref, *refs
):
    blocks, out_ref, scaled_ref = refs[:8], refs[8], refs[9]
    pack = pack_ref[...]
    inv = pack[:, 4:5]
    slots = slots_ref[...]
    w = jnp.where(slots == pack[:, 2:3], pack[:, 0:1], 0.0)
    w = w + jnp.where(slots == pack[:, 3:4], pack[:, 1:2], 0.0)
    w_hi, w_lo, _ = split3(w)
    l0, l1, l2 = split3(logit_ref[...])
    zero = jnp.zeros_like(l0)
    left = jnp.concatenate(
        [
            jnp.concatenate([w_hi, l0, l0, l0, l2], axis=1),
            jnp.concatenate([w_lo, l1, l1, zero, zero], axis=1),
        ],
        axis=0,
    )
    acc = jnp.zeros((TOK, 128), F32)
    for c in range(D // CHUNK):
        cols = slice(c * CHUNK, (c + 1) * CHUNK)
        r0, r1, r2 = split3(weight_ref[:, cols])
        right = jnp.concatenate([b[:, cols] for b in blocks] + [r0, r1, r2, r0], axis=0)
        both = jnp.dot(left, right, preferred_element_type=F32)
        scaled = (both[:TOK] + both[TOK:]) * gain_ref[:, cols]
        scaled_ref[:, cols] = scaled
        prod = scaled * hidden_ref[:, cols].astype(F32)
        for j in range(CHUNK // 128):
            acc = acc + prod[:, j * 128 : (j + 1) * 128]
    mean = jnp.sum(acc, axis=1, keepdims=True) * inv / D
    factor = inv * mean
    for c in range(D // CHUNK):
        cols = slice(c * CHUNK, (c + 1) * CHUNK)
        back = inv * (scaled_ref[:, cols] - hidden_ref[:, cols].astype(F32) * factor)
        out_ref[:, cols] = (grad_ref[:, cols].astype(F32) + back).astype(BF16)


def params(mib):
    return pltpu.CompilerParams(vmem_limit_bytes=mib * 1024 * 1024)


def reduce_all(v, at):
    v = v.reshape(1024, 128)
    for axis in ("y", "z"):
        v = v.reshape((4, v.shape[0] // 4, 128))
        me = at[axis]
        got = [
            lax.ppermute(
                lax.dynamic_index_in_dim(v, (me + d) & 3, 0, keepdims=False),
                AXES,
                shift_perm(axis, d),
            )
            for d in (1, 3, 2)
        ]
        v = lax.dynamic_index_in_dim(v, me, 0, keepdims=False) + got[0] + got[1] + got[2]
    for axis, d in (("c", 1), ("x", 1), ("x", 2)):
        v = v + lax.ppermute(v, AXES, xor_perm(axis, d))
    for axis in ("z", "y"):
        me = at[axis]
        parts = [v] + [lax.ppermute(v, AXES, shift_perm(axis, d)) for d in (1, 2, 3)]
        full = jnp.zeros((4,) + v.shape, F32)
        for d, part in enumerate(parts):
            full = lax.dynamic_update_index_in_dim(full, part, (me - d) & 3, 0)
        v = full.reshape(4 * v.shape[0], 128)
    return v.reshape(EXPERTS, D)


def body(
    grad_out, hidden, norm_gain, router_logits, router_weight, expert_ids, expert_grad, expert_out
):
    at = coords()
    gain = norm_gain.reshape(1, D)
    sources = [((at["x"] - s) & 3) * 2 + (at["c"] ^ m) for s, m in ROUTES]
    base = jnp.stack(sources).astype(F32) * ROWS
    slots = (base[:, None] + jnp.arange(ROWS, dtype=F32)[None, :]).reshape(1, 8 * ROWS)

    pack, probs, counts = pl.pallas_call(
        pre_kernel,
        out_shape=(
            jax.ShapeDtypeStruct((TOK, 8), F32),
            jax.ShapeDtypeStruct((TOK, EXPERTS), F32),
            jax.ShapeDtypeStruct((8, EXPERTS), F32),
        ),
        in_specs=[VMEM] * 3,
        out_specs=(VMEM,) * 3,
        compiler_params=params(16),
    )(expert_ids, router_logits, hidden)
    for axis, d in (("y", 1), ("y", 2), ("z", 1), ("z", 2), ("c", 1), ("x", 1), ("x", 2)):
        counts = counts + lax.ppermute(counts, AXES, xor_perm(axis, d))

    moved = []
    for array in (expert_out, expert_grad):
        for s, m in ROUTES[1:]:
            n = len(moved)
            if n >= WINDOW:
                array, (moved[n - WINDOW],) = after(array, moved[n - WINDOW])
            to = ((at["x"] + s) & 3) * 2 + (at["c"] ^ m)
            block = lax.dynamic_slice(array, (0, 0, to * CAP, 0), (1, 2, CAP, D))
            perm = [(i, ((i // 2 + s) % 4) * 2 + (i % 2 + m) % 2) for i in range(8)]
            moved.append(lax.ppermute(block.reshape(ROWS, D), "exp", perm))
    own = [
        lax.dynamic_slice(a, (0, 0, (at["x"] * 2 + at["c"]) * CAP, 0), (1, 2, CAP, D)).reshape(ROWS, D)
        for a in (expert_out, expert_grad)
    ]

    logit, partial = pl.pallas_call(
        mid_kernel,
        out_shape=(
            jax.ShapeDtypeStruct((TOK, EXPERTS), F32),
            jax.ShapeDtypeStruct((EXPERTS, D), F32),
        ),
        in_specs=[VMEM] * 16,
        out_specs=(VMEM,) * 2,
        compiler_params=params(24),
    )(slots, pack, expert_ids, probs, counts, gain, hidden, grad_out, own[0], *moved[:7])
    router_grad = reduce_all(partial, at)

    grad_hidden = pl.pallas_call(
        last_kernel,
        out_shape=jax.ShapeDtypeStruct((TOK, D), BF16),
        in_specs=[VMEM] * 15,
        out_specs=VMEM,
        scratch_shapes=[pltpu.VMEM((TOK, D), F32)],
        compiler_params=params(28),
    )(slots, pack, logit, router_weight, gain, hidden, grad_out, own[1], *moved[7:])
    return grad_hidden, router_grad


def solution(mesh):
    rows = P(("seq", "exp"), None)
    in_specs = (
        rows,
        rows,
        P(),
        rows,
        P(),
        rows,
        P("seq", "exp", None, None),
        P("seq", "exp", None, None),
    )
    return jax.shard_map(body, mesh=mesh, in_specs=in_specs, out_specs=(rows, P()), check_vma=False)
```

```python
import jax
import jax.numpy as jnp
from jax import lax
from jax.experimental import pallas as pl
from jax.experimental.pallas import tpu as pltpu
from jax.sharding import PartitionSpec as P

D = 8192
EXPERTS = 16
TOK = 128
CAP = 24
ROWS = 2 * CAP
TOKENS = 16384
AXES = ("seq", "exp")
CHUNK = 1024
F32 = jnp.float32
BF16 = jnp.bfloat16
VMEM = pl.BlockSpec(memory_space=pltpu.VMEM)

ROUTES = ((0, 0), (1, 0), (3, 0), (2, 0), (1, 1), (3, 1), (2, 1), (0, 1))


def coords():
    s, e = lax.axis_index("seq"), lax.axis_index("exp")
    return {"y": s >> 2, "z": s & 3, "x": e >> 1, "c": e & 1}


STRIDE = {"y": 32, "z": 8, "x": 2, "c": 1}
SIZE = {"y": 4, "z": 4, "x": 4, "c": 2}


def shift_perm(axis, d):
    out = []
    for i in range(128):
        a = (i // STRIDE[axis]) % SIZE[axis]
        out.append((i, i + ((a + d) % SIZE[axis] - a) * STRIDE[axis]))
    return out


def xor_perm(axis, d):
    return [(i, i ^ (d * STRIDE[axis])) for i in range(128)]


def after(*xs):
    return lax.optimization_barrier(xs)


def ring_permute(v, s, m):
    perm = [(i, (((i >> 1) + s) % 4) * 2 + ((i & 1) ^ m)) for i in range(8)]
    return lax.ppermute(v, "exp", perm)


def pick(v, axis, i):
    return lax.dynamic_index_in_dim(v, i, axis, keepdims=False)


def slot_numbers(sources):
    base = jnp.stack(sources).astype(F32) * ROWS
    return (base[:, None] + jnp.arange(ROWS, dtype=F32)[None, :]).reshape(1, 8 * ROWS)


def split3(v):
    a = v.astype(BF16)
    r = v - a.astype(F32)
    b = r.astype(BF16)
    c = (r - b.astype(F32)).astype(BF16)
    return a, b, c


def pre_kernel(ids_ref, logits_ref, hidden_ref, pack_ref, probs_ref, counts_ref):
    ids = ids_ref[...]
    logits = logits_ref[...]
    labels = lax.broadcasted_iota(jnp.int32, (TOK, EXPERTS), 1)
    oh = [(ids[:, k : k + 1] == labels).astype(F32) for k in range(2)]
    both = oh[0] + oh[1]
    row = lax.broadcasted_iota(jnp.int32, (TOK, TOK), 0)
    col = lax.broadcasted_iota(jnp.int32, (TOK, TOK), 1)
    before = (row > col).astype(F32).astype(BF16)
    ranks = jnp.dot(before, both.astype(BF16), preferred_element_type=F32)
    counts_ref[...] = jnp.broadcast_to(jnp.sum(both, axis=0, keepdims=True), (8, EXPERTS))
    index = [
        jnp.sum(oh[k] * (ranks + (CAP * labels).astype(F32)), axis=1, keepdims=True)
        for k in range(2)
    ]
    chosen = [jnp.sum(oh[k] * logits, axis=1, keepdims=True) for k in range(2)]
    top = jnp.maximum(chosen[0], chosen[1])
    w = [jnp.exp(c - top) for c in chosen]
    total = w[0] + w[1]
    e = jnp.exp(logits - jnp.max(logits, axis=1, keepdims=True))
    probs_ref[...] = e / jnp.sum(e, axis=1, keepdims=True)
    square = jnp.zeros((TOK, 128), F32)
    for c in range(D // CHUNK):
        h = hidden_ref[:, c * CHUNK : (c + 1) * CHUNK].astype(F32)
        h = h * h
        for j in range(CHUNK // 128):
            square = square + h[:, j * 128 : (j + 1) * 128]
    inv = lax.rsqrt(jnp.sum(square, axis=1, keepdims=True) / D + 1e-05)
    lane = lax.broadcasted_iota(jnp.int32, (TOK, 8), 1)
    pack = jnp.zeros((TOK, 8), F32)
    for i, v in enumerate((w[0] / total, w[1] / total, index[0], index[1], inv)):
        pack = jnp.where(lane == i, v, pack)
    pack_ref[...] = pack


def mid_kernel(
    slots_ref, pack_ref, ids_ref, probs_ref, counts_ref, gain_ref, hidden_ref, grad_ref, *refs
):
    blocks, (logit_ref, partial_ref) = refs[:8], refs[8:]
    pack = pack_ref[...]
    gate = [pack[:, 0:1], pack[:, 1:2]]
    inv = pack[:, 4:5]
    dots = jnp.zeros((TOK, 8 * ROWS), F32)
    for c in range(D // CHUNK):
        cols = slice(c * CHUNK, (c + 1) * CHUNK)
        picked = jnp.concatenate([b[:, cols] for b in blocks], axis=0)
        dots = dots + lax.dot_general(
            grad_ref[:, cols], picked, (((1,), (1,)), ((), ())), preferred_element_type=F32
        )
    slots = slots_ref[...]
    gate_dot = [
        jnp.sum(jnp.where(slots == pack[:, 2 + k : 3 + k], dots, 0.0), axis=1, keepdims=True)
        .astype(BF16)
        .astype(F32)
        for k in range(2)
    ]
    mean = gate[0] * gate_dot[0] + gate[1] * gate_dot[1]
    ids = ids_ref[...]
    labels = lax.broadcasted_iota(jnp.int32, (TOK, EXPERTS), 1)
    direct = jnp.zeros((TOK, EXPERTS), F32)
    for k in range(2):
        chosen = gate[k] * (gate_dot[k] - mean)
        direct = direct + jnp.where(ids[:, k : k + 1] == labels, chosen, 0.0)
    probs = probs_ref[...]
    load = counts_ref[0:1, :] * (EXPERTS / (2 * TOKENS))
    aux = probs * (load - jnp.sum(probs * load, axis=1, keepdims=True))
    logit = direct + aux
    logit_ref[...] = logit
    left = jnp.concatenate(split3(logit * inv), axis=1)
    for c in range(D // CHUNK):
        cols = slice(c * CHUNK, (c + 1) * CHUNK)
        p = lax.dot_general(
            left, hidden_ref[:, cols], (((0,), (0,)), ((), ())), preferred_element_type=F32
        )
        p = p[0:16] + p[16:32] + p[32:48]
        partial_ref[:, cols] = p * (gain_ref[:, cols] * (1.0 / 128.0))


def last_kernel(
    slots_ref, pack_ref, logit_ref, weight_ref, gain_ref, hidden_ref, grad_ref, *refs
):
    blocks, out_ref, scaled_ref = refs[:-2], refs[-2], refs[-1]
    pack = pack_ref[...]
    inv = pack[:, 4:5]
    slots = slots_ref[...]
    w = jnp.where(slots == pack[:, 2:3], pack[:, 0:1], 0.0)
    w = w + jnp.where(slots == pack[:, 3:4], pack[:, 1:2], 0.0)
    w_hi, w_lo, _ = split3(w)
    l0, l1, l2 = split3(logit_ref[...])
    zero = jnp.zeros_like(l0)
    left = jnp.concatenate(
        [
            jnp.concatenate([w_hi, l0, l0, l0, l2], axis=1),
            jnp.concatenate([w_lo, l1, l1, zero, zero], axis=1),
        ],
        axis=0,
    )
    acc = jnp.zeros((TOK, 128), F32)
    for c in range(D // CHUNK):
        cols = slice(c * CHUNK, (c + 1) * CHUNK)
        r0, r1, r2 = split3(weight_ref[:, cols])
        right = jnp.concatenate([b[:, cols] for b in blocks] + [r0, r1, r2, r0], axis=0)
        both = jnp.dot(left, right, preferred_element_type=F32)
        scaled = (both[:TOK] + both[TOK:]) * gain_ref[:, cols]
        scaled_ref[:, cols] = scaled
        prod = scaled * hidden_ref[:, cols].astype(F32)
        for j in range(CHUNK // 128):
            acc = acc + prod[:, j * 128 : (j + 1) * 128]
    mean = jnp.sum(acc, axis=1, keepdims=True) * inv / D
    factor = inv * mean
    for c in range(D // CHUNK):
        cols = slice(c * CHUNK, (c + 1) * CHUNK)
        back = inv * (scaled_ref[:, cols] - hidden_ref[:, cols].astype(F32) * factor)
        out_ref[:, cols] = (grad_ref[:, cols].astype(F32) + back).astype(BF16)


def params(mib):
    return pltpu.CompilerParams(vmem_limit_bytes=mib * 1024 * 1024)


def reduce_all(v, at):
    v = v.reshape(1024, 128)
    steps = [(axis, d) for axis in ("y", "z") for d in (2, 1)]
    for axis, d in steps:
        half = v.shape[0] // 2
        bit = (at[axis] & d) != 0
        send = jnp.where(bit, v[:half], v[half:])
        keep = jnp.where(bit, v[half:], v[:half])
        v = keep + lax.ppermute(send, AXES, xor_perm(axis, d))
    for axis, d in (("c", 1), ("x", 1), ("x", 2)):
        v = v + lax.ppermute(v, AXES, xor_perm(axis, d))
    for axis, d in reversed(steps):
        bit = (at[axis] & d) != 0
        got = lax.ppermute(v, AXES, xor_perm(axis, d))
        v = jnp.concatenate([jnp.where(bit, got, v), jnp.where(bit, v, got)], axis=0)
    return v.reshape(EXPERTS, D)


def body(
    grad_out, hidden, norm_gain, router_logits, router_weight, expert_ids, expert_grad, expert_out
):
    at = coords()
    gain = norm_gain.reshape(1, D)
    sources = [((at["x"] - s) & 3) * 2 + (at["c"] ^ m) for s, m in ROUTES]
    slots = slot_numbers(sources)
    grad_slots = slot_numbers([sources[i] for i in (0, 7, 1, 4, 2, 5, 3, 6)])

    pack, probs, counts = pl.pallas_call(
        pre_kernel,
        out_shape=(
            jax.ShapeDtypeStruct((TOK, 8), F32),
            jax.ShapeDtypeStruct((TOK, EXPERTS), F32),
            jax.ShapeDtypeStruct((8, EXPERTS), F32),
        ),
        in_specs=[VMEM] * 3,
        out_specs=(VMEM,) * 3,
        compiler_params=params(16),
    )(expert_ids, router_logits, hidden)
    me = at["x"] * 2 + at["c"]
    tally = [counts]
    for axis, d in (("y", 1), ("y", 2), ("z", 1), ("z", 2), ("c", 1), ("x", 1), ("x", 2)):
        tally.append(tally[-1] + lax.ppermute(tally[-1], AXES, xor_perm(axis, d)))

    by_core = expert_grad.reshape(2, 4, 2, CAP, D)
    swap = ring_permute(pick(by_core, 2, at["c"] ^ 1), 0, 1)
    mine = pick(by_core, 2, at["c"])

    outs = []
    for n, (s, m) in enumerate(ROUTES[1:]):
        array = expert_out
        if n == 3:
            array, swap = after(array, swap)
        if n > 3:
            array, outs[n - 4], tally[2 * n - 6] = after(array, outs[n - 4], tally[2 * n - 6])
        to = ((at["x"] + s) & 3) * 2 + (at["c"] ^ m)
        block = lax.dynamic_slice(array, (0, 0, to * CAP, 0), (1, 2, CAP, D))
        outs.append(ring_permute(block.reshape(ROWS, D), s, m))
    own_out = lax.dynamic_slice(expert_out, (0, 0, me * CAP, 0), (1, 2, CAP, D)).reshape(ROWS, D)

    grads = [pick(mine, 1, at["x"]).reshape(ROWS, D), pick(swap, 1, at["x"]).reshape(ROWS, D)]
    for n, s in enumerate((1, 3, 2)):
        a, b = mine, swap
        a, b, outs[n + 3] = after(a, b, outs[n + 3])
        if n == 0:
            a, tally[7] = after(a, tally[7])
        to = (at["x"] + s) & 3
        block = jnp.concatenate([pick(a, 1, to), pick(b, 1, to)], axis=0)
        grads.append(ring_permute(block.reshape(2 * ROWS, D), s, 0))

    logit, partial = pl.pallas_call(
        mid_kernel,
        out_shape=(
            jax.ShapeDtypeStruct((TOK, EXPERTS), F32),
            jax.ShapeDtypeStruct((EXPERTS, D), F32),
        ),
        in_specs=[VMEM] * 16,
        out_specs=(VMEM,) * 2,
        compiler_params=params(24),
    )(slots, pack, expert_ids, probs, tally[7], gain, hidden, grad_out, own_out, *outs)
    router_grad = reduce_all(partial, at)

    grad_hidden = pl.pallas_call(
        last_kernel,
        out_shape=jax.ShapeDtypeStruct((TOK, D), BF16),
        in_specs=[VMEM] * 12,
        out_specs=VMEM,
        scratch_shapes=[pltpu.VMEM((TOK, D), F32)],
        compiler_params=params(28),
    )(grad_slots, pack, logit, router_weight, gain, hidden, grad_out, *grads)
    return grad_hidden, router_grad


def solution(mesh):
    rows = P(("seq", "exp"), None)
    in_specs = (
        rows,
        rows,
        P(),
        rows,
        P(),
        rows,
        P("seq", "exp", None, None),
        P("seq", "exp", None, None),
    )
    return jax.shard_map(body, mesh=mesh, in_specs=in_specs, out_specs=(rows, P()), check_vma=False)
```

```python
import jax
import jax.numpy as jnp
from jax import lax
from jax.experimental import pallas as pl
from jax.experimental.pallas import tpu as pltpu
from jax.sharding import PartitionSpec as P

D = 8192
EXPERTS = 16
TOK = 128
CAP = 24
ROWS = 2 * CAP
TOKENS = 16384
AXES = ("seq", "exp")
CHUNK = 1024
F32 = jnp.float32
BF16 = jnp.bfloat16
VMEM = pl.BlockSpec(memory_space=pltpu.VMEM)

ROUTES = ((0, 0), (1, 0), (3, 0), (2, 0), (1, 1), (3, 1), (2, 1), (0, 1))


def coords():
    s, e = lax.axis_index("seq"), lax.axis_index("exp")
    return {"y": s >> 2, "z": s & 3, "x": e >> 1, "c": e & 1}


STRIDE = {"y": 32, "z": 8, "x": 2, "c": 1}
SIZE = {"y": 4, "z": 4, "x": 4, "c": 2}


def shift_perm(axis, d):
    out = []
    for i in range(128):
        a = (i // STRIDE[axis]) % SIZE[axis]
        out.append((i, i + ((a + d) % SIZE[axis] - a) * STRIDE[axis]))
    return out


def xor_perm(axis, d):
    return [(i, i ^ (d * STRIDE[axis])) for i in range(128)]


def after(*xs):
    return lax.optimization_barrier(xs)


def ring_permute(v, s, m):
    perm = [(i, (((i >> 1) + s) % 4) * 2 + ((i & 1) ^ m)) for i in range(8)]
    return lax.ppermute(v, "exp", perm)


def pick(v, axis, i):
    return lax.dynamic_index_in_dim(v, i, axis, keepdims=False)


def slot_numbers(sources):
    base = jnp.stack(sources).astype(F32) * ROWS
    return (base[:, None] + jnp.arange(ROWS, dtype=F32)[None, :]).reshape(1, 8 * ROWS)


def split3(v):
    a = v.astype(BF16)
    r = v - a.astype(F32)
    b = r.astype(BF16)
    c = (r - b.astype(F32)).astype(BF16)
    return a, b, c


def pre_kernel(ids_ref, logits_ref, hidden_ref, pack_ref, probs_ref, counts_ref):
    ids = ids_ref[...]
    logits = logits_ref[...]
    labels = lax.broadcasted_iota(jnp.int32, (TOK, EXPERTS), 1)
    oh = [(ids[:, k : k + 1] == labels).astype(F32) for k in range(2)]
    both = oh[0] + oh[1]
    row = lax.broadcasted_iota(jnp.int32, (TOK, TOK), 0)
    col = lax.broadcasted_iota(jnp.int32, (TOK, TOK), 1)
    before = (row > col).astype(F32).astype(BF16)
    ranks = jnp.dot(before, both.astype(BF16), preferred_element_type=F32)
    counts_ref[...] = jnp.broadcast_to(jnp.sum(both, axis=0, keepdims=True), (8, EXPERTS))
    index = [
        jnp.sum(oh[k] * (ranks + (CAP * labels).astype(F32)), axis=1, keepdims=True)
        for k in range(2)
    ]
    chosen = [jnp.sum(oh[k] * logits, axis=1, keepdims=True) for k in range(2)]
    top = jnp.maximum(chosen[0], chosen[1])
    w = [jnp.exp(c - top) for c in chosen]
    total = w[0] + w[1]
    e = jnp.exp(logits - jnp.max(logits, axis=1, keepdims=True))
    probs_ref[...] = e / jnp.sum(e, axis=1, keepdims=True)
    square = jnp.zeros((TOK, 128), F32)
    for c in range(D // CHUNK):
        h = hidden_ref[:, c * CHUNK : (c + 1) * CHUNK].astype(F32)
        h = h * h
        for j in range(CHUNK // 128):
            square = square + h[:, j * 128 : (j + 1) * 128]
    inv = lax.rsqrt(jnp.sum(square, axis=1, keepdims=True) / D + 1e-05)
    lane = lax.broadcasted_iota(jnp.int32, (TOK, 8), 1)
    pack = jnp.zeros((TOK, 8), F32)
    for i, v in enumerate((w[0] / total, w[1] / total, index[0], index[1], inv)):
        pack = jnp.where(lane == i, v, pack)
    pack_ref[...] = pack


def mid_kernel(
    slots_ref, pack_ref, ids_ref, probs_ref, counts_ref, gain_ref, hidden_ref, grad_ref, *refs
):
    blocks, (logit_ref, partial_ref, dots_ref, left_ref) = refs[:8], refs[8:]
    stage, c = pl.program_id(0), pl.program_id(1)

    @pl.when(stage == 0)
    def _():
        picked = jnp.concatenate([b[...] for b in blocks], axis=0)
        d = lax.dot_general(
            grad_ref[...], picked, (((1,), (1,)), ((), ())), preferred_element_type=F32
        )

        @pl.when(c == 0)
        def _():
            dots_ref[...] = d

        @pl.when(c > 0)
        def _():
            dots_ref[...] += d

    @pl.when((stage == 1) & (c == 0))
    def _():
        pack = pack_ref[...]
        gate = [pack[:, 0:1], pack[:, 1:2]]
        slots = slots_ref[...]
        dots = dots_ref[...]
        gate_dot = [
            jnp.sum(jnp.where(slots == pack[:, 2 + k : 3 + k], dots, 0.0), axis=1, keepdims=True)
            .astype(BF16)
            .astype(F32)
            for k in range(2)
        ]
        mean = gate[0] * gate_dot[0] + gate[1] * gate_dot[1]
        ids = ids_ref[...]
        labels = lax.broadcasted_iota(jnp.int32, (TOK, EXPERTS), 1)
        direct = jnp.zeros((TOK, EXPERTS), F32)
        for k in range(2):
            chosen = gate[k] * (gate_dot[k] - mean)
            direct = direct + jnp.where(ids[:, k : k + 1] == labels, chosen, 0.0)
        probs = probs_ref[...]
        load = counts_ref[0:1, :] * (EXPERTS / (2 * TOKENS))
        aux = probs * (load - jnp.sum(probs * load, axis=1, keepdims=True))
        logit = direct + aux
        logit_ref[...] = logit
        left_ref[...] = jnp.concatenate(split3(logit * pack[:, 4:5]), axis=1)

    @pl.when(stage == 1)
    def _():
        p = lax.dot_general(
            left_ref[...], hidden_ref[...], (((0,), (0,)), ((), ())), preferred_element_type=F32
        )
        p = (p[0:16] + p[16:32] + p[32:48]) * (gain_ref[...] * (1.0 / 128.0))
        for j in range(WIDE // 1024):
            partial_ref[:, c * (WIDE // 1024) + j, :] = p[:, j * 1024 : (j + 1) * 1024]


def last_kernel(
    slots_ref, pack_ref, logit_ref, weight_ref, gain_ref, hidden_ref, grad_ref, *refs
):
    blocks, (out_ref, scaled_ref, normed_ref, left_ref, acc_ref, factor_ref) = refs[:-6], refs[-6:]
    stage, c = pl.program_id(0), pl.program_id(1)
    cols = pl.ds(pl.multiple_of(c * WIDE, WIDE), WIDE)

    @pl.when((stage == 0) & (c == 0))
    def _():
        pack = pack_ref[...]
        slots = slots_ref[...]
        w = jnp.where(slots == pack[:, 2:3], pack[:, 0:1], 0.0)
        w = w + jnp.where(slots == pack[:, 3:4], pack[:, 1:2], 0.0)
        w_hi, w_lo, _ = split3(w)
        l0, l1, l2 = split3(logit_ref[...])
        zero = jnp.zeros_like(l0)
        left_ref[...] = jnp.concatenate(
            [
                jnp.concatenate([w_hi, l0, l0, l0, l2], axis=1),
                jnp.concatenate([w_lo, l1, l1, zero, zero], axis=1),
            ],
            axis=0,
        )
        acc_ref[...] = jnp.zeros_like(acc_ref)

    @pl.when(stage == 0)
    def _():
        r0, r1, r2 = split3(weight_ref[...])
        right = jnp.concatenate([b[...] for b in blocks] + [r0, r1, r2, r0], axis=0)
        both = jnp.dot(left_ref[...], right, preferred_element_type=F32)
        scaled = (both[:TOK] + both[TOK:]) * gain_ref[...]
        scaled_ref[:, cols] = scaled
        hidden = hidden_ref[...]
        normed_ref[:, cols] = hidden
        prod = scaled * hidden.astype(F32)
        acc = acc_ref[...]
        for j in range(WIDE // 128):
            acc = acc + prod[:, j * 128 : (j + 1) * 128]
        acc_ref[...] = acc

    @pl.when((stage == 1) & (c == 0))
    def _():
        inv = pack_ref[:, 4:5]
        mean = jnp.sum(acc_ref[...], axis=1, keepdims=True) * inv / D
        factor_ref[...] = jnp.broadcast_to(inv * mean, (TOK, 128))

    @pl.when(stage == 1)
    def _():
        inv = pack_ref[:, 4:5]
        factor = factor_ref[:, 0:1]
        back = inv * (scaled_ref[:, cols] - normed_ref[:, cols].astype(F32) * factor)
        out_ref[...] = (grad_ref[...].astype(F32) + back).astype(BF16)


STEPS = 4
WIDE = D // STEPS


def first(rows):
    return pl.BlockSpec((rows, WIDE), lambda p, c: (0, jnp.where(p == 0, c, STEPS - 1)))


def second(rows):
    return pl.BlockSpec((rows, WIDE), lambda p, c: (0, jnp.where(p == 0, 0, c)))


def params(mib):
    return pltpu.CompilerParams(vmem_limit_bytes=mib * 1024 * 1024)


def reduce_all(v):
    v = jnp.sum(lax.all_to_all(v, "seq", 0, 0, tiled=True), axis=0)
    for axis, d in (("c", 1), ("x", 1), ("x", 2)):
        v = v + lax.ppermute(v, AXES, xor_perm(axis, d))
    return lax.all_gather(v, "seq").reshape(EXPERTS, D)


def body(
    grad_out, hidden, norm_gain, router_logits, router_weight, expert_ids, expert_grad, expert_out
):
    at = coords()
    gain = norm_gain.reshape(1, D)
    sources = [((at["x"] - s) & 3) * 2 + (at["c"] ^ m) for s, m in ROUTES]
    slots = slot_numbers(sources)
    grad_slots = slot_numbers([sources[i] for i in (0, 7, 1, 4, 2, 5, 3, 6)])

    pack, probs, counts = pl.pallas_call(
        pre_kernel,
        out_shape=(
            jax.ShapeDtypeStruct((TOK, 8), F32),
            jax.ShapeDtypeStruct((TOK, EXPERTS), F32),
            jax.ShapeDtypeStruct((8, EXPERTS), F32),
        ),
        in_specs=[VMEM] * 3,
        out_specs=(VMEM,) * 3,
        compiler_params=params(16),
    )(expert_ids, router_logits, hidden)
    me = at["x"] * 2 + at["c"]
    tally = [counts]
    for axis, d in (("c", 1), ("x", 1), ("x", 2), ("y", 1), ("y", 2), ("z", 1), ("z", 2)):
        tally.append(tally[-1] + lax.ppermute(tally[-1], AXES, xor_perm(axis, d)))

    source, tally[2] = after(expert_grad, tally[2])
    by_core = source.reshape(2, 4, 2, CAP, D)
    swap = ring_permute(pick(by_core, 2, at["c"] ^ 1), 0, 1)
    mine = pick(by_core, 2, at["c"])

    outs = []
    for n, (s, m) in enumerate(ROUTES[1:]):
        array = expert_out
        if n > 3:
            array, outs[n - 4], tally[2 * n - 5] = after(array, outs[n - 4], tally[2 * n - 5])
        to = ((at["x"] + s) & 3) * 2 + (at["c"] ^ m)
        block = lax.dynamic_slice(array, (0, 0, to * CAP, 0), (1, 2, CAP, D))
        outs.append(ring_permute(block.reshape(ROWS, D), s, m))
    own_out = lax.dynamic_slice(expert_out, (0, 0, me * CAP, 0), (1, 2, CAP, D)).reshape(ROWS, D)

    grads = [pick(mine, 1, at["x"]).reshape(ROWS, D), pick(swap, 1, at["x"]).reshape(ROWS, D)]
    for n, s in enumerate((1, 3, 2)):
        a, b = mine, swap
        a, b, outs[n + 3] = after(a, b, outs[n + 3])
        to = (at["x"] + s) & 3
        block = jnp.concatenate([pick(a, 1, to), pick(b, 1, to)], axis=0)
        grads.append(ring_permute(block.reshape(2 * ROWS, D), s, 0))

    small = lambda *shape: pl.BlockSpec(shape, lambda p, c: (0,) * len(shape))
    logit, partial = pl.pallas_call(
        mid_kernel,
        grid=(2, STEPS),
        out_shape=(
            jax.ShapeDtypeStruct((TOK, EXPERTS), F32),
            jax.ShapeDtypeStruct((EXPERTS, 8, 1024), F32),
        ),
        in_specs=[
            small(1, 8 * ROWS),
            small(TOK, 8),
            small(TOK, 2),
            small(TOK, EXPERTS),
            small(8, EXPERTS),
            second(1),
            second(TOK),
            first(TOK),
        ]
        + [first(ROWS)] * 8,
        out_specs=(
            small(TOK, EXPERTS),
            small(EXPERTS, 8, 1024),
        ),
        scratch_shapes=[pltpu.VMEM((TOK, 8 * ROWS), F32), pltpu.VMEM((TOK, 3 * EXPERTS), BF16)],
        compiler_params=params(24),
    )(slots, pack, expert_ids, probs, tally[7], gain, hidden, grad_out, own_out, *outs)
    router_grad = reduce_all(partial)

    grad_hidden = pl.pallas_call(
        last_kernel,
        grid=(2, STEPS),
        out_shape=jax.ShapeDtypeStruct((TOK, D), BF16),
        in_specs=[
            small(1, 8 * ROWS),
            small(TOK, 8),
            small(TOK, EXPERTS),
            first(EXPERTS),
            first(1),
            first(TOK),
            second(TOK),
        ]
        + [first(g.shape[0]) for g in grads],
        out_specs=second(TOK),
        scratch_shapes=[
            pltpu.VMEM((TOK, D), F32),
            pltpu.VMEM((TOK, D), BF16),
            pltpu.VMEM((2 * TOK, 8 * ROWS + 4 * EXPERTS), BF16),
            pltpu.VMEM((TOK, 128), F32),
            pltpu.VMEM((TOK, 128), F32),
        ],
        compiler_params=params(28),
    )(grad_slots, pack, logit, router_weight, gain, hidden, grad_out, *grads)
    return grad_hidden, router_grad


def solution(mesh):
    rows = P(("seq", "exp"), None)
    in_specs = (
        rows,
        rows,
        P(),
        rows,
        P(),
        rows,
        P("seq", "exp", None, None),
        P("seq", "exp", None, None),
    )
    return jax.shard_map(body, mesh=mesh, in_specs=in_specs, out_specs=(rows, P()), check_vma=False)
```

```python
import jax
import jax.numpy as jnp
from jax import lax
from jax.experimental import pallas as pl
from jax.experimental.pallas import tpu as pltpu
from jax.sharding import PartitionSpec as P

D = 8192
EXPERTS = 16
TOK = 128
CAP = 24
ROWS = 2 * CAP
TOKENS = 16384
AXES = ("seq", "exp")
CHUNK = 1024
F32 = jnp.float32
BF16 = jnp.bfloat16
VMEM = pl.BlockSpec(memory_space=pltpu.VMEM)

ROUTES = ((0, 0), (1, 0), (3, 0), (2, 0), (1, 1), (3, 1), (2, 1), (0, 1))


def coords():
    s, e = lax.axis_index("seq"), lax.axis_index("exp")
    return {"y": s >> 2, "z": s & 3, "x": e >> 1, "c": e & 1}


STRIDE = {"y": 32, "z": 8, "x": 2, "c": 1}
SIZE = {"y": 4, "z": 4, "x": 4, "c": 2}


def shift_perm(axis, d):
    out = []
    for i in range(128):
        a = (i // STRIDE[axis]) % SIZE[axis]
        out.append((i, i + ((a + d) % SIZE[axis] - a) * STRIDE[axis]))
    return out


def xor_perm(axis, d):
    return [(i, i ^ (d * STRIDE[axis])) for i in range(128)]


def after(*xs):
    return lax.optimization_barrier(xs)


def ring_permute(v, s, m):
    perm = [(i, (((i >> 1) + s) % 4) * 2 + ((i & 1) ^ m)) for i in range(8)]
    return lax.ppermute(v, "exp", perm)


def pick(v, axis, i):
    return lax.dynamic_index_in_dim(v, i, axis, keepdims=False)


def slot_numbers(sources):
    base = jnp.stack(sources).astype(F32) * ROWS
    return (base[:, None] + jnp.arange(ROWS, dtype=F32)[None, :]).reshape(1, 8 * ROWS)


def split3(v):
    a = v.astype(BF16)
    r = v - a.astype(F32)
    b = r.astype(BF16)
    c = (r - b.astype(F32)).astype(BF16)
    return a, b, c


def pre_kernel(ids_ref, logits_ref, pack_ref, probs_ref, counts_ref):
    ids = ids_ref[...]
    logits = logits_ref[...]
    labels = lax.broadcasted_iota(jnp.int32, (TOK, EXPERTS), 1)
    oh = [(ids[:, k : k + 1] == labels).astype(F32) for k in range(2)]
    both = oh[0] + oh[1]
    row = lax.broadcasted_iota(jnp.int32, (TOK, TOK), 0)
    col = lax.broadcasted_iota(jnp.int32, (TOK, TOK), 1)
    before = (row > col).astype(F32).astype(BF16)
    ranks = jnp.dot(before, both.astype(BF16), preferred_element_type=F32)
    counts_ref[...] = jnp.broadcast_to(jnp.sum(both, axis=0, keepdims=True), (8, EXPERTS))
    index = [
        jnp.sum(oh[k] * (ranks + (CAP * labels).astype(F32)), axis=1, keepdims=True)
        for k in range(2)
    ]
    chosen = [jnp.sum(oh[k] * logits, axis=1, keepdims=True) for k in range(2)]
    top = jnp.maximum(chosen[0], chosen[1])
    w = [jnp.exp(c - top) for c in chosen]
    total = w[0] + w[1]
    e = jnp.exp(logits - jnp.max(logits, axis=1, keepdims=True))
    probs_ref[...] = e / jnp.sum(e, axis=1, keepdims=True)
    lane = lax.broadcasted_iota(jnp.int32, (TOK, 8), 1)
    pack = jnp.zeros((TOK, 8), F32)
    for i, v in enumerate((w[0] / total, w[1] / total, index[0], index[1])):
        pack = jnp.where(lane == i, v, pack)
    pack_ref[...] = pack


def mid_kernel(
    slots_ref,
    pack_ref,
    inv_ref,
    ids_ref,
    probs_ref,
    counts_ref,
    gain_ref,
    hidden_ref,
    grad_ref,
    *refs,
):
    blocks, (logit_ref, partial_ref, dots_ref, left_ref, total_ref) = refs[:8], refs[8:]
    stage, c = pl.program_id(0), pl.program_id(1)

    @pl.when(stage == 0)
    def _():
        picked = jnp.concatenate([b[:ROWS] for b in blocks], axis=0)
        d = lax.dot_general(
            grad_ref[...], picked, (((1,), (1,)), ((), ())), preferred_element_type=F32
        )

        @pl.when(c == 0)
        def _():
            dots_ref[...] = d
            total = counts_ref[...]
            for b in blocks[4:7]:
                other = b[ROWS : ROWS + 8, 0 : 2 * EXPERTS].astype(F32)
                total = total + other[:, :EXPERTS] + other[:, EXPERTS:]
            total_ref[...] = total

        @pl.when(c > 0)
        def _():
            dots_ref[...] += d

    @pl.when((stage == 1) & (c == 0))
    def _():
        pack = pack_ref[...]
        gate = [pack[:, 0:1], pack[:, 1:2]]
        slots = slots_ref[...]
        dots = dots_ref[...]
        gate_dot = [
            jnp.sum(jnp.where(slots == pack[:, 2 + k : 3 + k], dots, 0.0), axis=1, keepdims=True)
            .astype(BF16)
            .astype(F32)
            for k in range(2)
        ]
        mean = gate[0] * gate_dot[0] + gate[1] * gate_dot[1]
        ids = ids_ref[...]
        labels = lax.broadcasted_iota(jnp.int32, (TOK, EXPERTS), 1)
        direct = jnp.zeros((TOK, EXPERTS), F32)
        for k in range(2):
            chosen = gate[k] * (gate_dot[k] - mean)
            direct = direct + jnp.where(ids[:, k : k + 1] == labels, chosen, 0.0)
        probs = probs_ref[...]
        load = total_ref[0:1, :] * (EXPERTS / (2 * TOKENS))
        aux = probs * (load - jnp.sum(probs * load, axis=1, keepdims=True))
        logit = direct + aux
        logit_ref[...] = logit
        left_ref[...] = jnp.concatenate(split3(logit * inv_ref[...]), axis=1)

    @pl.when(stage == 1)
    def _():
        p = lax.dot_general(
            left_ref[...], hidden_ref[...], (((0,), (0,)), ((), ())), preferred_element_type=F32
        )
        p = (p[0:16] + p[16:32] + p[32:48]) * (gain_ref[...] * (1.0 / 128.0))
        for j in range(WIDE // 1024):
            partial_ref[:, c * (WIDE // 1024) + j, :] = p[:, j * 1024 : (j + 1) * 1024]


def last_kernel(
    slots_ref, pack_ref, inv_ref, logit_ref, weight_ref, gain_ref, hidden_ref, grad_ref, *refs
):
    blocks, (out_ref, scaled_ref, normed_ref, left_ref, acc_ref, factor_ref) = refs[:-6], refs[-6:]
    stage, c = pl.program_id(0), pl.program_id(1)
    cols = pl.ds(pl.multiple_of(c * WIDE, WIDE), WIDE)

    @pl.when((stage == 0) & (c == 0))
    def _():
        pack = pack_ref[...]
        slots = slots_ref[...]
        w = jnp.where(slots == pack[:, 2:3], pack[:, 0:1], 0.0)
        w = w + jnp.where(slots == pack[:, 3:4], pack[:, 1:2], 0.0)
        w_hi, w_lo, _ = split3(w)
        l0, l1, l2 = split3(logit_ref[...])
        zero = jnp.zeros_like(l0)
        left_ref[...] = jnp.concatenate(
            [
                jnp.concatenate([w_hi, l0, l0, l0, l2], axis=1),
                jnp.concatenate([w_lo, l1, l1, zero, zero], axis=1),
            ],
            axis=0,
        )
        acc_ref[...] = jnp.zeros_like(acc_ref)

    @pl.when(stage == 0)
    def _():
        r0, r1, r2 = split3(weight_ref[...])
        right = jnp.concatenate([b[...] for b in blocks] + [r0, r1, r2, r0], axis=0)
        both = jnp.dot(left_ref[...], right, preferred_element_type=F32)
        scaled = (both[:TOK] + both[TOK:]) * gain_ref[...]
        scaled_ref[:, cols] = scaled
        hidden = hidden_ref[...]
        normed_ref[:, cols] = hidden
        prod = scaled * hidden.astype(F32)
        acc = acc_ref[...]
        for j in range(WIDE // 128):
            acc = acc + prod[:, j * 128 : (j + 1) * 128]
        acc_ref[...] = acc

    @pl.when((stage == 1) & (c == 0))
    def _():
        inv = inv_ref[...]
        mean = jnp.sum(acc_ref[...], axis=1, keepdims=True) * inv / D
        factor_ref[...] = jnp.broadcast_to(inv * mean, (TOK, 128))

    @pl.when(stage == 1)
    def _():
        inv = inv_ref[...]
        factor = factor_ref[:, 0:1]
        back = inv * (scaled_ref[:, cols] - normed_ref[:, cols].astype(F32) * factor)
        out_ref[...] = (grad_ref[...].astype(F32) + back).astype(BF16)


STEPS = 4
WIDE = D // STEPS


def first(rows):
    return pl.BlockSpec((rows, WIDE), lambda p, c: (0, jnp.where(p == 0, c, STEPS - 1)))


def second(rows):
    return pl.BlockSpec((rows, WIDE), lambda p, c: (0, jnp.where(p == 0, 0, c)))


def params(mib):
    return pltpu.CompilerParams(vmem_limit_bytes=mib * 1024 * 1024)


def sum_x(v):
    a, b, c = [lax.ppermute(v, AXES, xor_perm("x", d)) for d in (1, 2, 3)]
    return (v + a) + (b + c)


def body(
    grad_out, hidden, norm_gain, router_logits, router_weight, expert_ids, expert_grad, expert_out
):
    at = coords()
    gain = norm_gain.reshape(1, D)
    sources = [((at["x"] - s) & 3) * 2 + (at["c"] ^ m) for s, m in ROUTES]
    slots = slot_numbers(sources)
    grad_slots = slot_numbers([sources[i] for i in (0, 7, 1, 4, 2, 5, 3, 6)])

    pack, probs, counts = pl.pallas_call(
        pre_kernel,
        out_shape=(
            jax.ShapeDtypeStruct((TOK, 8), F32),
            jax.ShapeDtypeStruct((TOK, EXPERTS), F32),
            jax.ShapeDtypeStruct((8, EXPERTS), F32),
        ),
        in_specs=[VMEM] * 2,
        out_specs=(VMEM,) * 3,
        compiler_params=params(8),
    )(expert_ids, router_logits)
    wide = hidden.astype(F32)
    inv = lax.rsqrt(jnp.mean(wide * wide, axis=1, keepdims=True) + 1e-05)
    me = at["x"] * 2 + at["c"]
    tally = [counts]
    for axis, d in (("y", 1), ("y", 2), ("z", 1), ("z", 2), ("c", 1)):
        tally.append(tally[-1] + lax.ppermute(tally[-1], AXES, xor_perm(axis, d)))
    share = tally[5][0:1].astype(BF16)
    share = jnp.concatenate([share, (tally[5][0:1] - share.astype(F32)).astype(BF16)], axis=1)
    share = jnp.pad(share, ((0, 7), (0, D - 2 * EXPERTS)))

    source, tally[1] = after(expert_grad, tally[1])
    by_core = source.reshape(2, 4, 2, CAP, D)
    swap = ring_permute(pick(by_core, 2, at["c"] ^ 1), 0, 1)
    mine = pick(by_core, 2, at["c"])

    outs = []
    for n, (s, m) in enumerate(ROUTES[1:]):
        array = expert_out
        if n == 3:
            array, swap, share = after(array, swap, share)
        if n > 3:
            array, outs[n - 4] = after(array, outs[n - 4])
        to = ((at["x"] + s) & 3) * 2 + (at["c"] ^ m)
        block = lax.dynamic_slice(array, (0, 0, to * CAP, 0), (1, 2, CAP, D))
        block = block.reshape(ROWS, D)
        if 3 <= n <= 5:
            block = jnp.concatenate([block, share], axis=0)
        outs.append(ring_permute(block, s, m))
    own_out = lax.dynamic_slice(expert_out, (0, 0, me * CAP, 0), (1, 2, CAP, D)).reshape(ROWS, D)

    def send_grad(s, *deps):
        a, b, *deps = after(mine, swap, *deps)
        to = (at["x"] + s) & 3
        block = jnp.concatenate([pick(a, 1, to), pick(b, 1, to)], axis=0)
        return ring_permute(block.reshape(2 * ROWS, D), s, 0), *deps

    grads = [pick(mine, 1, at["x"]).reshape(ROWS, D), pick(swap, 1, at["x"]).reshape(ROWS, D)]
    for s, n in ((1, 3), (3, 4)):
        moved, outs[n] = send_grad(s, outs[n])
        grads.append(moved)

    small = lambda *shape: pl.BlockSpec(shape, lambda p, c: (0,) * len(shape))
    logit, partial = pl.pallas_call(
        mid_kernel,
        grid=(2, STEPS),
        out_shape=(
            jax.ShapeDtypeStruct((TOK, EXPERTS), F32),
            jax.ShapeDtypeStruct((EXPERTS, 8, 1024), F32),
        ),
        in_specs=[
            small(1, 8 * ROWS),
            small(TOK, 8),
            small(TOK, 1),
            small(TOK, 2),
            small(TOK, EXPERTS),
            small(8, EXPERTS),
            second(1),
            second(TOK),
            first(TOK),
        ]
        + [first(b.shape[0]) for b in (own_out, *outs)],
        out_specs=(
            small(TOK, EXPERTS),
            small(EXPERTS, 8, 1024),
        ),
        scratch_shapes=[
            pltpu.VMEM((TOK, 8 * ROWS), F32),
            pltpu.VMEM((TOK, 3 * EXPERTS), BF16),
            pltpu.VMEM((8, EXPERTS), F32),
        ],
        cost_estimate=pl.CostEstimate(flops=20_000_000_000, bytes_accessed=60_000_000, transcendentals=0),
        compiler_params=params(20),
    )(slots, pack, inv, expert_ids, probs, tally[5], gain, hidden, grad_out, own_out, *outs)
    partial = jnp.sum(lax.all_to_all(partial, "seq", 0, 0, tiled=True), axis=0)
    partial = partial + lax.ppermute(partial, AXES, xor_perm("c", 1))
    partial, grads[2], grads[3] = after(partial, grads[2], grads[3])
    partial = sum_x(partial)
    moved, partial = send_grad(2, partial)
    grads.append(moved)
    router_grad = lax.all_gather(partial, "seq").reshape(EXPERTS, D)

    grad_hidden = pl.pallas_call(
        last_kernel,
        grid=(2, STEPS),
        out_shape=jax.ShapeDtypeStruct((TOK, D), BF16),
        in_specs=[
            small(1, 8 * ROWS),
            small(TOK, 8),
            small(TOK, 1),
            small(TOK, EXPERTS),
            first(EXPERTS),
            first(1),
            first(TOK),
            second(TOK),
        ]
        + [first(g.shape[0]) for g in grads],
        out_specs=second(TOK),
        scratch_shapes=[
            pltpu.VMEM((TOK, D), F32),
            pltpu.VMEM((TOK, D), BF16),
            pltpu.VMEM((2 * TOK, 8 * ROWS + 4 * EXPERTS), BF16),
            pltpu.VMEM((TOK, 128), F32),
            pltpu.VMEM((TOK, 128), F32),
        ],
        compiler_params=params(28),
    )(grad_slots, pack, inv, logit, router_weight, gain, hidden, grad_out, *grads)
    return grad_hidden, router_grad


def solution(mesh):
    rows = P(("seq", "exp"), None)
    in_specs = (
        rows,
        rows,
        P(),
        rows,
        P(),
        rows,
        P("seq", "exp", None, None),
        P("seq", "exp", None, None),
    )
    return jax.shard_map(body, mesh=mesh, in_specs=in_specs, out_specs=(rows, P()), check_vma=False)
```

```python
import jax
import jax.numpy as jnp
from jax import lax
from jax.experimental import pallas as pl
from jax.experimental.pallas import tpu as pltpu
from jax.sharding import PartitionSpec as P

D = 8192
EXPERTS = 16
TOK = 128
CAP = 24
ROWS = 2 * CAP
TOKENS = 16384
AXES = ("seq", "exp")
CHUNK = 1024
F32 = jnp.float32
BF16 = jnp.bfloat16
VMEM = pl.BlockSpec(memory_space=pltpu.VMEM)

ROUTES = ((0, 0), (1, 0), (3, 0), (2, 0), (1, 1), (3, 1), (2, 1), (0, 1))


def coords():
    s, e = lax.axis_index("seq"), lax.axis_index("exp")
    return {"y": s >> 2, "z": s & 3, "x": e >> 1, "c": e & 1}


STRIDE = {"y": 32, "z": 8, "x": 2, "c": 1}
SIZE = {"y": 4, "z": 4, "x": 4, "c": 2}


def shift_perm(axis, d):
    out = []
    for i in range(128):
        a = (i // STRIDE[axis]) % SIZE[axis]
        out.append((i, i + ((a + d) % SIZE[axis] - a) * STRIDE[axis]))
    return out


def xor_perm(axis, d):
    return [(i, i ^ (d * STRIDE[axis])) for i in range(128)]


def after(*xs):
    return lax.optimization_barrier(xs)


def ring_permute(v, s, m):
    perm = [(i, (((i >> 1) + s) % 4) * 2 + ((i & 1) ^ m)) for i in range(8)]
    return lax.ppermute(v, "exp", perm)


def slot_numbers(sources):
    base = jnp.stack(sources).astype(F32) * ROWS
    return (base[:, None] + jnp.arange(ROWS, dtype=F32)[None, :]).reshape(1, 8 * ROWS)


def split3(v):
    a = v.astype(BF16)
    r = v - a.astype(F32)
    b = r.astype(BF16)
    c = (r - b.astype(F32)).astype(BF16)
    return a, b, c


def pre_kernel(ids_ref, logits_ref, pack_ref, probs_ref, counts_ref):
    ids = ids_ref[...]
    logits = logits_ref[...]
    labels = lax.broadcasted_iota(jnp.int32, (TOK, EXPERTS), 1)
    oh = [(ids[:, k : k + 1] == labels).astype(F32) for k in range(2)]
    both = oh[0] + oh[1]
    row = lax.broadcasted_iota(jnp.int32, (TOK, TOK), 0)
    col = lax.broadcasted_iota(jnp.int32, (TOK, TOK), 1)
    before = (row > col).astype(F32).astype(BF16)
    ranks = jnp.dot(before, both.astype(BF16), preferred_element_type=F32)
    counts_ref[...] = jnp.broadcast_to(jnp.sum(both, axis=0, keepdims=True), (8, EXPERTS))
    index = [
        jnp.sum(oh[k] * (ranks + (CAP * labels).astype(F32)), axis=1, keepdims=True)
        for k in range(2)
    ]
    chosen = [jnp.sum(oh[k] * logits, axis=1, keepdims=True) for k in range(2)]
    top = jnp.maximum(chosen[0], chosen[1])
    w = [jnp.exp(c - top) for c in chosen]
    total = w[0] + w[1]
    e = jnp.exp(logits - jnp.max(logits, axis=1, keepdims=True))
    probs_ref[...] = e / jnp.sum(e, axis=1, keepdims=True)
    lane = lax.broadcasted_iota(jnp.int32, (TOK, 8), 1)
    pack = jnp.zeros((TOK, 8), F32)
    for i, v in enumerate((w[0] / total, w[1] / total, index[0], index[1])):
        pack = jnp.where(lane == i, v, pack)
    pack_ref[...] = pack


def mid_kernel(
    slots_ref,
    pack_ref,
    inv_ref,
    ids_ref,
    probs_ref,
    counts_ref,
    gain_ref,
    hidden_ref,
    grad_ref,
    *refs,
):
    blocks, (logit_ref, partial_ref, dots_ref, left_ref, total_ref) = refs[:8], refs[8:]
    stage, c = pl.program_id(0), pl.program_id(1)

    @pl.when(stage == 0)
    def _():
        picked = jnp.concatenate([b[:ROWS] for b in blocks], axis=0)
        d = lax.dot_general(
            grad_ref[...], picked, (((1,), (1,)), ((), ())), preferred_element_type=F32
        )

        @pl.when(c == 0)
        def _():
            dots_ref[...] = d
            total = counts_ref[...]
            for b in blocks[4:7]:
                other = b[ROWS : ROWS + 8, 0 : 2 * EXPERTS].astype(F32)
                total = total + other[:, :EXPERTS] + other[:, EXPERTS:]
            total_ref[...] = total

        @pl.when(c > 0)
        def _():
            dots_ref[...] += d

    @pl.when((stage == 1) & (c == 0))
    def _():
        pack = pack_ref[...]
        gate = [pack[:, 0:1], pack[:, 1:2]]
        slots = slots_ref[...]
        dots = dots_ref[...]
        gate_dot = [
            jnp.sum(jnp.where(slots == pack[:, 2 + k : 3 + k], dots, 0.0), axis=1, keepdims=True)
            .astype(BF16)
            .astype(F32)
            for k in range(2)
        ]
        mean = gate[0] * gate_dot[0] + gate[1] * gate_dot[1]
        ids = ids_ref[...]
        labels = lax.broadcasted_iota(jnp.int32, (TOK, EXPERTS), 1)
        direct = jnp.zeros((TOK, EXPERTS), F32)
        for k in range(2):
            chosen = gate[k] * (gate_dot[k] - mean)
            direct = direct + jnp.where(ids[:, k : k + 1] == labels, chosen, 0.0)
        probs = probs_ref[...]
        load = total_ref[0:1, :] * (EXPERTS / (2 * TOKENS))
        aux = probs * (load - jnp.sum(probs * load, axis=1, keepdims=True))
        logit = direct + aux
        logit_ref[...] = logit
        left_ref[...] = jnp.concatenate(split3(logit * inv_ref[...]), axis=1)

    @pl.when(stage == 1)
    def _():
        p = lax.dot_general(
            left_ref[...], hidden_ref[...], (((0,), (0,)), ((), ())), preferred_element_type=F32
        )
        p = (p[0:16] + p[16:32] + p[32:48]) * (gain_ref[...] * (1.0 / 128.0))
        for j in range(WIDE // 1024):
            partial_ref[:, c * (WIDE // 1024) + j, :] = p[:, j * 1024 : (j + 1) * 1024]


def last_kernel(
    slots_ref, pack_ref, inv_ref, logit_ref, weight_ref, gain_ref, hidden_ref, grad_ref, *refs
):
    blocks, (out_ref, scaled_ref, normed_ref, left_ref, acc_ref, factor_ref) = refs[:-6], refs[-6:]
    stage, c = pl.program_id(0), pl.program_id(1)
    cols = pl.ds(pl.multiple_of(c * WIDE, WIDE), WIDE)

    @pl.when((stage == 0) & (c == 0))
    def _():
        pack = pack_ref[...]
        slots = slots_ref[...]
        w = jnp.where(slots == pack[:, 2:3], pack[:, 0:1], 0.0)
        w = w + jnp.where(slots == pack[:, 3:4], pack[:, 1:2], 0.0)
        w_hi, w_lo, _ = split3(w)
        l0, l1, l2 = split3(logit_ref[...])
        zero = jnp.zeros_like(l0)
        left_ref[...] = jnp.concatenate(
            [
                jnp.concatenate([w_hi, l0, l0, l0, l2], axis=1),
                jnp.concatenate([w_lo, l1, l1, zero, zero], axis=1),
            ],
            axis=0,
        )
        acc_ref[...] = jnp.zeros_like(acc_ref)

    @pl.when(stage == 0)
    def _():
        r0, r1, r2 = split3(weight_ref[...])
        right = jnp.concatenate([b[...] for b in blocks] + [r0, r1, r2, r0], axis=0)
        both = jnp.dot(left_ref[...], right, preferred_element_type=F32)
        scaled = (both[:TOK] + both[TOK:]) * gain_ref[...]
        scaled_ref[:, cols] = scaled
        hidden = hidden_ref[...]
        normed_ref[:, cols] = hidden
        prod = scaled * hidden.astype(F32)
        acc = acc_ref[...]
        for j in range(WIDE // 128):
            acc = acc + prod[:, j * 128 : (j + 1) * 128]
        acc_ref[...] = acc

    @pl.when((stage == 1) & (c == 0))
    def _():
        inv = inv_ref[...]
        mean = jnp.sum(acc_ref[...], axis=1, keepdims=True) * inv / D
        factor_ref[...] = jnp.broadcast_to(inv * mean, (TOK, 128))

    @pl.when(stage == 1)
    def _():
        inv = inv_ref[...]
        factor = factor_ref[:, 0:1]
        back = inv * (scaled_ref[:, cols] - normed_ref[:, cols].astype(F32) * factor)
        out_ref[...] = (grad_ref[...].astype(F32) + back).astype(BF16)


STEPS = 4
WIDE = D // STEPS


def first(rows):
    return pl.BlockSpec((rows, WIDE), lambda p, c: (0, jnp.where(p == 0, c, STEPS - 1)))


def second(rows):
    return pl.BlockSpec((rows, WIDE), lambda p, c: (0, jnp.where(p == 0, 0, c)))


def params(mib):
    return pltpu.CompilerParams(vmem_limit_bytes=mib * 1024 * 1024)


def sum_x(v):
    a, b, c = [lax.ppermute(v, AXES, xor_perm("x", d)) for d in (1, 2, 3)]
    return (v + a) + (b + c)


def body(
    grad_out, hidden, norm_gain, router_logits, router_weight, expert_ids, expert_grad, expert_out
):
    at = coords()
    gain = norm_gain.reshape(1, D)
    sources = [((at["x"] - s) & 3) * 2 + (at["c"] ^ m) for s, m in ROUTES]
    slots = slot_numbers(sources)

    def block(array, s, m):
        to = ((at["x"] + s) & 3) * 2 + (at["c"] ^ m)
        return lax.dynamic_slice(array, (0, 0, to * CAP, 0), (1, 2, CAP, D)).reshape(ROWS, D)

    ready = [block(expert_out, s, m) for s, m in ROUTES[1:4]]
    ids, *ready = after(expert_ids, *ready)
    outs = [ring_permute(b, s, m) for b, (s, m) in zip(ready, ROUTES[1:4])]

    pack, probs, counts = pl.pallas_call(
        pre_kernel,
        out_shape=(
            jax.ShapeDtypeStruct((TOK, 8), F32),
            jax.ShapeDtypeStruct((TOK, EXPERTS), F32),
            jax.ShapeDtypeStruct((8, EXPERTS), F32),
        ),
        in_specs=[VMEM] * 2,
        out_specs=(VMEM,) * 3,
        compiler_params=params(8),
    )(ids, router_logits)
    wide = hidden.astype(F32)
    inv = lax.rsqrt(jnp.mean(wide * wide, axis=1, keepdims=True) + 1e-05)
    tally = [counts]
    for axis, d in (("y", 1), ("y", 2), ("z", 1), ("z", 2), ("c", 1)):
        tally.append(tally[-1] + lax.ppermute(tally[-1], AXES, xor_perm(axis, d)))
    share = tally[5][0:1].astype(BF16)
    share = jnp.concatenate([share, (tally[5][0:1] - share.astype(F32)).astype(BF16)], axis=1)
    share = jnp.pad(share, ((0, 7), (0, D - 2 * EXPERTS)))

    source, tally[1] = after(expert_out, tally[1])
    ready = [block(source, s, m) for s, m in ROUTES[4:]]
    ready = [jnp.concatenate([b, share], axis=0) for b in ready[:3]] + ready[3:]
    for n, (b, (s, m)) in enumerate(zip(ready, ROUTES[4:])):
        if n != 1:
            b, outs[n % 3] = after(b, outs[n % 3])
        outs.append(ring_permute(b, s, m))
    own_out = block(expert_out, 0, 0)

    source, tally[2] = after(expert_grad, tally[2])
    grads = [block(source, 0, 0)]
    for n, (s, m) in zip((3, 3, 4), ROUTES[1:4]):
        b, outs[n] = after(block(source, s, m), outs[n])
        grads.append(ring_permute(b, s, m))
    source, tally[3] = after(expert_grad, tally[3])
    rest = [block(source, s, m) for s, m in ROUTES[4:]]

    small = lambda *shape: pl.BlockSpec(shape, lambda p, c: (0,) * len(shape))
    logit, partial = pl.pallas_call(
        mid_kernel,
        grid=(2, STEPS),
        out_shape=(
            jax.ShapeDtypeStruct((TOK, EXPERTS), F32),
            jax.ShapeDtypeStruct((EXPERTS, 8, 1024), F32),
        ),
        in_specs=[
            small(1, 8 * ROWS),
            small(TOK, 8),
            small(TOK, 1),
            small(TOK, 2),
            small(TOK, EXPERTS),
            small(8, EXPERTS),
            second(1),
            second(TOK),
            first(TOK),
        ]
        + [first(b.shape[0]) for b in (own_out, *outs)],
        out_specs=(
            small(TOK, EXPERTS),
            small(EXPERTS, 8, 1024),
        ),
        scratch_shapes=[
            pltpu.VMEM((TOK, 8 * ROWS), F32),
            pltpu.VMEM((TOK, 3 * EXPERTS), BF16),
            pltpu.VMEM((8, EXPERTS), F32),
        ],
        cost_estimate=pl.CostEstimate(flops=20_000_000_000, bytes_accessed=60_000_000, transcendentals=0),
        compiler_params=params(20),
    )(slots, pack, inv, expert_ids, probs, tally[5], gain, hidden, grad_out, own_out, *outs)
    partial = jnp.sum(lax.all_to_all(partial, "seq", 0, 0, tiled=True), axis=0)
    partial = partial + lax.ppermute(partial, AXES, xor_perm("c", 1))
    partial, *grads[1:4] = after(partial, *grads[1:4])
    partial = sum_x(partial)
    *rest, partial = after(*rest, partial)
    grads += [ring_permute(b, s, m) for b, (s, m) in zip(rest, ROUTES[4:])]
    router_grad = lax.all_gather(partial, "seq").reshape(EXPERTS, D)

    grad_hidden = pl.pallas_call(
        last_kernel,
        grid=(2, STEPS),
        out_shape=jax.ShapeDtypeStruct((TOK, D), BF16),
        in_specs=[
            small(1, 8 * ROWS),
            small(TOK, 8),
            small(TOK, 1),
            small(TOK, EXPERTS),
            first(EXPERTS),
            first(1),
            first(TOK),
            second(TOK),
        ]
        + [first(g.shape[0]) for g in grads],
        out_specs=second(TOK),
        scratch_shapes=[
            pltpu.VMEM((TOK, D), F32),
            pltpu.VMEM((TOK, D), BF16),
            pltpu.VMEM((2 * TOK, 8 * ROWS + 4 * EXPERTS), BF16),
            pltpu.VMEM((TOK, 128), F32),
            pltpu.VMEM((TOK, 128), F32),
        ],
        compiler_params=params(60),
    )(slots, pack, inv, logit, router_weight, gain, hidden, grad_out, *grads)
    return grad_hidden, router_grad


def solution(mesh):
    rows = P(("seq", "exp"), None)
    in_specs = (
        rows,
        rows,
        P(),
        rows,
        P(),
        rows,
        P("seq", "exp", None, None),
        P("seq", "exp", None, None),
    )
    return jax.shard_map(body, mesh=mesh, in_specs=in_specs, out_specs=(rows, P()), check_vma=False)
```

```python
import jax
import jax.numpy as jnp
from jax import lax
from jax.experimental import pallas as pl
from jax.experimental.pallas import tpu as pltpu
from jax.sharding import PartitionSpec as P

D = 8192
EXPERTS = 16
TOK = 128
CAP = 24
ROWS = 2 * CAP
TOKENS = 16384
AXES = ("seq", "exp")
CHUNK = 1024
F32 = jnp.float32
BF16 = jnp.bfloat16
VMEM = pl.BlockSpec(memory_space=pltpu.VMEM)

ROUTES = ((0, 0), (2, 0), (1, 0), (3, 0), (2, 1), (1, 1), (3, 1), (0, 1))


def coords():
    s, e = lax.axis_index("seq"), lax.axis_index("exp")
    return {"y": s >> 2, "z": s & 3, "x": e >> 1, "c": e & 1}


STRIDE = {"y": 32, "z": 8, "x": 2, "c": 1}
SIZE = {"y": 4, "z": 4, "x": 4, "c": 2}


def shift_perm(axis, d):
    out = []
    for i in range(128):
        a = (i // STRIDE[axis]) % SIZE[axis]
        out.append((i, i + ((a + d) % SIZE[axis] - a) * STRIDE[axis]))
    return out


def xor_perm(axis, d):
    return [(i, i ^ (d * STRIDE[axis])) for i in range(128)]


def after(*xs):
    return lax.optimization_barrier(xs)


def ring_permute(v, s, m):
    perm = [(i, (((i >> 1) + s) % 4) * 2 + ((i & 1) ^ m)) for i in range(8)]
    return lax.ppermute(v, "exp", perm)


def slot_numbers(sources):
    base = jnp.stack(sources).astype(F32) * ROWS
    return (base[:, None] + jnp.arange(ROWS, dtype=F32)[None, :]).reshape(1, 8 * ROWS)


def split3(v):
    a = v.astype(BF16)
    r = v - a.astype(F32)
    b = r.astype(BF16)
    c = (r - b.astype(F32)).astype(BF16)
    return a, b, c


def pre_kernel(ids_ref, logits_ref, pack_ref, probs_ref, counts_ref):
    ids = ids_ref[...]
    logits = logits_ref[...]
    labels = lax.broadcasted_iota(jnp.int32, (TOK, EXPERTS), 1)
    oh = [(ids[:, k : k + 1] == labels).astype(F32) for k in range(2)]
    both = oh[0] + oh[1]
    row = lax.broadcasted_iota(jnp.int32, (TOK, TOK), 0)
    col = lax.broadcasted_iota(jnp.int32, (TOK, TOK), 1)
    before = (row > col).astype(F32).astype(BF16)
    ranks = jnp.dot(before, both.astype(BF16), preferred_element_type=F32)
    counts_ref[...] = jnp.broadcast_to(jnp.sum(both, axis=0, keepdims=True), (8, EXPERTS))
    index = [
        jnp.sum(oh[k] * (ranks + (CAP * labels).astype(F32)), axis=1, keepdims=True)
        for k in range(2)
    ]
    chosen = [jnp.sum(oh[k] * logits, axis=1, keepdims=True) for k in range(2)]
    top = jnp.maximum(chosen[0], chosen[1])
    w = [jnp.exp(c - top) for c in chosen]
    total = w[0] + w[1]
    e = jnp.exp(logits - jnp.max(logits, axis=1, keepdims=True))
    probs_ref[...] = e / jnp.sum(e, axis=1, keepdims=True)
    lane = lax.broadcasted_iota(jnp.int32, (TOK, 8), 1)
    pack = jnp.zeros((TOK, 8), F32)
    for i, v in enumerate((w[0] / total, w[1] / total, index[0], index[1])):
        pack = jnp.where(lane == i, v, pack)
    pack_ref[...] = pack


def mid_kernel(
    slots_ref,
    pack_ref,
    inv_ref,
    ids_ref,
    probs_ref,
    counts_ref,
    gain_ref,
    hidden_ref,
    grad_ref,
    *refs,
):
    blocks, (logit_ref, partial_ref, dots_ref, left_ref, total_ref) = refs[:8], refs[8:]
    stage, c = pl.program_id(0), pl.program_id(1)

    @pl.when(stage == 0)
    def _():
        picked = jnp.concatenate([b[:ROWS] for b in blocks], axis=0)
        d = lax.dot_general(
            grad_ref[...], picked, (((1,), (1,)), ((), ())), preferred_element_type=F32
        )

        @pl.when(c == 0)
        def _():
            dots_ref[...] = d
            total = counts_ref[...]
            for b in blocks[4:7]:
                other = b[ROWS : ROWS + 8, 0 : 2 * EXPERTS].astype(F32)
                total = total + other[:, :EXPERTS] + other[:, EXPERTS:]
            total_ref[...] = total

        @pl.when(c > 0)
        def _():
            dots_ref[...] += d

    @pl.when((stage == 1) & (c == 0))
    def _():
        pack = pack_ref[...]
        gate = [pack[:, 0:1], pack[:, 1:2]]
        slots = slots_ref[...]
        dots = dots_ref[...]
        gate_dot = [
            jnp.sum(jnp.where(slots == pack[:, 2 + k : 3 + k], dots, 0.0), axis=1, keepdims=True)
            .astype(BF16)
            .astype(F32)
            for k in range(2)
        ]
        mean = gate[0] * gate_dot[0] + gate[1] * gate_dot[1]
        ids = ids_ref[...]
        labels = lax.broadcasted_iota(jnp.int32, (TOK, EXPERTS), 1)
        direct = jnp.zeros((TOK, EXPERTS), F32)
        for k in range(2):
            chosen = gate[k] * (gate_dot[k] - mean)
            direct = direct + jnp.where(ids[:, k : k + 1] == labels, chosen, 0.0)
        probs = probs_ref[...]
        load = total_ref[0:1, :] * (EXPERTS / (2 * TOKENS))
        aux = probs * (load - jnp.sum(probs * load, axis=1, keepdims=True))
        logit = direct + aux
        logit_ref[...] = logit
        left_ref[...] = jnp.concatenate(split3(logit * inv_ref[...]), axis=1)

    @pl.when(stage == 1)
    def _():
        p = lax.dot_general(
            left_ref[...], hidden_ref[...], (((0,), (0,)), ((), ())), preferred_element_type=F32
        )
        p = (p[0:16] + p[16:32] + p[32:48]) * (gain_ref[...] * (1.0 / 128.0))
        for j in range(WIDE // 512):
            partial_ref[c // 2, :, (c % 2) * 4 + j, :] = p[:, j * 512 : (j + 1) * 512]


def last_kernel(
    slots_ref, pack_ref, inv_ref, logit_ref, weight_ref, gain_ref, hidden_ref, grad_ref, *refs
):
    blocks, (out_ref, scaled_ref, normed_ref, left_ref, acc_ref, factor_ref) = refs[:-6], refs[-6:]
    stage, c = pl.program_id(0), pl.program_id(1)
    cols = pl.ds(pl.multiple_of(c * WIDE, WIDE), WIDE)

    @pl.when((stage == 0) & (c == 0))
    def _():
        pack = pack_ref[...]
        slots = slots_ref[...]
        w = jnp.where(slots == pack[:, 2:3], pack[:, 0:1], 0.0)
        w = w + jnp.where(slots == pack[:, 3:4], pack[:, 1:2], 0.0)
        w_hi, w_lo, _ = split3(w)
        l0, l1, l2 = split3(logit_ref[...])
        zero = jnp.zeros_like(l0)
        left_ref[...] = jnp.concatenate(
            [
                jnp.concatenate([w_hi, l0, l0, l0, l2], axis=1),
                jnp.concatenate([w_lo, l1, l1, zero, zero], axis=1),
            ],
            axis=0,
        )
        acc_ref[...] = jnp.zeros_like(acc_ref)

    @pl.when(stage == 0)
    def _():
        r0, r1, r2 = split3(weight_ref[...])
        right = jnp.concatenate([b[...] for b in blocks] + [r0, r1, r2, r0], axis=0)
        both = jnp.dot(left_ref[...], right, preferred_element_type=F32)
        scaled = (both[:TOK] + both[TOK:]) * gain_ref[...]
        scaled_ref[:, cols] = scaled
        hidden = hidden_ref[...]
        normed_ref[:, cols] = hidden
        prod = scaled * hidden.astype(F32)
        acc = acc_ref[...]
        for j in range(WIDE // 128):
            acc = acc + prod[:, j * 128 : (j + 1) * 128]
        acc_ref[...] = acc

    @pl.when((stage == 1) & (c == 0))
    def _():
        inv = inv_ref[...]
        mean = jnp.sum(acc_ref[...], axis=1, keepdims=True) * inv / D
        factor_ref[...] = jnp.broadcast_to(inv * mean, (TOK, 128))

    @pl.when(stage == 1)
    def _():
        inv = inv_ref[...]
        factor = factor_ref[:, 0:1]
        back = inv * (scaled_ref[:, cols] - normed_ref[:, cols].astype(F32) * factor)
        out_ref[...] = (grad_ref[...].astype(F32) + back).astype(BF16)


STEPS = 4
WIDE = D // STEPS


def first(rows):
    return pl.BlockSpec((rows, WIDE), lambda p, c: (0, jnp.where(p == 0, c, STEPS - 1)))


def second(rows):
    return pl.BlockSpec((rows, WIDE), lambda p, c: (0, jnp.where(p == 0, 0, c)))


def params(mib):
    return pltpu.CompilerParams(vmem_limit_bytes=mib * 1024 * 1024)


def sum_x(v):
    a, b, c = [lax.ppermute(v, AXES, xor_perm("x", d)) for d in (1, 2, 3)]
    return (v + a) + (b + c)


def body(
    grad_out, hidden, norm_gain, router_logits, router_weight, expert_ids, expert_grad, expert_out
):
    at = coords()
    gain = norm_gain.reshape(1, D)
    sources = [((at["x"] - s) & 3) * 2 + (at["c"] ^ m) for s, m in ROUTES]
    slots = slot_numbers(sources)

    def block(array, s, m):
        to = ((at["x"] + s) & 3) * 2 + (at["c"] ^ m)
        return lax.dynamic_slice(array, (0, 0, to * CAP, 0), (1, 2, CAP, D)).reshape(ROWS, D)

    ready = [block(expert_out, s, m) for s, m in ROUTES[1:4]]
    ids, ready[0] = after(expert_ids, ready[0])
    outs = [ring_permute(b, s, m) for b, (s, m) in zip(ready, ROUTES[1:4])]

    pack, probs, counts = pl.pallas_call(
        pre_kernel,
        out_shape=(
            jax.ShapeDtypeStruct((TOK, 8), F32),
            jax.ShapeDtypeStruct((TOK, EXPERTS), F32),
            jax.ShapeDtypeStruct((8, EXPERTS), F32),
        ),
        in_specs=[VMEM] * 2,
        out_specs=(VMEM,) * 3,
        compiler_params=params(8),
    )(ids, router_logits)
    wide = hidden.astype(F32)
    inv = lax.rsqrt(jnp.mean(wide * wide, axis=1, keepdims=True) + 1e-05)
    tally = [counts]
    for axis, d in (("y", 1), ("y", 2), ("z", 1), ("z", 2), ("c", 1)):
        tally.append(tally[-1] + lax.ppermute(tally[-1], AXES, xor_perm(axis, d)))
    share = tally[5][0:1].astype(BF16)
    share = jnp.concatenate([share, (tally[5][0:1] - share.astype(F32)).astype(BF16)], axis=1)
    share = jnp.pad(share, ((0, 7), (0, D - 2 * EXPERTS)))

    source, tally[1] = after(expert_out, tally[1])
    ready = [block(source, s, m) for s, m in ROUTES[4:]]
    ready = [jnp.concatenate([b, share], axis=0) for b in ready[:3]] + ready[3:]
    for n, (b, (s, m)) in enumerate(zip(ready, ROUTES[4:])):
        if n > 0:
            b, outs[n % 3] = after(b, outs[n % 3])
        outs.append(ring_permute(b, s, m))
    own_out = block(expert_out, 0, 0)

    source, tally[2] = after(expert_grad, tally[2])
    grads = [block(source, 0, 0)]
    for n, (s, m) in zip((4, 5, 5), ROUTES[1:4]):
        b, outs[n] = after(block(source, s, m), outs[n])
        grads.append(ring_permute(b, s, m))
    source, tally[3] = after(expert_grad, tally[3])
    rest = [block(source, s, m) for s, m in ROUTES[4:]]

    small = lambda *shape: pl.BlockSpec(shape, lambda p, c: (0,) * len(shape))
    logit, partial = pl.pallas_call(
        mid_kernel,
        grid=(2, STEPS),
        out_shape=(
            jax.ShapeDtypeStruct((TOK, EXPERTS), F32),
            jax.ShapeDtypeStruct((2, EXPERTS, 8, 512), F32),
        ),
        in_specs=[
            small(1, 8 * ROWS),
            small(TOK, 8),
            small(TOK, 1),
            small(TOK, 2),
            small(TOK, EXPERTS),
            small(8, EXPERTS),
            second(1),
            second(TOK),
            first(TOK),
        ]
        + [first(b.shape[0]) for b in (own_out, *outs)],
        out_specs=(
            small(TOK, EXPERTS),
            small(2, EXPERTS, 8, 512),
        ),
        scratch_shapes=[
            pltpu.VMEM((TOK, 8 * ROWS), F32),
            pltpu.VMEM((TOK, 3 * EXPERTS), BF16),
            pltpu.VMEM((8, EXPERTS), F32),
        ],
        cost_estimate=pl.CostEstimate(flops=20_000_000_000, bytes_accessed=60_000_000, transcendentals=0),
        compiler_params=params(20),
    )(slots, pack, inv, expert_ids, probs, tally[5], gain, hidden, grad_out, own_out, *outs)
    mine, other = [lax.dynamic_index_in_dim(partial, at["c"] ^ i, 0, False) for i in range(2)]
    partial = mine + lax.ppermute(other, AXES, xor_perm("c", 1))
    partial = jnp.sum(lax.all_to_all(partial, "seq", 0, 0, tiled=True), axis=0)
    partial, *grads[1:4] = after(partial, *grads[1:4])
    partial = sum_x(partial)
    *rest, partial = after(*rest, partial)
    grads += [ring_permute(b, s, m) for b, (s, m) in zip(rest, ROUTES[4:])]
    mine = lax.all_gather(partial, "seq").reshape(EXPERTS, D // 2)
    mine, *grads[4:] = after(mine, *grads[4:])
    other = lax.ppermute(mine, AXES, xor_perm("c", 1))
    low = at["c"] == 0
    router_grad = jnp.concatenate([jnp.where(low, mine, other), jnp.where(low, other, mine)], axis=1)

    grad_hidden = pl.pallas_call(
        last_kernel,
        grid=(2, STEPS),
        out_shape=jax.ShapeDtypeStruct((TOK, D), BF16),
        in_specs=[
            small(1, 8 * ROWS),
            small(TOK, 8),
            small(TOK, 1),
            small(TOK, EXPERTS),
            first(EXPERTS),
            first(1),
            first(TOK),
            second(TOK),
        ]
        + [first(g.shape[0]) for g in grads],
        out_specs=second(TOK),
        scratch_shapes=[
            pltpu.VMEM((TOK, D), F32),
            pltpu.VMEM((TOK, D), BF16),
            pltpu.VMEM((2 * TOK, 8 * ROWS + 4 * EXPERTS), BF16),
            pltpu.VMEM((TOK, 128), F32),
            pltpu.VMEM((TOK, 128), F32),
        ],
        compiler_params=params(60),
    )(slots, pack, inv, logit, router_weight, gain, hidden, grad_out, *grads)
    return grad_hidden, router_grad


def solution(mesh):
    rows = P(("seq", "exp"), None)
    in_specs = (
        rows,
        rows,
        P(),
        rows,
        P(),
        rows,
        P("seq", "exp", None, None),
        P("seq", "exp", None, None),
    )
    return jax.shard_map(body, mesh=mesh, in_specs=in_specs, out_specs=(rows, P()), check_vma=False)
```

```python
import jax
import jax.numpy as jnp
from jax import lax
from jax.experimental import pallas as pl
from jax.experimental.pallas import tpu as pltpu
from jax.sharding import PartitionSpec as P

D = 8192
EXPERTS = 16
TOK = 128
CAP = 24
ROWS = 2 * CAP
TOKENS = 16384
AXES = ("seq", "exp")
CHUNK = 1024
F32 = jnp.float32
BF16 = jnp.bfloat16
VMEM = pl.BlockSpec(memory_space=pltpu.VMEM)

ROUTES = ((0, 0), (1, 0), (3, 0), (2, 0), (1, 1), (3, 1), (2, 1), (0, 1))


def coords():
    s, e = lax.axis_index("seq"), lax.axis_index("exp")
    return {"y": s >> 2, "z": s & 3, "x": e >> 1, "c": e & 1}


STRIDE = {"y": 32, "z": 8, "x": 2, "c": 1}
SIZE = {"y": 4, "z": 4, "x": 4, "c": 2}


def shift_perm(axis, d):
    out = []
    for i in range(128):
        a = (i // STRIDE[axis]) % SIZE[axis]
        out.append((i, i + ((a + d) % SIZE[axis] - a) * STRIDE[axis]))
    return out


def xor_perm(axis, d):
    return [(i, i ^ (d * STRIDE[axis])) for i in range(128)]


def after(*xs):
    return lax.optimization_barrier(xs)


def ring_permute(v, s, m):
    perm = [(i, (((i >> 1) + s) % 4) * 2 + ((i & 1) ^ m)) for i in range(8)]
    return lax.ppermute(v, "exp", perm)


def slot_numbers(sources):
    base = jnp.stack(sources).astype(F32) * ROWS
    return (base[:, None] + jnp.arange(ROWS, dtype=F32)[None, :]).reshape(1, 8 * ROWS)


def split3(v):
    a = v.astype(BF16)
    r = v - a.astype(F32)
    b = r.astype(BF16)
    c = (r - b.astype(F32)).astype(BF16)
    return a, b, c


def pre_kernel(ids_ref, logits_ref, pack_ref, probs_ref, counts_ref):
    ids = ids_ref[...]
    logits = logits_ref[...]
    labels = lax.broadcasted_iota(jnp.int32, (TOK, EXPERTS), 1)
    oh = [(ids[:, k : k + 1] == labels).astype(F32) for k in range(2)]
    both = oh[0] + oh[1]
    row = lax.broadcasted_iota(jnp.int32, (TOK, TOK), 0)
    col = lax.broadcasted_iota(jnp.int32, (TOK, TOK), 1)
    before = (row > col).astype(F32).astype(BF16)
    ranks = jnp.dot(before, both.astype(BF16), preferred_element_type=F32)
    counts_ref[...] = jnp.broadcast_to(jnp.sum(both, axis=0, keepdims=True), (8, EXPERTS))
    index = [
        jnp.sum(oh[k] * (ranks + (CAP * labels).astype(F32)), axis=1, keepdims=True)
        for k in range(2)
    ]
    chosen = [jnp.sum(oh[k] * logits, axis=1, keepdims=True) for k in range(2)]
    top = jnp.maximum(chosen[0], chosen[1])
    w = [jnp.exp(c - top) for c in chosen]
    total = w[0] + w[1]
    e = jnp.exp(logits - jnp.max(logits, axis=1, keepdims=True))
    probs_ref[...] = e / jnp.sum(e, axis=1, keepdims=True)
    lane = lax.broadcasted_iota(jnp.int32, (TOK, 8), 1)
    pack = jnp.zeros((TOK, 8), F32)
    for i, v in enumerate((w[0] / total, w[1] / total, index[0], index[1])):
        pack = jnp.where(lane == i, v, pack)
    pack_ref[...] = pack


def mid_kernel(
    slots_ref,
    pack_ref,
    inv_ref,
    ids_ref,
    probs_ref,
    counts_ref,
    gain_ref,
    hidden_ref,
    grad_ref,
    *refs,
):
    blocks, shares = refs[:8], refs[8:11]
    logit_ref, partial_ref, dots_ref, left_ref, total_ref = refs[11:]
    stage, c = pl.program_id(0), pl.program_id(1)

    @pl.when(stage == 0)
    def _():
        picked = jnp.concatenate([b[...] for b in blocks], axis=0)
        d = lax.dot_general(
            grad_ref[...], picked, (((1,), (1,)), ((), ())), preferred_element_type=F32
        )

        @pl.when(c == 0)
        def _():
            dots_ref[...] = d
            total = counts_ref[...]
            for b in shares:
                other = b[...].astype(F32)[0:8]
                total = total + other[:, :EXPERTS] + other[:, EXPERTS : 2 * EXPERTS]
            total_ref[...] = total

        @pl.when(c > 0)
        def _():
            dots_ref[...] += d

    @pl.when((stage == 1) & (c == 0))
    def _():
        pack = pack_ref[...]
        gate = [pack[:, 0:1], pack[:, 1:2]]
        slots = slots_ref[...]
        dots = dots_ref[...]
        gate_dot = [
            jnp.sum(jnp.where(slots == pack[:, 2 + k : 3 + k], dots, 0.0), axis=1, keepdims=True)
            .astype(BF16)
            .astype(F32)
            for k in range(2)
        ]
        mean = gate[0] * gate_dot[0] + gate[1] * gate_dot[1]
        ids = ids_ref[...]
        labels = lax.broadcasted_iota(jnp.int32, (TOK, EXPERTS), 1)
        direct = jnp.zeros((TOK, EXPERTS), F32)
        for k in range(2):
            chosen = gate[k] * (gate_dot[k] - mean)
            direct = direct + jnp.where(ids[:, k : k + 1] == labels, chosen, 0.0)
        probs = probs_ref[...]
        load = total_ref[0:1, :] * (EXPERTS / (2 * TOKENS))
        aux = probs * (load - jnp.sum(probs * load, axis=1, keepdims=True))
        logit = direct + aux
        logit_ref[...] = logit
        left_ref[...] = jnp.concatenate(split3(logit * inv_ref[...]), axis=1)

    @pl.when(stage == 1)
    def _():
        p = lax.dot_general(
            left_ref[...], hidden_ref[...], (((0,), (0,)), ((), ())), preferred_element_type=F32
        )
        p = (p[0:16] + p[16:32] + p[32:48]) * (gain_ref[...] * (1.0 / 128.0))
        for j in range(WIDE // 1024):
            partial_ref[:, c * (WIDE // 1024) + j, :] = p[:, j * 1024 : (j + 1) * 1024]


def weights(slots, pack):
    w = jnp.where(slots == pack[:, 2:3], pack[:, 0:1], 0.0)
    w = w + jnp.where(slots == pack[:, 3:4], pack[:, 1:2], 0.0)
    return split3(w)[:2]


def row_sums(scaled, hidden):
    prod = scaled * hidden.astype(F32)
    total = prod[:, 0:128]
    for j in range(1, WIDE // 128):
        total = total + prod[:, j * 128 : (j + 1) * 128]
    return total


def half_kernel(
    slots_ref, pack_ref, logit_ref, weight_ref, gain_ref, hidden_ref, *refs
):
    blocks, (part_ref, sums_ref, left_ref) = refs[:-3], refs[-3:]
    c = pl.program_id(0)

    @pl.when(c == 0)
    def _():
        w_hi, w_lo = weights(slots_ref[...], pack_ref[...])
        l0, l1, l2 = split3(logit_ref[...])
        zero = jnp.zeros_like(l0)
        left_ref[...] = jnp.concatenate(
            [
                jnp.concatenate([w_hi, l0, l0, l0, l2], axis=1),
                jnp.concatenate([w_lo, l1, l1, zero, zero], axis=1),
            ],
            axis=0,
        )
        sums_ref[...] = jnp.zeros_like(sums_ref)

    r0, r1, r2 = split3(weight_ref[...])
    right = jnp.concatenate([b[...] for b in blocks] + [r0, r1, r2, r0], axis=0)
    both = jnp.dot(left_ref[...], right, preferred_element_type=F32)
    part = (both[:TOK] + both[TOK:]) * gain_ref[...]
    part_ref[...] = part
    sums_ref[...] += row_sums(part, hidden_ref[...])


def last_kernel(
    slots_ref, pack_ref, inv_ref, sums_ref, gain_ref, part_ref, hidden_ref, grad_ref, *refs
):
    blocks, (out_ref, scaled_ref, normed_ref, left_ref, acc_ref, factor_ref) = refs[:-6], refs[-6:]
    stage, c = pl.program_id(0), pl.program_id(1)
    cols = pl.ds(pl.multiple_of(c * WIDE, WIDE), WIDE)

    @pl.when((stage == 0) & (c == 0))
    def _():
        left_ref[...] = jnp.concatenate(weights(slots_ref[...], pack_ref[...]), axis=0)
        acc_ref[...] = sums_ref[...]

    @pl.when(stage == 0)
    def _():
        right = jnp.concatenate([b[...] for b in blocks], axis=0)
        both = jnp.dot(left_ref[...], right, preferred_element_type=F32)
        more = (both[:TOK] + both[TOK:]) * gain_ref[...]
        scaled_ref[:, cols] = part_ref[...] + more
        hidden = hidden_ref[...]
        normed_ref[:, cols] = hidden
        acc_ref[...] += row_sums(more, hidden)

    @pl.when((stage == 1) & (c == 0))
    def _():
        inv = inv_ref[...]
        mean = jnp.sum(acc_ref[...], axis=1, keepdims=True) * inv / D
        factor_ref[...] = jnp.broadcast_to(inv * mean, (TOK, 128))

    @pl.when(stage == 1)
    def _():
        inv = inv_ref[...]
        factor = factor_ref[:, 0:1]
        back = inv * (scaled_ref[:, cols] - normed_ref[:, cols].astype(F32) * factor)
        out_ref[...] = (grad_ref[...].astype(F32) + back).astype(BF16)


STEPS = 4
WIDE = D // STEPS


def first(rows):
    return pl.BlockSpec((rows, WIDE), lambda p, c: (0, jnp.where(p == 0, c, STEPS - 1)))


def second(rows):
    return pl.BlockSpec((rows, WIDE), lambda p, c: (0, jnp.where(p == 0, 0, c)))


def params(mib):
    return pltpu.CompilerParams(vmem_limit_bytes=mib * 1024 * 1024)


def body(
    grad_out, hidden, norm_gain, router_logits, router_weight, expert_ids, expert_grad, expert_out
):
    at = coords()
    gain = norm_gain.reshape(1, D)
    sources = [((at["x"] - s) & 3) * 2 + (at["c"] ^ m) for s, m in ROUTES]
    slots = slot_numbers(sources)

    def block(array, s, m):
        to = ((at["x"] + s) & 3) * 2 + (at["c"] ^ m)
        return lax.dynamic_slice(array, (0, 0, to * CAP, 0), (1, 2, CAP, D)).reshape(ROWS, D)

    ready = [block(expert_out, s, m) for s, m in ROUTES[1:4]]
    ids, *ready = after(expert_ids, *ready)
    outs = [ring_permute(b, s, m) for b, (s, m) in zip(ready, ROUTES[1:4])]

    pack, probs, counts = pl.pallas_call(
        pre_kernel,
        out_shape=(
            jax.ShapeDtypeStruct((TOK, 8), F32),
            jax.ShapeDtypeStruct((TOK, EXPERTS), F32),
            jax.ShapeDtypeStruct((8, EXPERTS), F32),
        ),
        in_specs=[VMEM] * 2,
        out_specs=(VMEM,) * 3,
        compiler_params=params(8),
    )(ids, router_logits)
    wide = hidden.astype(F32)
    inv = lax.rsqrt(jnp.mean(wide * wide, axis=1, keepdims=True) + 1e-05)
    tally = [counts]
    for axis, d in (("y", 1), ("y", 2), ("z", 1), ("z", 2), ("c", 1)):
        tally.append(tally[-1] + lax.ppermute(tally[-1], AXES, xor_perm(axis, d)))
    share = tally[5][0:1].astype(BF16)
    share = jnp.concatenate([share, (tally[5][0:1] - share.astype(F32)).astype(BF16)], axis=1)
    share = jnp.broadcast_to(jnp.pad(share, ((0, 0), (0, 128 - 2 * EXPERTS))), (ROWS, 128))

    source, tally[1] = after(expert_out, tally[1])
    ready = [block(source, s, m) for s, m in ROUTES[4:]]
    ready = [jnp.concatenate([b, share], axis=1) for b in ready[:3]] + ready[3:]
    for n, (b, (s, m)) in enumerate(zip(ready, ROUTES[4:])):
        if n != 1:
            b, outs[n % 3] = after(b, outs[n % 3])
        outs.append(ring_permute(b, s, m))
    own_out = block(expert_out, 0, 0)

    source, tally[2] = after(expert_grad, tally[2])
    grads = [block(source, 0, 0)]
    for n, (s, m) in zip((3, 3, 4), ROUTES[1:4]):
        b, outs[n] = after(block(source, s, m), outs[n])
        grads.append(ring_permute(b, s, m))
    source, tally[3] = after(expert_grad, tally[3])
    rest = [block(source, s, m) for s, m in ROUTES[4:]]

    small = lambda *shape: pl.BlockSpec(shape, lambda p, c: (0,) * len(shape))
    logit, partial = pl.pallas_call(
        mid_kernel,
        grid=(2, STEPS),
        out_shape=(
            jax.ShapeDtypeStruct((TOK, EXPERTS), F32),
            jax.ShapeDtypeStruct((EXPERTS, 8, 1024), F32),
        ),
        in_specs=[
            small(1, 8 * ROWS),
            small(TOK, 8),
            small(TOK, 1),
            small(TOK, 2),
            small(TOK, EXPERTS),
            small(8, EXPERTS),
            second(1),
            second(TOK),
            first(TOK),
        ]
        + [first(ROWS)] * 8
        + [pl.BlockSpec((ROWS, 128), lambda p, c: (0, D // 128))] * 3,
        out_specs=(
            small(TOK, EXPERTS),
            small(EXPERTS, 8, 1024),
        ),
        scratch_shapes=[
            pltpu.VMEM((TOK, 8 * ROWS), F32),
            pltpu.VMEM((TOK, 3 * EXPERTS), BF16),
            pltpu.VMEM((8, EXPERTS), F32),
        ],
        cost_estimate=pl.CostEstimate(flops=20_000_000_000, bytes_accessed=60_000_000, transcendentals=0),
        compiler_params=params(20),
    )(slots, pack, inv, expert_ids, probs, tally[5], gain, hidden, grad_out, own_out, *outs, *outs[3:6])
    partial = jnp.sum(lax.all_to_all(partial, "seq", 0, 0, tiled=True), axis=0)
    partial = partial + lax.ppermute(partial, AXES, xor_perm("c", 1))
    near = [lax.ppermute(partial, AXES, xor_perm("x", d)) for d in (1, 2)]
    partial, *grads[1:4] = after(partial, *grads[1:4])
    partial = (partial + near[0]) + (near[1] + lax.ppermute(partial, AXES, xor_perm("x", 3)))
    partial, *rest = after(partial, *rest)
    grads += [ring_permute(b, s, m) for b, (s, m) in zip(rest, ROUTES[4:])]
    once = lambda rows: pl.BlockSpec((rows, WIDE), lambda c: (0, c))
    fixed = lambda *shape: pl.BlockSpec(shape, lambda c: (0,) * len(shape))
    half = 4 * ROWS
    begin, partial = after(pack, partial)
    part, sums = pl.pallas_call(
        half_kernel,
        grid=(STEPS,),
        out_shape=(
            jax.ShapeDtypeStruct((TOK, D), F32),
            jax.ShapeDtypeStruct((TOK, 128), F32),
        ),
        in_specs=[
            fixed(1, half),
            fixed(TOK, 8),
            fixed(TOK, EXPERTS),
            once(EXPERTS),
            once(1),
            once(TOK),
        ]
        + [once(ROWS)] * 4,
        out_specs=(once(TOK), fixed(TOK, 128)),
        scratch_shapes=[pltpu.VMEM((2 * TOK, half + 4 * EXPERTS), BF16)],
        compiler_params=params(24),
        cost_estimate=pl.CostEstimate(flops=10_000_000_000, bytes_accessed=30_000_000, transcendentals=0),
    )(slots[:, :half], begin, logit, router_weight, gain, hidden, *grads[:4])
    partial, sums = after(partial, sums)
    router_grad = lax.all_gather(partial, "seq").reshape(EXPERTS, D)

    grad_hidden = pl.pallas_call(
        last_kernel,
        grid=(2, STEPS),
        out_shape=jax.ShapeDtypeStruct((TOK, D), BF16),
        in_specs=[
            small(1, half),
            small(TOK, 8),
            small(TOK, 1),
            small(TOK, 128),
            first(1),
            first(TOK),
            first(TOK),
            second(TOK),
        ]
        + [first(ROWS)] * 4,
        out_specs=second(TOK),
        scratch_shapes=[
            pltpu.VMEM((TOK, D), F32),
            pltpu.VMEM((TOK, D), BF16),
            pltpu.VMEM((2 * TOK, half), BF16),
            pltpu.VMEM((TOK, 128), F32),
            pltpu.VMEM((TOK, 128), F32),
        ],
        compiler_params=params(60),
    )(slots[:, half:], pack, inv, sums, gain, part, hidden, grad_out, *grads[4:])
    return grad_hidden, router_grad


def solution(mesh):
    rows = P(("seq", "exp"), None)
    in_specs = (
        rows,
        rows,
        P(),
        rows,
        P(),
        rows,
        P("seq", "exp", None, None),
        P("seq", "exp", None, None),
    )
    return jax.shard_map(body, mesh=mesh, in_specs=in_specs, out_specs=(rows, P()), check_vma=False)
```

```python
import jax
import jax.numpy as jnp
from jax import lax
from jax.experimental import pallas as pl
from jax.experimental.pallas import tpu as pltpu
from jax.sharding import PartitionSpec as P

D = 8192
EXPERTS = 16
TOK = 128
CAP = 24
ROWS = 2 * CAP
TOKENS = 16384
AXES = ("seq", "exp")
CHUNK = 1024
F32 = jnp.float32
BF16 = jnp.bfloat16
VMEM = pl.BlockSpec(memory_space=pltpu.VMEM)

ROUTES = ((0, 0), (1, 0), (3, 0), (2, 0), (1, 1), (3, 1), (2, 1), (0, 1))


def coords():
    s, e = lax.axis_index("seq"), lax.axis_index("exp")
    return {"y": s >> 2, "z": s & 3, "x": e >> 1, "c": e & 1}


STRIDE = {"y": 32, "z": 8, "x": 2, "c": 1}
SIZE = {"y": 4, "z": 4, "x": 4, "c": 2}


def shift_perm(axis, d):
    out = []
    for i in range(128):
        a = (i // STRIDE[axis]) % SIZE[axis]
        out.append((i, i + ((a + d) % SIZE[axis] - a) * STRIDE[axis]))
    return out


def xor_perm(axis, d):
    return [(i, i ^ (d * STRIDE[axis])) for i in range(128)]


def after(*xs):
    return lax.optimization_barrier(xs)


def ring_permute(v, s, m):
    perm = [(i, (((i >> 1) + s) % 4) * 2 + ((i & 1) ^ m)) for i in range(8)]
    return lax.ppermute(v, "exp", perm)


def slot_numbers(sources):
    base = jnp.stack(sources).astype(F32) * ROWS
    return (base[:, None] + jnp.arange(ROWS, dtype=F32)[None, :]).reshape(1, 8 * ROWS)


def split3(v):
    a = v.astype(BF16)
    r = v - a.astype(F32)
    b = r.astype(BF16)
    c = (r - b.astype(F32)).astype(BF16)
    return a, b, c


def pre_kernel(ids_ref, logits_ref, pack_ref, probs_ref, counts_ref):
    ids = ids_ref[...]
    logits = logits_ref[...]
    labels = lax.broadcasted_iota(jnp.int32, (TOK, EXPERTS), 1)
    oh = [(ids[:, k : k + 1] == labels).astype(F32) for k in range(2)]
    both = oh[0] + oh[1]
    row = lax.broadcasted_iota(jnp.int32, (TOK, TOK), 0)
    col = lax.broadcasted_iota(jnp.int32, (TOK, TOK), 1)
    before = (row > col).astype(F32).astype(BF16)
    ranks = jnp.dot(before, both.astype(BF16), preferred_element_type=F32)
    counts_ref[...] = jnp.broadcast_to(jnp.sum(both, axis=0, keepdims=True), (8, EXPERTS))
    index = [
        jnp.sum(oh[k] * (ranks + (CAP * labels).astype(F32)), axis=1, keepdims=True)
        for k in range(2)
    ]
    chosen = [jnp.sum(oh[k] * logits, axis=1, keepdims=True) for k in range(2)]
    top = jnp.maximum(chosen[0], chosen[1])
    w = [jnp.exp(c - top) for c in chosen]
    total = w[0] + w[1]
    e = jnp.exp(logits - jnp.max(logits, axis=1, keepdims=True))
    probs_ref[...] = e / jnp.sum(e, axis=1, keepdims=True)
    lane = lax.broadcasted_iota(jnp.int32, (TOK, 8), 1)
    pack = jnp.zeros((TOK, 8), F32)
    for i, v in enumerate((w[0] / total, w[1] / total, index[0], index[1])):
        pack = jnp.where(lane == i, v, pack)
    pack_ref[...] = pack


def mid_kernel(
    slots_ref,
    pack_ref,
    inv_ref,
    ids_ref,
    probs_ref,
    counts_ref,
    gain_ref,
    hidden_ref,
    grad_ref,
    *refs,
):
    blocks, shares = refs[:8], refs[8:11]
    logit_ref, partial_ref, dots_ref, left_ref, total_ref = refs[11:]
    stage, c = pl.program_id(0), pl.program_id(1)

    @pl.when(stage == 0)
    def _():
        picked = jnp.concatenate([b[...] for b in blocks], axis=0)
        d = lax.dot_general(
            grad_ref[...], picked, (((1,), (1,)), ((), ())), preferred_element_type=F32
        )

        @pl.when(c == 0)
        def _():
            dots_ref[...] = d
            total = counts_ref[...]
            for b in shares:
                other = b[...].astype(F32)[0:8]
                total = total + other[:, :EXPERTS] + other[:, EXPERTS : 2 * EXPERTS]
            total_ref[...] = total

        @pl.when(c > 0)
        def _():
            dots_ref[...] += d

    @pl.when((stage == 1) & (c == 0))
    def _():
        pack = pack_ref[...]
        gate = [pack[:, 0:1], pack[:, 1:2]]
        slots = slots_ref[...]
        dots = dots_ref[...]
        gate_dot = [
            jnp.sum(jnp.where(slots == pack[:, 2 + k : 3 + k], dots, 0.0), axis=1, keepdims=True)
            .astype(BF16)
            .astype(F32)
            for k in range(2)
        ]
        mean = gate[0] * gate_dot[0] + gate[1] * gate_dot[1]
        ids = ids_ref[...]
        labels = lax.broadcasted_iota(jnp.int32, (TOK, EXPERTS), 1)
        direct = jnp.zeros((TOK, EXPERTS), F32)
        for k in range(2):
            chosen = gate[k] * (gate_dot[k] - mean)
            direct = direct + jnp.where(ids[:, k : k + 1] == labels, chosen, 0.0)
        probs = probs_ref[...]
        load = total_ref[0:1, :] * (EXPERTS / (2 * TOKENS))
        aux = probs * (load - jnp.sum(probs * load, axis=1, keepdims=True))
        logit = direct + aux
        logit = logit * inv_ref[...]
        logit_ref[...] = logit
        left_ref[...] = jnp.concatenate(split3(logit), axis=1)

    @pl.when(stage == 1)
    def _():
        p = lax.dot_general(
            left_ref[...], hidden_ref[...], (((0,), (0,)), ((), ())), preferred_element_type=F32
        )
        p = (p[0:16] + p[16:32] + p[32:48]) * (gain_ref[...] * (1.0 / 128.0))
        for j in range(WIDE // 1024):
            partial_ref[:, c * (WIDE // 1024) + j, :] = p[:, j * 1024 : (j + 1) * 1024]


def weights(slots, pack, inv):
    w = jnp.where(slots == pack[:, 2:3], pack[:, 0:1], 0.0)
    w = w + jnp.where(slots == pack[:, 3:4], pack[:, 1:2], 0.0)
    return split3(w * inv)[:2]


def row_sums(scaled, hidden):
    prod = scaled * hidden.astype(F32)
    total = prod[:, 0:128]
    for j in range(1, WIDE // 128):
        total = total + prod[:, j * 128 : (j + 1) * 128]
    return total


def half_kernel(
    slots_ref, pack_ref, inv_ref, logit_ref, weight_ref, gain_ref, hidden_ref, grad_ref, *refs
):
    blocks, (part_ref, sums_ref, left_ref) = refs[:-3], refs[-3:]
    c = pl.program_id(0)

    @pl.when(c == 0)
    def _():
        w_hi, w_lo = weights(slots_ref[...], pack_ref[...], inv_ref[...])
        l0, l1, l2 = split3(logit_ref[...])
        left_ref[...] = jnp.concatenate([w_hi, w_lo, l0, l0, l0, l1, l1, l2], axis=1)
        sums_ref[...] = jnp.zeros_like(sums_ref)

    r0, r1, r2 = split3(weight_ref[...])
    rows = [b[...] for b in blocks]
    right = jnp.concatenate(rows + rows + [r0, r1, r2, r0, r1, r0], axis=0)
    scaled = jnp.dot(left_ref[...], right, preferred_element_type=F32) * gain_ref[...]
    part_ref[...] = grad_ref[...].astype(F32) + scaled
    sums_ref[...] += row_sums(scaled, hidden_ref[...])


def last_kernel(
    slots_ref, pack_ref, inv_ref, sums_ref, gain_ref, part_ref, hidden_ref, *refs
):
    blocks, (out_ref, part_scr, left_ref, acc_ref, factor_ref) = refs[:-5], refs[-5:]
    stage, c = pl.program_id(0), pl.program_id(1)
    cols = pl.ds(pl.multiple_of(c * WIDE, WIDE), WIDE)

    @pl.when((stage == 0) & (c == 0))
    def _():
        left_ref[...] = jnp.concatenate(
            weights(slots_ref[...], pack_ref[...], inv_ref[...]), axis=1
        )
        acc_ref[...] = sums_ref[...]

    @pl.when(stage == 0)
    def _():
        rows = [b[...] for b in blocks]
        right = jnp.concatenate(rows + rows, axis=0)
        scaled = jnp.dot(left_ref[...], right, preferred_element_type=F32) * gain_ref[...]
        part_scr[:, cols] = part_ref[...] + scaled
        acc_ref[...] += row_sums(scaled, hidden_ref[...])

    @pl.when((stage == 1) & (c == 0))
    def _():
        inv = inv_ref[...]
        mean = jnp.sum(acc_ref[...], axis=1, keepdims=True) / D
        factor_ref[...] = jnp.broadcast_to(inv * inv * mean, (TOK, 128))

    @pl.when(stage == 1)
    def _():
        normed = hidden_ref[...].astype(F32) * factor_ref[:, 0:1]
        out_ref[...] = (part_scr[:, cols] - normed).astype(BF16)


STEPS = 4
WIDE = D // STEPS


def first(rows):
    return pl.BlockSpec((rows, WIDE), lambda p, c: (0, jnp.where(p == 0, c, STEPS - 1)))


def twice(rows):
    return pl.BlockSpec((rows, WIDE), lambda p, c: (0, c))


def second(rows):
    return pl.BlockSpec((rows, WIDE), lambda p, c: (0, jnp.where(p == 0, 0, c)))


def params(mib):
    return pltpu.CompilerParams(vmem_limit_bytes=mib * 1024 * 1024)


def body(
    grad_out, hidden, norm_gain, router_logits, router_weight, expert_ids, expert_grad, expert_out
):
    at = coords()
    gain = norm_gain.reshape(1, D)
    sources = [((at["x"] - s) & 3) * 2 + (at["c"] ^ m) for s, m in ROUTES]
    slots = slot_numbers(sources)

    def block(array, s, m):
        to = ((at["x"] + s) & 3) * 2 + (at["c"] ^ m)
        return lax.dynamic_slice(array, (0, 0, to * CAP, 0), (1, 2, CAP, D)).reshape(ROWS, D)

    ready = [block(expert_out, s, m) for s, m in ROUTES[1:4]]
    ids, *ready = after(expert_ids, *ready)
    outs = [ring_permute(b, s, m) for b, (s, m) in zip(ready, ROUTES[1:4])]

    pack, probs, counts = pl.pallas_call(
        pre_kernel,
        out_shape=(
            jax.ShapeDtypeStruct((TOK, 8), F32),
            jax.ShapeDtypeStruct((TOK, EXPERTS), F32),
            jax.ShapeDtypeStruct((8, EXPERTS), F32),
        ),
        in_specs=[VMEM] * 2,
        out_specs=(VMEM,) * 3,
        compiler_params=params(8),
    )(ids, router_logits)
    wide = hidden.astype(F32)
    inv = lax.rsqrt(jnp.mean(wide * wide, axis=1, keepdims=True) + 1e-05)
    tally = [counts]
    for axis, d in (("y", 1), ("y", 2), ("z", 1), ("z", 2), ("c", 1)):
        tally.append(tally[-1] + lax.ppermute(tally[-1], AXES, xor_perm(axis, d)))
    share = tally[5][0:1].astype(BF16)
    share = jnp.concatenate([share, (tally[5][0:1] - share.astype(F32)).astype(BF16)], axis=1)
    share = jnp.broadcast_to(jnp.pad(share, ((0, 0), (0, 128 - 2 * EXPERTS))), (ROWS, 128))

    source, tally[1] = after(expert_out, tally[1])
    ready = [block(source, s, m) for s, m in ROUTES[4:]]
    ready = [jnp.concatenate([b, share], axis=1) for b in ready[:3]] + ready[3:]
    for n, (b, (s, m)) in enumerate(zip(ready, ROUTES[4:])):
        if n != 1:
            b, outs[n % 3] = after(b, outs[n % 3])
        outs.append(ring_permute(b, s, m))
    own_out = block(expert_out, 0, 0)

    source, tally[2] = after(expert_grad, tally[2])
    grads = [block(source, 0, 0)]
    for n, (s, m) in zip((3, 3, 4), ROUTES[1:4]):
        b, outs[n] = after(block(source, s, m), outs[n])
        grads.append(ring_permute(b, s, m))
    source, tally[3] = after(expert_grad, tally[3])
    rest = [block(source, s, m) for s, m in ROUTES[4:]]

    small = lambda *shape: pl.BlockSpec(shape, lambda p, c: (0,) * len(shape))
    logit, partial = pl.pallas_call(
        mid_kernel,
        grid=(2, STEPS),
        out_shape=(
            jax.ShapeDtypeStruct((TOK, EXPERTS), F32),
            jax.ShapeDtypeStruct((EXPERTS, 8, 1024), F32),
        ),
        in_specs=[
            small(1, 8 * ROWS),
            small(TOK, 8),
            small(TOK, 1),
            small(TOK, 2),
            small(TOK, EXPERTS),
            small(8, EXPERTS),
            second(1),
            second(TOK),
            first(TOK),
        ]
        + [first(ROWS)] * 8
        + [pl.BlockSpec((ROWS, 128), lambda p, c: (0, D // 128))] * 3,
        out_specs=(
            small(TOK, EXPERTS),
            small(EXPERTS, 8, 1024),
        ),
        scratch_shapes=[
            pltpu.VMEM((TOK, 8 * ROWS), F32),
            pltpu.VMEM((TOK, 3 * EXPERTS), BF16),
            pltpu.VMEM((8, EXPERTS), F32),
        ],
        cost_estimate=pl.CostEstimate(flops=20_000_000_000, bytes_accessed=60_000_000, transcendentals=0),
        compiler_params=params(20),
    )(slots, pack, inv, expert_ids, probs, tally[5], gain, hidden, grad_out, own_out, *outs, *outs[3:6])
    partial = jnp.sum(lax.all_to_all(partial, "seq", 0, 0, tiled=True), axis=0)
    partial = partial + lax.ppermute(partial, AXES, xor_perm("c", 1))
    near = [lax.ppermute(partial, AXES, xor_perm("x", d)) for d in (1, 2)]
    partial, *grads[1:4] = after(partial, *grads[1:4])
    partial = (partial + near[0]) + (near[1] + lax.ppermute(partial, AXES, xor_perm("x", 3)))
    partial, *rest = after(partial, *rest)
    grads += [ring_permute(b, s, m) for b, (s, m) in zip(rest, ROUTES[4:])]
    once = lambda rows: pl.BlockSpec((rows, WIDE), lambda c: (0, c))
    fixed = lambda *shape: pl.BlockSpec(shape, lambda c: (0,) * len(shape))
    half = 4 * ROWS
    begin, partial = after(pack, partial)
    part, sums = pl.pallas_call(
        half_kernel,
        grid=(STEPS,),
        out_shape=(
            jax.ShapeDtypeStruct((TOK, D), F32),
            jax.ShapeDtypeStruct((TOK, 128), F32),
        ),
        in_specs=[
            fixed(1, half),
            fixed(TOK, 8),
            fixed(TOK, 1),
            fixed(TOK, EXPERTS),
            once(EXPERTS),
            once(1),
            once(TOK),
            once(TOK),
        ]
        + [once(ROWS)] * 4,
        out_specs=(once(TOK), fixed(TOK, 128)),
        scratch_shapes=[pltpu.VMEM((TOK, 2 * half + 6 * EXPERTS), BF16)],
        compiler_params=params(24),
        cost_estimate=pl.CostEstimate(
            flops=10_000_000_000, bytes_accessed=30_000_000, transcendentals=0
        ),
    )(slots[:, :half], begin, inv, logit, router_weight, gain, hidden, grad_out, *grads[:4])
    partial, sums = after(partial, sums)
    router_grad = lax.all_gather(partial, "seq").reshape(EXPERTS, D)

    grad_hidden = pl.pallas_call(
        last_kernel,
        grid=(2, STEPS),
        out_shape=jax.ShapeDtypeStruct((TOK, D), BF16),
        in_specs=[
            small(1, half),
            small(TOK, 8),
            small(TOK, 1),
            small(TOK, 128),
            first(1),
            first(TOK),
            twice(TOK),
        ]
        + [first(ROWS)] * 4,
        out_specs=second(TOK),
        scratch_shapes=[
            pltpu.VMEM((TOK, D), F32),
            pltpu.VMEM((TOK, 2 * half), BF16),
            pltpu.VMEM((TOK, 128), F32),
            pltpu.VMEM((TOK, 128), F32),
        ],
        compiler_params=params(24),
    )(slots[:, half:], pack, inv, sums, gain, part, hidden, *grads[4:])
    return grad_hidden, router_grad


def solution(mesh):
    rows = P(("seq", "exp"), None)
    in_specs = (
        rows,
        rows,
        P(),
        rows,
        P(),
        rows,
        P("seq", "exp", None, None),
        P("seq", "exp", None, None),
    )
    return jax.shard_map(body, mesh=mesh, in_specs=in_specs, out_specs=(rows, P()), check_vma=False)
```

```python
import jax
import jax.numpy as jnp
from jax import lax
from jax.experimental import pallas as pl
from jax.experimental.pallas import tpu as pltpu
from jax.sharding import PartitionSpec as P

D = 8192
EXPERTS = 16
TOK = 128
CAP = 24
ROWS = 2 * CAP
TOKENS = 16384
AXES = ("seq", "exp")
CHUNK = 1024
F32 = jnp.float32
BF16 = jnp.bfloat16
VMEM = pl.BlockSpec(memory_space=pltpu.VMEM)

ROUTES = ((0, 0), (1, 0), (3, 0), (2, 0), (1, 1), (3, 1), (2, 1), (0, 1))


def coords():
    s, e = lax.axis_index("seq"), lax.axis_index("exp")
    return {"y": s >> 2, "z": s & 3, "x": e >> 1, "c": e & 1}


STRIDE = {"y": 32, "z": 8, "x": 2, "c": 1}
SIZE = {"y": 4, "z": 4, "x": 4, "c": 2}


def shift_perm(axis, d):
    out = []
    for i in range(128):
        a = (i // STRIDE[axis]) % SIZE[axis]
        out.append((i, i + ((a + d) % SIZE[axis] - a) * STRIDE[axis]))
    return out


def xor_perm(axis, d):
    return [(i, i ^ (d * STRIDE[axis])) for i in range(128)]


def after(*xs):
    return lax.optimization_barrier(xs)


def ring_permute(v, s, m):
    perm = [(i, (((i >> 1) + s) % 4) * 2 + ((i & 1) ^ m)) for i in range(8)]
    return lax.ppermute(v, "exp", perm)


def slot_numbers(sources):
    base = jnp.stack(sources).astype(F32) * ROWS
    return (base[:, None] + jnp.arange(ROWS, dtype=F32)[None, :]).reshape(1, 8 * ROWS)


def split3(v):
    a = v.astype(BF16)
    r = v - a.astype(F32)
    b = r.astype(BF16)
    c = (r - b.astype(F32)).astype(BF16)
    return a, b, c


def pre_kernel(ids_ref, logits_ref, pack_ref, probs_ref, counts_ref):
    ids = ids_ref[...]
    logits = logits_ref[...]
    labels = lax.broadcasted_iota(jnp.int32, (TOK, EXPERTS), 1)
    oh = [(ids[:, k : k + 1] == labels).astype(F32) for k in range(2)]
    both = oh[0] + oh[1]
    row = lax.broadcasted_iota(jnp.int32, (TOK, TOK), 0)
    col = lax.broadcasted_iota(jnp.int32, (TOK, TOK), 1)
    before = (row > col).astype(F32).astype(BF16)
    ranks = jnp.dot(before, both.astype(BF16), preferred_element_type=F32)
    counts_ref[...] = jnp.broadcast_to(jnp.sum(both, axis=0, keepdims=True), (8, EXPERTS))
    index = [
        jnp.sum(oh[k] * (ranks + (CAP * labels).astype(F32)), axis=1, keepdims=True)
        for k in range(2)
    ]
    chosen = [jnp.sum(oh[k] * logits, axis=1, keepdims=True) for k in range(2)]
    top = jnp.maximum(chosen[0], chosen[1])
    w = [jnp.exp(c - top) for c in chosen]
    total = w[0] + w[1]
    e = jnp.exp(logits - jnp.max(logits, axis=1, keepdims=True))
    probs_ref[...] = e / jnp.sum(e, axis=1, keepdims=True)
    lane = lax.broadcasted_iota(jnp.int32, (TOK, 8), 1)
    pack = jnp.zeros((TOK, 8), F32)
    for i, v in enumerate((w[0] / total, w[1] / total, index[0], index[1])):
        pack = jnp.where(lane == i, v, pack)
    pack_ref[...] = pack


def mid_kernel(
    slots_ref,
    pack_ref,
    inv_ref,
    ids_ref,
    probs_ref,
    counts_ref,
    gain_ref,
    hidden_ref,
    grad_ref,
    *refs,
):
    blocks, shares = refs[:8], refs[8:11]
    logit_ref, partial_ref, dots_ref, left_ref, total_ref = refs[11:]
    stage, c = pl.program_id(0), pl.program_id(1)

    @pl.when(stage == 0)
    def _():
        picked = jnp.concatenate([b[...] for b in blocks], axis=0)
        d = lax.dot_general(
            grad_ref[...], picked, (((1,), (1,)), ((), ())), preferred_element_type=F32
        )

        @pl.when(c == 0)
        def _():
            dots_ref[...] = d
            total = counts_ref[...]
            for b in shares:
                other = b[...].astype(F32)[0:8]
                total = total + other[:, :EXPERTS] + other[:, EXPERTS : 2 * EXPERTS]
            total_ref[...] = total

        @pl.when(c > 0)
        def _():
            dots_ref[...] += d

    @pl.when((stage == 1) & (c == 0))
    def _():
        pack = pack_ref[...]
        gate = [pack[:, 0:1], pack[:, 1:2]]
        slots = slots_ref[...]
        dots = dots_ref[...]
        gate_dot = [
            jnp.sum(jnp.where(slots == pack[:, 2 + k : 3 + k], dots, 0.0), axis=1, keepdims=True)
            .astype(BF16)
            .astype(F32)
            for k in range(2)
        ]
        mean = gate[0] * gate_dot[0] + gate[1] * gate_dot[1]
        ids = ids_ref[...]
        labels = lax.broadcasted_iota(jnp.int32, (TOK, EXPERTS), 1)
        direct = jnp.zeros((TOK, EXPERTS), F32)
        for k in range(2):
            chosen = gate[k] * (gate_dot[k] - mean)
            direct = direct + jnp.where(ids[:, k : k + 1] == labels, chosen, 0.0)
        probs = probs_ref[...]
        load = total_ref[0:1, :] * (EXPERTS / (2 * TOKENS))
        aux = probs * (load - jnp.sum(probs * load, axis=1, keepdims=True))
        logit = direct + aux
        logit = logit * inv_ref[...]
        logit_ref[...] = logit
        left_ref[...] = jnp.concatenate(split3(logit), axis=1)

    @pl.when(stage == 1)
    def _():
        p = lax.dot_general(
            left_ref[...], hidden_ref[...], (((0,), (0,)), ((), ())), preferred_element_type=F32
        )
        p = (p[0:16] + p[16:32] + p[32:48]) * (gain_ref[...] * (1.0 / 128.0))
        for j in range(WIDE // 1024):
            partial_ref[:, c * (WIDE // 1024) + j, :] = p[:, j * 1024 : (j + 1) * 1024]


def weights(slots, pack, inv):
    w = jnp.where(slots == pack[:, 2:3], pack[:, 0:1], 0.0)
    w = w + jnp.where(slots == pack[:, 3:4], pack[:, 1:2], 0.0)
    return split3(w * inv)[:2]


def row_sums(scaled, hidden):
    prod = scaled * hidden.astype(F32)
    total = prod[:, 0:128]
    for j in range(1, WIDE // 128):
        total = total + prod[:, j * 128 : (j + 1) * 128]
    return total


def half_kernel(
    slots_ref, pack_ref, inv_ref, logit_ref, weight_ref, gain_ref, hidden_ref, grad_ref, *refs
):
    blocks, (part_ref, sums_ref, left_ref) = refs[:-3], refs[-3:]
    c = pl.program_id(0)

    @pl.when(c == 0)
    def _():
        w_hi, w_lo = weights(slots_ref[...], pack_ref[...], inv_ref[...])
        l0, l1, l2 = split3(logit_ref[...])
        left_ref[...] = jnp.concatenate([w_hi, w_lo, l0, l0, l0, l1, l1, l2], axis=1)
        sums_ref[...] = jnp.zeros_like(sums_ref)

    r0, r1, r2 = split3(weight_ref[...])
    rows = [b[...] for b in blocks]
    right = jnp.concatenate(rows + rows + [r0, r1, r2, r0, r1, r0], axis=0)
    scaled = jnp.dot(left_ref[...], right, preferred_element_type=F32) * gain_ref[...]
    part_ref[...] = grad_ref[...].astype(F32) + scaled
    sums_ref[...] += row_sums(scaled, hidden_ref[...])


def last_kernel(
    slots_ref, pack_ref, inv_ref, sums_ref, gain_ref, part_ref, hidden_ref, *refs
):
    blocks, (out_ref, part_scr, left_ref, acc_ref, factor_ref) = refs[:-5], refs[-5:]
    stage, c = pl.program_id(0), pl.program_id(1)
    cols = pl.ds(pl.multiple_of(c * WIDE, WIDE), WIDE)

    @pl.when((stage == 0) & (c == 0))
    def _():
        left_ref[...] = jnp.concatenate(
            weights(slots_ref[...], pack_ref[...], inv_ref[...]), axis=1
        )
        acc_ref[...] = sums_ref[...]

    @pl.when(stage == 0)
    def _():
        rows = [b[...] for b in blocks]
        right = jnp.concatenate(rows + rows, axis=0)
        scaled = jnp.dot(left_ref[...], right, preferred_element_type=F32) * gain_ref[...]
        part_scr[:, cols] = part_ref[...] + scaled
        acc_ref[...] += row_sums(scaled, hidden_ref[...])

    @pl.when((stage == 1) & (c == 0))
    def _():
        inv = inv_ref[...]
        mean = jnp.sum(acc_ref[...], axis=1, keepdims=True) / D
        factor_ref[...] = jnp.broadcast_to(inv * inv * mean, (TOK, 128))

    @pl.when(stage == 1)
    def _():
        normed = hidden_ref[...].astype(F32) * factor_ref[:, 0:1]
        out_ref[...] = (part_scr[:, cols] - normed).astype(BF16)


STEPS = 4
WIDE = D // STEPS


def first(rows):
    return pl.BlockSpec((rows, WIDE), lambda p, c: (0, jnp.where(p == 0, c, STEPS - 1)))


def twice(rows):
    return pl.BlockSpec((rows, WIDE), lambda p, c: (0, c))


def second(rows):
    return pl.BlockSpec((rows, WIDE), lambda p, c: (0, jnp.where(p == 0, 0, c)))


def params(mib):
    return pltpu.CompilerParams(vmem_limit_bytes=mib * 1024 * 1024)


def body(
    grad_out, hidden, norm_gain, router_logits, router_weight, expert_ids, expert_grad, expert_out
):
    at = coords()
    gain = norm_gain.reshape(1, D)
    sources = [((at["x"] - s) & 3) * 2 + (at["c"] ^ m) for s, m in ROUTES]
    slots = slot_numbers(sources)

    def block(array, s, m):
        to = ((at["x"] + s) & 3) * 2 + (at["c"] ^ m)
        return lax.dynamic_slice(array, (0, 0, to * CAP, 0), (1, 2, CAP, D)).reshape(ROWS, D)

    ready = [block(expert_out, s, m) for s, m in ROUTES[1:4]]
    ids, *ready = after(expert_ids, *ready)
    outs = [ring_permute(b, s, m) for b, (s, m) in zip(ready, ROUTES[1:4])]

    pack, probs, counts = pl.pallas_call(
        pre_kernel,
        out_shape=(
            jax.ShapeDtypeStruct((TOK, 8), F32),
            jax.ShapeDtypeStruct((TOK, EXPERTS), F32),
            jax.ShapeDtypeStruct((8, EXPERTS), F32),
        ),
        in_specs=[VMEM] * 2,
        out_specs=(VMEM,) * 3,
        compiler_params=params(8),
    )(ids, router_logits)
    wide = hidden.astype(F32)
    inv = lax.rsqrt(jnp.mean(wide * wide, axis=1, keepdims=True) + 1e-05)
    tally = [counts]
    for axis, d in (("y", 1), ("y", 2), ("z", 1), ("z", 2), ("c", 1)):
        tally.append(tally[-1] + lax.ppermute(tally[-1], AXES, xor_perm(axis, d)))
    share = tally[5][0:1].astype(BF16)
    share = jnp.concatenate([share, (tally[5][0:1] - share.astype(F32)).astype(BF16)], axis=1)
    share = jnp.broadcast_to(jnp.pad(share, ((0, 0), (0, 128 - 2 * EXPERTS))), (ROWS, 128))

    source, tally[1] = after(expert_out, tally[1])
    ready = [block(source, s, m) for s, m in ROUTES[4:]]
    ready = [jnp.concatenate([b, share], axis=1) for b in ready[:3]] + ready[3:]
    for n, (b, (s, m)) in enumerate(zip(ready, ROUTES[4:])):
        if n != 1:
            b, outs[n % 3] = after(b, outs[n % 3])
        outs.append(ring_permute(b, s, m))
    own_out = block(expert_out, 0, 0)

    source, tally[2] = after(expert_grad, tally[2])
    grads = [block(source, 0, 0)]
    for n, (s, m) in zip((3, 3, 4), ROUTES[1:4]):
        b, outs[n] = after(block(source, s, m), outs[n])
        grads.append(ring_permute(b, s, m))
    source, tally[3] = after(expert_grad, tally[3])
    rest = [block(source, s, m) for s, m in ROUTES[4:]]

    small = lambda *shape: pl.BlockSpec(shape, lambda p, c: (0,) * len(shape))
    logit, partial = pl.pallas_call(
        mid_kernel,
        grid=(2, STEPS),
        out_shape=(
            jax.ShapeDtypeStruct((TOK, EXPERTS), F32),
            jax.ShapeDtypeStruct((EXPERTS, 8, 1024), F32),
        ),
        in_specs=[
            small(1, 8 * ROWS),
            small(TOK, 8),
            small(TOK, 1),
            small(TOK, 2),
            small(TOK, EXPERTS),
            small(8, EXPERTS),
            second(1),
            second(TOK),
            first(TOK),
        ]
        + [first(ROWS)] * 8
        + [pl.BlockSpec((ROWS, 128), lambda p, c: (0, D // 128))] * 3,
        out_specs=(
            small(TOK, EXPERTS),
            small(EXPERTS, 8, 1024),
        ),
        scratch_shapes=[
            pltpu.VMEM((TOK, 8 * ROWS), F32),
            pltpu.VMEM((TOK, 3 * EXPERTS), BF16),
            pltpu.VMEM((8, EXPERTS), F32),
        ],
        cost_estimate=pl.CostEstimate(flops=20_000_000_000, bytes_accessed=60_000_000, transcendentals=0),
        compiler_params=params(20),
    )(slots, pack, inv, expert_ids, probs, tally[5], gain, hidden, grad_out, own_out, *outs, *outs[3:6])
    partial = jnp.sum(lax.all_to_all(partial, "seq", 0, 0, tiled=True), axis=0)
    partial = partial + lax.ppermute(partial, AXES, xor_perm("c", 1))
    near = [lax.ppermute(partial, AXES, xor_perm("x", d)) for d in (1, 2)]
    partial, *grads[1:4] = after(partial, *grads[1:4])
    partial = (partial + near[0]) + (near[1] + lax.ppermute(partial, AXES, xor_perm("x", 3)))
    partial, *rest = after(partial, *rest)
    grads += [ring_permute(b, s, m) for b, (s, m) in zip(rest, ROUTES[4:])]
    once = lambda rows: pl.BlockSpec((rows, WIDE), lambda c: (0, c))
    fixed = lambda *shape: pl.BlockSpec(shape, lambda c: (0,) * len(shape))
    half = 4 * ROWS
    begin, partial = after(pack, partial)
    part, sums = pl.pallas_call(
        half_kernel,
        grid=(STEPS,),
        out_shape=(
            jax.ShapeDtypeStruct((TOK, D), F32),
            jax.ShapeDtypeStruct((TOK, 128), F32),
        ),
        in_specs=[
            fixed(1, half),
            fixed(TOK, 8),
            fixed(TOK, 1),
            fixed(TOK, EXPERTS),
            once(EXPERTS),
            once(1),
            once(TOK),
            once(TOK),
        ]
        + [once(ROWS)] * 4,
        out_specs=(once(TOK), fixed(TOK, 128)),
        scratch_shapes=[pltpu.VMEM((TOK, 2 * half + 6 * EXPERTS), BF16)],
        compiler_params=params(60),
        cost_estimate=pl.CostEstimate(
            flops=10_000_000_000, bytes_accessed=30_000_000, transcendentals=0
        ),
    )(slots[:, :half], begin, inv, logit, router_weight, gain, hidden, grad_out, *grads[:4])
    partial, sums = after(partial, sums)
    along_z = [[4 * y + z for z in range(4)] for y in range(4)]
    along_y = [[4 * y + z for y in range(4)] for z in range(4)]
    partial = lax.all_gather(partial, "seq", axis_index_groups=along_z)
    router_grad = lax.all_gather(partial, "seq", axis_index_groups=along_y).reshape(EXPERTS, D)

    grad_hidden = pl.pallas_call(
        last_kernel,
        grid=(2, STEPS),
        out_shape=jax.ShapeDtypeStruct((TOK, D), BF16),
        in_specs=[
            small(1, half),
            small(TOK, 8),
            small(TOK, 1),
            small(TOK, 128),
            first(1),
            first(TOK),
            twice(TOK),
        ]
        + [first(ROWS)] * 4,
        out_specs=second(TOK),
        scratch_shapes=[
            pltpu.VMEM((TOK, D), F32),
            pltpu.VMEM((TOK, 2 * half), BF16),
            pltpu.VMEM((TOK, 128), F32),
            pltpu.VMEM((TOK, 128), F32),
        ],
        compiler_params=params(60),
    )(slots[:, half:], pack, inv, sums, gain, part, hidden, *grads[4:])
    return grad_hidden, router_grad


def solution(mesh):
    rows = P(("seq", "exp"), None)
    in_specs = (
        rows,
        rows,
        P(),
        rows,
        P(),
        rows,
        P("seq", "exp", None, None),
        P("seq", "exp", None, None),
    )
    return jax.shard_map(body, mesh=mesh, in_specs=in_specs, out_specs=(rows, P()), check_vma=False)
```

```python
import jax
import jax.numpy as jnp
from jax import lax
from jax.experimental import pallas as pl
from jax.experimental.pallas import tpu as pltpu
from jax.sharding import PartitionSpec as P

D = 8192
EXPERTS = 16
TOK = 128
CAP = 24
ROWS = 2 * CAP
TOKENS = 16384
AXES = ("seq", "exp")
CHUNK = 1024
F32 = jnp.float32
BF16 = jnp.bfloat16
VMEM = pl.BlockSpec(memory_space=pltpu.VMEM)

ROUTES = ((0, 0), (1, 0), (3, 0), (2, 0), (1, 1), (3, 1), (2, 1), (0, 1))


def coords():
    s, e = lax.axis_index("seq"), lax.axis_index("exp")
    return {"y": s >> 2, "z": s & 3, "x": e >> 1, "c": e & 1}


STRIDE = {"y": 32, "z": 8, "x": 2, "c": 1}
SIZE = {"y": 4, "z": 4, "x": 4, "c": 2}


def shift_perm(axis, d):
    out = []
    for i in range(128):
        a = (i // STRIDE[axis]) % SIZE[axis]
        out.append((i, i + ((a + d) % SIZE[axis] - a) * STRIDE[axis]))
    return out


def xor_perm(axis, d):
    return [(i, i ^ (d * STRIDE[axis])) for i in range(128)]


def after(*xs):
    return lax.optimization_barrier(xs)


def ring_permute(v, s, m):
    perm = [(i, (((i >> 1) + s) % 4) * 2 + ((i & 1) ^ m)) for i in range(8)]
    return lax.ppermute(v, "exp", perm)


def slot_numbers(sources):
    base = jnp.stack(sources).astype(F32) * ROWS
    return (base[:, None] + jnp.arange(ROWS, dtype=F32)[None, :]).reshape(1, 8 * ROWS)


def split3(v):
    a = v.astype(BF16)
    r = v - a.astype(F32)
    b = r.astype(BF16)
    c = (r - b.astype(F32)).astype(BF16)
    return a, b, c


def pre_kernel(ids_ref, logits_ref, pack_ref, probs_ref, counts_ref):
    ids = ids_ref[...]
    logits = logits_ref[...]
    labels = lax.broadcasted_iota(jnp.int32, (TOK, EXPERTS), 1)
    oh = [(ids[:, k : k + 1] == labels).astype(F32) for k in range(2)]
    both = oh[0] + oh[1]
    row = lax.broadcasted_iota(jnp.int32, (TOK, TOK), 0)
    col = lax.broadcasted_iota(jnp.int32, (TOK, TOK), 1)
    before = (row > col).astype(F32).astype(BF16)
    ranks = jnp.dot(before, both.astype(BF16), preferred_element_type=F32)
    counts_ref[...] = jnp.broadcast_to(jnp.sum(both, axis=0, keepdims=True), (8, EXPERTS))
    index = [
        jnp.sum(oh[k] * (ranks + (CAP * labels).astype(F32)), axis=1, keepdims=True)
        for k in range(2)
    ]
    chosen = [jnp.sum(oh[k] * logits, axis=1, keepdims=True) for k in range(2)]
    top = jnp.maximum(chosen[0], chosen[1])
    w = [jnp.exp(c - top) for c in chosen]
    total = w[0] + w[1]
    e = jnp.exp(logits - jnp.max(logits, axis=1, keepdims=True))
    probs_ref[...] = e / jnp.sum(e, axis=1, keepdims=True)
    lane = lax.broadcasted_iota(jnp.int32, (TOK, 8), 1)
    pack = jnp.zeros((TOK, 8), F32)
    for i, v in enumerate((w[0] / total, w[1] / total, index[0], index[1])):
        pack = jnp.where(lane == i, v, pack)
    pack_ref[...] = pack


def mid_kernel(
    slots_ref,
    pack_ref,
    inv_ref,
    ids_ref,
    probs_ref,
    counts_ref,
    gain_ref,
    hidden_ref,
    grad_ref,
    *refs,
):
    blocks, shares = refs[:8], refs[8:11]
    logit_ref, partial_ref, dots_ref, left_ref, total_ref = refs[11:]
    stage, c = pl.program_id(0), pl.program_id(1)

    @pl.when(stage == 0)
    def _():
        picked = jnp.concatenate([b[...] for b in blocks], axis=0)
        d = lax.dot_general(
            grad_ref[...], picked, (((1,), (1,)), ((), ())), preferred_element_type=F32
        )

        @pl.when(c == 0)
        def _():
            dots_ref[...] = d
            total = counts_ref[...]
            for b in shares:
                other = b[...].astype(F32)[0:8]
                total = total + other[:, :EXPERTS] + other[:, EXPERTS : 2 * EXPERTS]
            total_ref[...] = total

        @pl.when(c > 0)
        def _():
            dots_ref[...] += d

    @pl.when((stage == 1) & (c == 0))
    def _():
        pack = pack_ref[...]
        gate = [pack[:, 0:1], pack[:, 1:2]]
        slots = slots_ref[...]
        dots = dots_ref[...]
        gate_dot = [
            jnp.sum(jnp.where(slots == pack[:, 2 + k : 3 + k], dots, 0.0), axis=1, keepdims=True)
            .astype(BF16)
            .astype(F32)
            for k in range(2)
        ]
        mean = gate[0] * gate_dot[0] + gate[1] * gate_dot[1]
        ids = ids_ref[...]
        labels = lax.broadcasted_iota(jnp.int32, (TOK, EXPERTS), 1)
        direct = jnp.zeros((TOK, EXPERTS), F32)
        for k in range(2):
            chosen = gate[k] * (gate_dot[k] - mean)
            direct = direct + jnp.where(ids[:, k : k + 1] == labels, chosen, 0.0)
        probs = probs_ref[...]
        load = total_ref[0:1, :] * (EXPERTS / (2 * TOKENS))
        aux = probs * (load - jnp.sum(probs * load, axis=1, keepdims=True))
        logit = direct + aux
        logit = logit * inv_ref[...]
        logit_ref[...] = logit
        left_ref[...] = jnp.concatenate(split3(logit), axis=1)

    @pl.when(stage == 1)
    def _():
        p = lax.dot_general(
            left_ref[...], hidden_ref[...], (((0,), (0,)), ((), ())), preferred_element_type=F32
        )
        p = (p[0:16] + p[16:32] + p[32:48]) * (gain_ref[...] * (1.0 / 128.0))
        for j in range(WIDE // 1024):
            partial_ref[:, c * (WIDE // 1024) + j, :] = p[:, j * 1024 : (j + 1) * 1024]


def weights(slots, pack, inv):
    w = jnp.where(slots == pack[:, 2:3], pack[:, 0:1], 0.0)
    w = w + jnp.where(slots == pack[:, 3:4], pack[:, 1:2], 0.0)
    return split3(w * inv)[:2]


def row_sums(scaled, hidden):
    prod = scaled * hidden.astype(F32)
    total = prod[:, 0:128]
    for j in range(1, WIDE // 128):
        total = total + prod[:, j * 128 : (j + 1) * 128]
    return total


def half_kernel(
    slots_ref, pack_ref, inv_ref, logit_ref, weight_ref, gain_ref, hidden_ref, grad_ref, *refs
):
    blocks, (part_ref, sums_ref, left_ref) = refs[:-3], refs[-3:]
    c = pl.program_id(0)

    @pl.when(c == 0)
    def _():
        w_hi, w_lo = weights(slots_ref[...], pack_ref[...], inv_ref[...])
        l0, l1, l2 = split3(logit_ref[...])
        left_ref[...] = jnp.concatenate([w_hi, w_lo, l0, l0, l0, l1, l1, l2], axis=1)
        sums_ref[...] = jnp.zeros_like(sums_ref)

    r0, r1, r2 = split3(weight_ref[...])
    rows = [b[...] for b in blocks]
    right = jnp.concatenate(rows + rows + [r0, r1, r2, r0, r1, r0], axis=0)
    scaled = jnp.dot(left_ref[...], right, preferred_element_type=F32) * gain_ref[...]
    part_ref[...] = grad_ref[...].astype(F32) + scaled
    sums_ref[...] += row_sums(scaled, hidden_ref[...])


def last_kernel(
    slots_ref, pack_ref, inv_ref, sums_ref, gain_ref, part_ref, hidden_ref, *refs
):
    blocks, (out_ref, part_scr, left_ref, acc_ref, factor_ref) = refs[:-5], refs[-5:]
    stage, c = pl.program_id(0), pl.program_id(1)
    cols = pl.ds(pl.multiple_of(c * WIDE, WIDE), WIDE)

    @pl.when((stage == 0) & (c == 0))
    def _():
        left_ref[...] = jnp.concatenate(
            weights(slots_ref[...], pack_ref[...], inv_ref[...]), axis=1
        )
        acc_ref[...] = sums_ref[...]

    @pl.when(stage == 0)
    def _():
        rows = [b[...] for b in blocks]
        right = jnp.concatenate(rows + rows, axis=0)
        scaled = jnp.dot(left_ref[...], right, preferred_element_type=F32) * gain_ref[...]
        part_scr[:, cols] = part_ref[...] + scaled
        acc_ref[...] += row_sums(scaled, hidden_ref[...])

    @pl.when((stage == 1) & (c == 0))
    def _():
        inv = inv_ref[...]
        mean = jnp.sum(acc_ref[...], axis=1, keepdims=True) / D
        factor_ref[...] = jnp.broadcast_to(inv * inv * mean, (TOK, 128))

    @pl.when(stage == 1)
    def _():
        normed = hidden_ref[...].astype(F32) * factor_ref[:, 0:1]
        out_ref[...] = (part_scr[:, cols] - normed).astype(BF16)


STEPS = 4
WIDE = D // STEPS


def first(rows):
    return pl.BlockSpec((rows, WIDE), lambda p, c: (0, jnp.where(p == 0, c, STEPS - 1)))


def twice(rows):
    return pl.BlockSpec((rows, WIDE), lambda p, c: (0, c))


def second(rows):
    return pl.BlockSpec((rows, WIDE), lambda p, c: (0, jnp.where(p == 0, 0, c)))


def params(mib):
    return pltpu.CompilerParams(vmem_limit_bytes=mib * 1024 * 1024)


def body(
    grad_out, hidden, norm_gain, router_logits, router_weight, expert_ids, expert_grad, expert_out
):
    at = coords()
    gain = norm_gain.reshape(1, D)
    sources = [((at["x"] - s) & 3) * 2 + (at["c"] ^ m) for s, m in ROUTES]
    slots = slot_numbers(sources)

    def block(array, s, m):
        to = ((at["x"] + s) & 3) * 2 + (at["c"] ^ m)
        return lax.dynamic_slice(array, (0, 0, to * CAP, 0), (1, 2, CAP, D)).reshape(ROWS, D)

    ready = [block(expert_out, s, m) for s, m in ROUTES[1:4]]
    ids, *ready = after(expert_ids, *ready)
    outs = [ring_permute(b, s, m) for b, (s, m) in zip(ready, ROUTES[1:4])]

    pack, probs, counts = pl.pallas_call(
        pre_kernel,
        out_shape=(
            jax.ShapeDtypeStruct((TOK, 8), F32),
            jax.ShapeDtypeStruct((TOK, EXPERTS), F32),
            jax.ShapeDtypeStruct((8, EXPERTS), F32),
        ),
        in_specs=[VMEM] * 2,
        out_specs=(VMEM,) * 3,
        compiler_params=params(8),
    )(ids, router_logits)
    wide = hidden.astype(F32)
    inv = lax.rsqrt(jnp.mean(wide * wide, axis=1, keepdims=True) + 1e-05)
    tally = [counts]
    for axis, d in (("y", 1), ("y", 2), ("z", 1), ("z", 2), ("c", 1)):
        tally.append(tally[-1] + lax.ppermute(tally[-1], AXES, xor_perm(axis, d)))
    share = tally[5][0:1].astype(BF16)
    share = jnp.concatenate([share, (tally[5][0:1] - share.astype(F32)).astype(BF16)], axis=1)
    share = jnp.broadcast_to(jnp.pad(share, ((0, 0), (0, 128 - 2 * EXPERTS))), (ROWS, 128))

    source, tally[1] = after(expert_out, tally[1])
    ready = [block(source, s, m) for s, m in ROUTES[4:]]
    ready = [jnp.concatenate([b, share], axis=1) for b in ready[:3]] + ready[3:]
    for n, (b, (s, m)) in enumerate(zip(ready, ROUTES[4:])):
        if n != 1:
            b, outs[n % 3] = after(b, outs[n % 3])
        outs.append(ring_permute(b, s, m))
    own_out = block(expert_out, 0, 0)

    source, tally[2] = after(expert_grad, tally[2])
    grads = [block(source, 0, 0)]
    for n, (s, m) in zip((3, 3, 4), ROUTES[1:4]):
        b, outs[n] = after(block(source, s, m), outs[n])
        grads.append(ring_permute(b, s, m))
    source, tally[3] = after(expert_grad, tally[3])
    rest = [block(source, s, m) for s, m in ROUTES[4:]]

    small = lambda *shape: pl.BlockSpec(shape, lambda p, c: (0,) * len(shape))
    logit, partial = pl.pallas_call(
        mid_kernel,
        grid=(2, STEPS),
        out_shape=(
            jax.ShapeDtypeStruct((TOK, EXPERTS), F32),
            jax.ShapeDtypeStruct((EXPERTS, 8, 1024), F32),
        ),
        in_specs=[
            small(1, 8 * ROWS),
            small(TOK, 8),
            small(TOK, 1),
            small(TOK, 2),
            small(TOK, EXPERTS),
            small(8, EXPERTS),
            second(1),
            second(TOK),
            first(TOK),
        ]
        + [first(ROWS)] * 8
        + [pl.BlockSpec((ROWS, 128), lambda p, c: (0, D // 128))] * 3,
        out_specs=(
            small(TOK, EXPERTS),
            small(EXPERTS, 8, 1024),
        ),
        scratch_shapes=[
            pltpu.VMEM((TOK, 8 * ROWS), F32),
            pltpu.VMEM((TOK, 3 * EXPERTS), BF16),
            pltpu.VMEM((8, EXPERTS), F32),
        ],
        cost_estimate=pl.CostEstimate(flops=20_000_000_000, bytes_accessed=60_000_000, transcendentals=0),
        compiler_params=params(20),
    )(slots, pack, inv, expert_ids, probs, tally[5], gain, hidden, grad_out, own_out, *outs, *outs[3:6])
    partial = jnp.sum(lax.all_to_all(partial, "seq", 0, 0, tiled=True), axis=0)
    partial = partial + lax.ppermute(partial, AXES, xor_perm("c", 1))
    near = [lax.ppermute(partial, AXES, xor_perm("x", d)) for d in (1, 2)]
    partial, *grads[1:4] = after(partial, *grads[1:4])
    partial = (partial + near[0]) + (near[1] + lax.ppermute(partial, AXES, xor_perm("x", 3)))
    partial, *rest = after(partial, *rest)
    grads += [ring_permute(b, s, m) for b, (s, m) in zip(rest, ROUTES[4:])]
    once = lambda rows: pl.BlockSpec((rows, WIDE), lambda c: (0, c))
    fixed = lambda *shape: pl.BlockSpec(shape, lambda c: (0,) * len(shape))
    half = 4 * ROWS
    router_grad = lax.all_gather(partial, "seq").reshape(EXPERTS, D)
    begin, router_grad = after(pack, router_grad)
    part, sums = pl.pallas_call(
        half_kernel,
        grid=(STEPS,),
        out_shape=(
            jax.ShapeDtypeStruct((TOK, D), F32),
            jax.ShapeDtypeStruct((TOK, 128), F32),
        ),
        in_specs=[
            fixed(1, half),
            fixed(TOK, 8),
            fixed(TOK, 1),
            fixed(TOK, EXPERTS),
            once(EXPERTS),
            once(1),
            once(TOK),
            once(TOK),
        ]
        + [once(ROWS)] * 4,
        out_specs=(once(TOK), fixed(TOK, 128)),
        scratch_shapes=[pltpu.VMEM((TOK, 2 * half + 6 * EXPERTS), BF16)],
        compiler_params=params(24),
        cost_estimate=pl.CostEstimate(flops=1_000, bytes_accessed=1_000, transcendentals=0),
    )(slots[:, :half], begin, inv, logit, router_weight, gain, hidden, grad_out, *grads[:4])

    grad_hidden = pl.pallas_call(
        last_kernel,
        grid=(2, STEPS),
        out_shape=jax.ShapeDtypeStruct((TOK, D), BF16),
        in_specs=[
            small(1, half),
            small(TOK, 8),
            small(TOK, 1),
            small(TOK, 128),
            first(1),
            first(TOK),
            twice(TOK),
        ]
        + [first(ROWS)] * 4,
        out_specs=second(TOK),
        scratch_shapes=[
            pltpu.VMEM((TOK, D), F32),
            pltpu.VMEM((TOK, 2 * half), BF16),
            pltpu.VMEM((TOK, 128), F32),
            pltpu.VMEM((TOK, 128), F32),
        ],
        compiler_params=params(24),
    )(slots[:, half:], pack, inv, sums, gain, part, hidden, *grads[4:])
    return grad_hidden, router_grad


def solution(mesh):
    rows = P(("seq", "exp"), None)
    in_specs = (
        rows,
        rows,
        P(),
        rows,
        P(),
        rows,
        P("seq", "exp", None, None),
        P("seq", "exp", None, None),
    )
    return jax.shard_map(body, mesh=mesh, in_specs=in_specs, out_specs=(rows, P()), check_vma=False)
```

```python
import jax
import jax.numpy as jnp
from jax import lax
from jax.experimental import pallas as pl
from jax.experimental.pallas import tpu as pltpu
from jax.sharding import PartitionSpec as P

D = 8192
EXPERTS = 16
TOK = 128
CAP = 24
ROWS = 2 * CAP
TOKENS = 16384
AXES = ("seq", "exp")
CHUNK = 1024
F32 = jnp.float32
BF16 = jnp.bfloat16
VMEM = pl.BlockSpec(memory_space=pltpu.VMEM)

ROUTES = ((0, 0), (1, 0), (3, 0), (2, 0), (1, 1), (3, 1), (2, 1), (0, 1))


def coords():
    s, e = lax.axis_index("seq"), lax.axis_index("exp")
    return {"y": s >> 2, "z": s & 3, "x": e >> 1, "c": e & 1}


STRIDE = {"y": 32, "z": 8, "x": 2, "c": 1}
SIZE = {"y": 4, "z": 4, "x": 4, "c": 2}


def shift_perm(axis, d):
    out = []
    for i in range(128):
        a = (i // STRIDE[axis]) % SIZE[axis]
        out.append((i, i + ((a + d) % SIZE[axis] - a) * STRIDE[axis]))
    return out


def xor_perm(axis, d):
    return [(i, i ^ (d * STRIDE[axis])) for i in range(128)]


def after(*xs):
    return lax.optimization_barrier(xs)


def ring_permute(v, s, m):
    perm = [(i, (((i >> 1) + s) % 4) * 2 + ((i & 1) ^ m)) for i in range(8)]
    return lax.ppermute(v, "exp", perm)


def slot_numbers(sources):
    base = jnp.stack(sources).astype(F32) * ROWS
    return (base[:, None] + jnp.arange(ROWS, dtype=F32)[None, :]).reshape(1, len(sources) * ROWS)


def split3(v):
    a = v.astype(BF16)
    r = v - a.astype(F32)
    b = r.astype(BF16)
    c = (r - b.astype(F32)).astype(BF16)
    return a, b, c


def pre_kernel(ids_ref, logits_ref, pack_ref, probs_ref, counts_ref):
    ids = ids_ref[...]
    logits = logits_ref[...]
    labels = lax.broadcasted_iota(jnp.int32, (TOK, EXPERTS), 1)
    oh = [(ids[:, k : k + 1] == labels).astype(F32) for k in range(2)]
    both = oh[0] + oh[1]
    row = lax.broadcasted_iota(jnp.int32, (TOK, TOK), 0)
    col = lax.broadcasted_iota(jnp.int32, (TOK, TOK), 1)
    before = (row > col).astype(F32).astype(BF16)
    ranks = jnp.dot(before, both.astype(BF16), preferred_element_type=F32)
    counts_ref[...] = jnp.broadcast_to(jnp.sum(both, axis=0, keepdims=True), (8, EXPERTS))
    index = [
        jnp.sum(oh[k] * (ranks + (CAP * labels).astype(F32)), axis=1, keepdims=True)
        for k in range(2)
    ]
    chosen = [jnp.sum(oh[k] * logits, axis=1, keepdims=True) for k in range(2)]
    top = jnp.maximum(chosen[0], chosen[1])
    w = [jnp.exp(c - top) for c in chosen]
    total = w[0] + w[1]
    e = jnp.exp(logits - jnp.max(logits, axis=1, keepdims=True))
    probs_ref[...] = e / jnp.sum(e, axis=1, keepdims=True)
    lane = lax.broadcasted_iota(jnp.int32, (TOK, 8), 1)
    pack = jnp.zeros((TOK, 8), F32)
    for i, v in enumerate((w[0] / total, w[1] / total, index[0], index[1])):
        pack = jnp.where(lane == i, v, pack)
    pack_ref[...] = pack


def mid_kernel(
    slots_ref,
    pack_ref,
    inv_ref,
    ids_ref,
    probs_ref,
    counts_ref,
    gain_ref,
    hidden_ref,
    grad_ref,
    *refs,
):
    blocks, shares = refs[:8], refs[8:11]
    logit_ref, partial_ref, dots_ref, left_ref, total_ref = refs[11:]
    stage, c = pl.program_id(0), pl.program_id(1)

    @pl.when(stage == 0)
    def _():
        picked = jnp.concatenate([b[...] for b in blocks], axis=0)
        d = lax.dot_general(
            grad_ref[...], picked, (((1,), (1,)), ((), ())), preferred_element_type=F32
        )

        @pl.when(c == 0)
        def _():
            dots_ref[...] = d
            total = counts_ref[...]
            for b in shares:
                other = b[...].astype(F32)[0:8]
                total = total + other[:, :EXPERTS] + other[:, EXPERTS : 2 * EXPERTS]
            total_ref[...] = total

        @pl.when(c > 0)
        def _():
            dots_ref[...] += d

    @pl.when((stage == 1) & (c == 0))
    def _():
        pack = pack_ref[...]
        gate = [pack[:, 0:1], pack[:, 1:2]]
        slots = slots_ref[...]
        dots = dots_ref[...]
        gate_dot = [
            jnp.sum(jnp.where(slots == pack[:, 2 + k : 3 + k], dots, 0.0), axis=1, keepdims=True)
            .astype(BF16)
            .astype(F32)
            for k in range(2)
        ]
        mean = gate[0] * gate_dot[0] + gate[1] * gate_dot[1]
        ids = ids_ref[...]
        labels = lax.broadcasted_iota(jnp.int32, (TOK, EXPERTS), 1)
        direct = jnp.zeros((TOK, EXPERTS), F32)
        for k in range(2):
            chosen = gate[k] * (gate_dot[k] - mean)
            direct = direct + jnp.where(ids[:, k : k + 1] == labels, chosen, 0.0)
        probs = probs_ref[...]
        load = total_ref[0:1, :] * (EXPERTS / (2 * TOKENS))
        aux = probs * (load - jnp.sum(probs * load, axis=1, keepdims=True))
        logit = direct + aux
        logit = logit * inv_ref[...]
        logit_ref[...] = logit
        left_ref[...] = jnp.concatenate(split3(logit), axis=1)

    @pl.when(stage == 1)
    def _():
        p = lax.dot_general(
            left_ref[...], hidden_ref[...], (((0,), (0,)), ((), ())), preferred_element_type=F32
        )
        p = (p[0:16] + p[16:32] + p[32:48]) * (gain_ref[...] * (1.0 / 128.0))
        for j in range(WIDE // 1024):
            partial_ref[:, c * (WIDE // 1024) + j, :] = p[:, j * 1024 : (j + 1) * 1024]


def weights(slots, pack, inv):
    w = jnp.where(slots == pack[:, 2:3], pack[:, 0:1], 0.0)
    w = w + jnp.where(slots == pack[:, 3:4], pack[:, 1:2], 0.0)
    return split3(w * inv)[:2]


def row_sums(scaled, hidden):
    prod = scaled * hidden.astype(F32)
    total = prod[:, 0:128]
    for j in range(1, WIDE // 128):
        total = total + prod[:, j * 128 : (j + 1) * 128]
    return total


def half_kernel(
    slots_ref, pack_ref, inv_ref, logit_ref, weight_ref, gain_ref, hidden_ref, grad_ref, *refs
):
    blocks, (part_ref, sums_ref, left_ref) = refs[:-3], refs[-3:]
    c = pl.program_id(0)

    @pl.when(c == 0)
    def _():
        w_hi, w_lo = weights(slots_ref[...], pack_ref[...], inv_ref[...])
        l0, l1, l2 = split3(logit_ref[...])
        left_ref[...] = jnp.concatenate([w_hi, w_lo, l0, l0, l0, l1, l1, l2], axis=1)
        sums_ref[...] = jnp.zeros_like(sums_ref)

    r0, r1, r2 = split3(weight_ref[...])
    rows = [b[...] for b in blocks]
    right = jnp.concatenate(rows + rows + [r0, r1, r2, r0, r1, r0], axis=0)
    scaled = jnp.dot(left_ref[...], right, preferred_element_type=F32) * gain_ref[...]
    part_ref[...] = grad_ref[...].astype(F32) + scaled
    sums_ref[...] += row_sums(scaled, hidden_ref[...])


def last_kernel(
    slots_ref, pack_ref, inv_ref, sums_ref, gain_ref, part_ref, hidden_ref, *refs
):
    blocks, (out_ref, part_scr, hidden_scr, left_ref, acc_ref, factor_ref) = refs[:-6], refs[-6:]
    stage, c = pl.program_id(0), pl.program_id(1)
    cols = pl.ds(pl.multiple_of(c * WIDE, WIDE), WIDE)

    @pl.when((stage == 0) & (c == 0))
    def _():
        left_ref[...] = jnp.concatenate(
            weights(slots_ref[...], pack_ref[...], inv_ref[...]), axis=1
        )
        acc_ref[...] = sums_ref[...]

    @pl.when(stage == 0)
    def _():
        rows = [b[...] for b in blocks]
        right = jnp.concatenate(rows + rows, axis=0)
        scaled = jnp.dot(left_ref[...], right, preferred_element_type=F32) * gain_ref[...]
        part_scr[:, cols] = part_ref[...] + scaled
        hidden = hidden_ref[...]
        hidden_scr[:, cols] = hidden
        acc_ref[...] += row_sums(scaled, hidden)

    @pl.when((stage == 1) & (c == 0))
    def _():
        inv = inv_ref[...]
        mean = jnp.sum(acc_ref[...], axis=1, keepdims=True) / D
        factor_ref[...] = jnp.broadcast_to(inv * inv * mean, (TOK, 128))

    @pl.when(stage == 1)
    def _():
        normed = hidden_scr[:, cols].astype(F32) * factor_ref[:, 0:1]
        out_ref[...] = (part_scr[:, cols] - normed).astype(BF16)


STEPS = 4
WIDE = D // STEPS


def first(rows):
    return pl.BlockSpec((rows, WIDE), lambda p, c: (0, jnp.where(p == 0, c, STEPS - 1)))


def second(rows):
    return pl.BlockSpec((rows, WIDE), lambda p, c: (0, jnp.where(p == 0, 0, c)))


def params(mib):
    return pltpu.CompilerParams(vmem_limit_bytes=mib * 1024 * 1024)


def body(
    grad_out, hidden, norm_gain, router_logits, router_weight, expert_ids, expert_grad, expert_out
):
    at = coords()
    gain = norm_gain.reshape(1, D)
    sources = [((at["x"] - s) & 3) * 2 + (at["c"] ^ m) for s, m in ROUTES]
    slots = slot_numbers(sources)
    late_slots = slot_numbers([sources[i] for i in (6, 4, 5, 7)])

    def block(array, s, m):
        to = ((at["x"] + s) & 3) * 2 + (at["c"] ^ m)
        return lax.dynamic_slice(array, (0, 0, to * CAP, 0), (1, 2, CAP, D)).reshape(ROWS, D)

    ready = [block(expert_out, s, m) for s, m in ROUTES[1:4]]
    ids, *ready = after(expert_ids, *ready)
    outs = [ring_permute(b, s, m) for b, (s, m) in zip(ready, ROUTES[1:4])]

    pack, probs, counts = pl.pallas_call(
        pre_kernel,
        out_shape=(
            jax.ShapeDtypeStruct((TOK, 8), F32),
            jax.ShapeDtypeStruct((TOK, EXPERTS), F32),
            jax.ShapeDtypeStruct((8, EXPERTS), F32),
        ),
        in_specs=[VMEM] * 2,
        out_specs=(VMEM,) * 3,
        compiler_params=params(8),
    )(ids, router_logits)
    wide = hidden.astype(F32)
    inv = lax.rsqrt(jnp.mean(wide * wide, axis=1, keepdims=True) + 1e-05)
    tally = [counts]
    for axis, d in (("y", 1), ("y", 2), ("z", 1), ("z", 2), ("c", 1)):
        tally.append(tally[-1] + lax.ppermute(tally[-1], AXES, xor_perm(axis, d)))
    share = tally[5][0:1].astype(BF16)
    share = jnp.concatenate([share, (tally[5][0:1] - share.astype(F32)).astype(BF16)], axis=1)
    share = jnp.broadcast_to(jnp.pad(share, ((0, 0), (0, 128 - 2 * EXPERTS))), (ROWS, 128))

    source, tally[1] = after(expert_out, tally[1])
    ready = [block(source, s, m) for s, m in ROUTES[4:]]
    ready = [jnp.concatenate([b, share], axis=1) for b in ready[:3]] + ready[3:]
    for n, (b, (s, m)) in enumerate(zip(ready, ROUTES[4:])):
        if n != 1:
            b, outs[n % 3] = after(b, outs[n % 3])
        outs.append(ring_permute(b, s, m))
    own_out = block(expert_out, 0, 0)

    source, tally[2] = after(expert_grad, tally[2])
    grads = [block(source, 0, 0)]
    for n, (s, m) in zip((3, 3, 4), ROUTES[1:4]):
        b, outs[n] = after(block(source, s, m), outs[n])
        grads.append(ring_permute(b, s, m))
    source, tally[3] = after(expert_grad, tally[3])
    late = [ROUTES[i] for i in (6, 4, 5, 7)]
    rest = [block(source, s, m) for s, m in late]

    small = lambda *shape: pl.BlockSpec(shape, lambda p, c: (0,) * len(shape))
    logit, partial = pl.pallas_call(
        mid_kernel,
        grid=(2, STEPS),
        out_shape=(
            jax.ShapeDtypeStruct((TOK, EXPERTS), F32),
            jax.ShapeDtypeStruct((EXPERTS, 8, 1024), F32),
        ),
        in_specs=[
            small(1, 8 * ROWS),
            small(TOK, 8),
            small(TOK, 1),
            small(TOK, 2),
            small(TOK, EXPERTS),
            small(8, EXPERTS),
            second(1),
            second(TOK),
            first(TOK),
        ]
        + [first(ROWS)] * 8
        + [pl.BlockSpec((ROWS, 128), lambda p, c: (0, D // 128))] * 3,
        out_specs=(
            small(TOK, EXPERTS),
            small(EXPERTS, 8, 1024),
        ),
        scratch_shapes=[
            pltpu.VMEM((TOK, 8 * ROWS), F32),
            pltpu.VMEM((TOK, 3 * EXPERTS), BF16),
            pltpu.VMEM((8, EXPERTS), F32),
        ],
        cost_estimate=pl.CostEstimate(flops=20_000_000_000, bytes_accessed=60_000_000, transcendentals=0),
        compiler_params=params(20),
    )(slots, pack, inv, expert_ids, probs, tally[5], gain, hidden, grad_out, own_out, *outs, *outs[3:6])
    partial = jnp.sum(lax.all_to_all(partial, "seq", 0, 0, tiled=True), axis=0)
    partial = partial + lax.ppermute(partial, AXES, xor_perm("c", 1))
    near = [lax.ppermute(partial, AXES, xor_perm("x", d)) for d in (1, 2)]
    partial, *grads[1:4] = after(partial, *grads[1:4])
    partial = (partial + near[0]) + (near[1] + lax.ppermute(partial, AXES, xor_perm("x", 3)))
    partial, *rest = after(partial, *rest)
    grads += [ring_permute(b, s, m) for b, (s, m) in zip(rest, late)]
    once = lambda rows: pl.BlockSpec((rows, WIDE), lambda c: (0, c))
    fixed = lambda *shape: pl.BlockSpec(shape, lambda c: (0,) * len(shape))
    half = 4 * ROWS
    begin, partial = after(pack, partial)
    part, sums = pl.pallas_call(
        half_kernel,
        grid=(STEPS,),
        out_shape=(
            jax.ShapeDtypeStruct((TOK, D), F32),
            jax.ShapeDtypeStruct((TOK, 128), F32),
        ),
        in_specs=[
            fixed(1, half),
            fixed(TOK, 8),
            fixed(TOK, 1),
            fixed(TOK, EXPERTS),
            once(EXPERTS),
            once(1),
            once(TOK),
            once(TOK),
        ]
        + [once(ROWS)] * 4,
        out_specs=(once(TOK), fixed(TOK, 128)),
        scratch_shapes=[pltpu.VMEM((TOK, 2 * half + 6 * EXPERTS), BF16)],
        compiler_params=params(60),
        cost_estimate=pl.CostEstimate(
            flops=10_000_000_000, bytes_accessed=30_000_000, transcendentals=0
        ),
    )(slots[:, :half], begin, inv, logit, router_weight, gain, hidden, grad_out, *grads[:4])
    partial, sums = after(partial, sums)
    router_grad = lax.all_gather(partial, "seq").reshape(EXPERTS, D)

    grad_hidden = pl.pallas_call(
        last_kernel,
        grid=(2, STEPS),
        out_shape=jax.ShapeDtypeStruct((TOK, D), BF16),
        in_specs=[
            small(1, half),
            small(TOK, 8),
            small(TOK, 1),
            small(TOK, 128),
            first(1),
            first(TOK),
            first(TOK),
        ]
        + [first(ROWS)] * 4,
        out_specs=second(TOK),
        scratch_shapes=[
            pltpu.VMEM((TOK, D), F32),
            pltpu.VMEM((TOK, D), BF16),
            pltpu.VMEM((TOK, 2 * half), BF16),
            pltpu.VMEM((TOK, 128), F32),
            pltpu.VMEM((TOK, 128), F32),
        ],
        compiler_params=params(60),
    )(late_slots, pack, inv, sums, gain, part, hidden, *grads[4:])
    return grad_hidden, router_grad


def solution(mesh):
    rows = P(("seq", "exp"), None)
    in_specs = (
        rows,
        rows,
        P(),
        rows,
        P(),
        rows,
        P("seq", "exp", None, None),
        P("seq", "exp", None, None),
    )
    return jax.shard_map(body, mesh=mesh, in_specs=in_specs, out_specs=(rows, P()), check_vma=False)
```

```python
import jax
import jax.numpy as jnp
from jax import lax
from jax.experimental import pallas as pl
from jax.experimental.pallas import tpu as pltpu
from jax.sharding import PartitionSpec as P

D = 8192
EXPERTS = 16
TOK = 128
CAP = 24
ROWS = 2 * CAP
TOKENS = 16384
AXES = ("seq", "exp")
CHUNK = 1024
F32 = jnp.float32
BF16 = jnp.bfloat16
VMEM = pl.BlockSpec(memory_space=pltpu.VMEM)

ROUTES = ((0, 0), (1, 0), (3, 0), (2, 0), (1, 1), (3, 1), (2, 1), (0, 1))


def coords():
    s, e = lax.axis_index("seq"), lax.axis_index("exp")
    return {"y": s >> 2, "z": s & 3, "x": e >> 1, "c": e & 1}


STRIDE = {"y": 32, "z": 8, "x": 2, "c": 1}
SIZE = {"y": 4, "z": 4, "x": 4, "c": 2}


def shift_perm(axis, d):
    out = []
    for i in range(128):
        a = (i // STRIDE[axis]) % SIZE[axis]
        out.append((i, i + ((a + d) % SIZE[axis] - a) * STRIDE[axis]))
    return out


def xor_perm(axis, d):
    return [(i, i ^ (d * STRIDE[axis])) for i in range(128)]


def after(*xs):
    return lax.optimization_barrier(xs)


def ring_permute(v, s, m):
    perm = [(i, (((i >> 1) + s) % 4) * 2 + ((i & 1) ^ m)) for i in range(8)]
    return lax.ppermute(v, "exp", perm)


def slot_numbers(sources):
    base = jnp.stack(sources).astype(F32) * ROWS
    return (base[:, None] + jnp.arange(ROWS, dtype=F32)[None, :]).reshape(1, len(sources) * ROWS)


def split3(v):
    a = v.astype(BF16)
    r = v - a.astype(F32)
    b = r.astype(BF16)
    c = (r - b.astype(F32)).astype(BF16)
    return a, b, c


def pre_kernel(ids_ref, logits_ref, pack_ref, probs_ref, counts_ref):
    ids = ids_ref[...]
    logits = logits_ref[...]
    labels = lax.broadcasted_iota(jnp.int32, (TOK, EXPERTS), 1)
    oh = [(ids[:, k : k + 1] == labels).astype(F32) for k in range(2)]
    both = oh[0] + oh[1]
    row = lax.broadcasted_iota(jnp.int32, (TOK, TOK), 0)
    col = lax.broadcasted_iota(jnp.int32, (TOK, TOK), 1)
    before = (row > col).astype(F32).astype(BF16)
    ranks = jnp.dot(before, both.astype(BF16), preferred_element_type=F32)
    counts_ref[...] = jnp.broadcast_to(jnp.sum(both, axis=0, keepdims=True), (8, EXPERTS))
    index = [
        jnp.sum(oh[k] * (ranks + (CAP * labels).astype(F32)), axis=1, keepdims=True)
        for k in range(2)
    ]
    chosen = [jnp.sum(oh[k] * logits, axis=1, keepdims=True) for k in range(2)]
    top = jnp.maximum(chosen[0], chosen[1])
    w = [jnp.exp(c - top) for c in chosen]
    total = w[0] + w[1]
    e = jnp.exp(logits - jnp.max(logits, axis=1, keepdims=True))
    probs_ref[...] = e / jnp.sum(e, axis=1, keepdims=True)
    lane = lax.broadcasted_iota(jnp.int32, (TOK, 8), 1)
    pack = jnp.zeros((TOK, 8), F32)
    for i, v in enumerate((w[0] / total, w[1] / total, index[0], index[1])):
        pack = jnp.where(lane == i, v, pack)
    pack_ref[...] = pack


def mid_kernel(
    slots_ref,
    pack_ref,
    inv_ref,
    ids_ref,
    probs_ref,
    counts_ref,
    gain_ref,
    hidden_ref,
    grad_ref,
    *refs,
):
    blocks, shares = refs[:8], refs[8:11]
    logit_ref, partial_ref, dots_ref, left_ref, total_ref = refs[11:]
    stage, c = pl.program_id(0), pl.program_id(1)

    @pl.when(stage == 0)
    def _():
        picked = jnp.concatenate([b[...] for b in blocks], axis=0)
        d = lax.dot_general(
            grad_ref[...], picked, (((1,), (1,)), ((), ())), preferred_element_type=F32
        )

        @pl.when(c == 0)
        def _():
            dots_ref[...] = d
            total = counts_ref[...]
            for b in shares:
                other = b[...].astype(F32)[0:8]
                total = total + other[:, :EXPERTS] + other[:, EXPERTS : 2 * EXPERTS]
            total_ref[...] = total

        @pl.when(c > 0)
        def _():
            dots_ref[...] += d

    @pl.when((stage == 1) & (c == 0))
    def _():
        pack = pack_ref[...]
        gate = [pack[:, 0:1], pack[:, 1:2]]
        slots = slots_ref[...]
        dots = dots_ref[...]
        gate_dot = [
            jnp.sum(jnp.where(slots == pack[:, 2 + k : 3 + k], dots, 0.0), axis=1, keepdims=True)
            .astype(BF16)
            .astype(F32)
            for k in range(2)
        ]
        mean = gate[0] * gate_dot[0] + gate[1] * gate_dot[1]
        ids = ids_ref[...]
        labels = lax.broadcasted_iota(jnp.int32, (TOK, EXPERTS), 1)
        direct = jnp.zeros((TOK, EXPERTS), F32)
        for k in range(2):
            chosen = gate[k] * (gate_dot[k] - mean)
            direct = direct + jnp.where(ids[:, k : k + 1] == labels, chosen, 0.0)
        probs = probs_ref[...]
        load = total_ref[0:1, :] * (EXPERTS / (2 * TOKENS))
        aux = probs * (load - jnp.sum(probs * load, axis=1, keepdims=True))
        logit = direct + aux
        logit = logit * inv_ref[...]
        logit_ref[...] = logit
        left_ref[...] = jnp.concatenate(split3(logit), axis=1)

    @pl.when(stage == 1)
    def _():
        p = lax.dot_general(
            left_ref[...], hidden_ref[...], (((0,), (0,)), ((), ())), preferred_element_type=F32
        )
        p = (p[0:16] + p[16:32] + p[32:48]) * (gain_ref[...] * (1.0 / 128.0))
        for j in range(WIDE // 1024):
            partial_ref[:, c * (WIDE // 1024) + j, :] = p[:, j * 1024 : (j + 1) * 1024]


def weights(slots, pack, inv):
    w = jnp.where(slots == pack[:, 2:3], pack[:, 0:1], 0.0)
    w = w + jnp.where(slots == pack[:, 3:4], pack[:, 1:2], 0.0)
    return split3(w * inv)[:2]


def row_sums(scaled, hidden):
    prod = scaled * hidden.astype(F32)
    total = prod[:, 0:128]
    for j in range(1, WIDE // 128):
        total = total + prod[:, j * 128 : (j + 1) * 128]
    return total


def half_kernel(
    slots_ref, pack_ref, inv_ref, logit_ref, weight_ref, gain_ref, hidden_ref, grad_ref, *refs
):
    blocks, (part_ref, sums_ref, left_ref) = refs[:-3], refs[-3:]
    c = pl.program_id(0)

    @pl.when(c == 0)
    def _():
        w_hi, w_lo = weights(slots_ref[...], pack_ref[...], inv_ref[...])
        l0, l1, l2 = split3(logit_ref[...])
        left_ref[...] = jnp.concatenate([w_hi, w_lo, l0, l0, l0, l1, l1, l2], axis=1)
        sums_ref[...] = jnp.zeros_like(sums_ref)

    r0, r1, r2 = split3(weight_ref[...])
    rows = [b[...] for b in blocks]
    right = jnp.concatenate(rows + rows + [r0, r1, r2, r0, r1, r0], axis=0)
    scaled = jnp.dot(left_ref[...], right, preferred_element_type=F32) * gain_ref[...]
    part_ref[...] = grad_ref[...].astype(F32) + scaled
    sums_ref[...] += row_sums(scaled, hidden_ref[...])


def last_kernel(
    slots_ref, pack_ref, inv_ref, sums_ref, gain_ref, part_ref, hidden_ref, *refs
):
    blocks, (out_ref, part_scr, hidden_scr, left_ref, acc_ref, factor_ref) = refs[:-6], refs[-6:]
    stage, c = pl.program_id(0), pl.program_id(1)
    cols = pl.ds(pl.multiple_of(c * WIDE, WIDE), WIDE)

    @pl.when((stage == 0) & (c == 0))
    def _():
        left_ref[...] = jnp.concatenate(
            weights(slots_ref[...], pack_ref[...], inv_ref[...]), axis=1
        )
        acc_ref[...] = sums_ref[...]

    @pl.when(stage == 0)
    def _():
        rows = [b[...] for b in blocks]
        right = jnp.concatenate(rows + rows, axis=0)
        scaled = jnp.dot(left_ref[...], right, preferred_element_type=F32) * gain_ref[...]
        part_scr[:, cols] = part_ref[...] + scaled
        hidden = hidden_ref[...]
        hidden_scr[:, cols] = hidden
        acc_ref[...] += row_sums(scaled, hidden)

    @pl.when((stage == 1) & (c == 0))
    def _():
        inv = inv_ref[...]
        mean = jnp.sum(acc_ref[...], axis=1, keepdims=True) / D
        factor_ref[...] = jnp.broadcast_to(inv * inv * mean, (TOK, 128))

    @pl.when(stage == 1)
    def _():
        normed = hidden_scr[:, cols].astype(F32) * factor_ref[:, 0:1]
        out_ref[...] = (part_scr[:, cols] - normed).astype(BF16)


STEPS = 4
WIDE = D // STEPS


def first(rows):
    return pl.BlockSpec((rows, WIDE), lambda p, c: (0, jnp.where(p == 0, c, STEPS - 1)))


def second(rows):
    return pl.BlockSpec((rows, WIDE), lambda p, c: (0, jnp.where(p == 0, 0, c)))


def params(mib):
    return pltpu.CompilerParams(vmem_limit_bytes=mib * 1024 * 1024)


def body(
    grad_out, hidden, norm_gain, router_logits, router_weight, expert_ids, expert_grad, expert_out
):
    at = coords()
    gain = norm_gain.reshape(1, D)
    sources = [((at["x"] - s) & 3) * 2 + (at["c"] ^ m) for s, m in ROUTES]
    slots = slot_numbers(sources)
    early_slots = slot_numbers([sources[i] for i in (0, 1, 2, 3, 7)])
    late_slots = slot_numbers([sources[i] for i in (6, 4, 5)])

    def block(array, s, m):
        to = ((at["x"] + s) & 3) * 2 + (at["c"] ^ m)
        return lax.dynamic_slice(array, (0, 0, to * CAP, 0), (1, 2, CAP, D)).reshape(ROWS, D)

    ready = [block(expert_out, s, m) for s, m in ROUTES[1:4]]
    ids, *ready = after(expert_ids, *ready)
    outs = [ring_permute(b, s, m) for b, (s, m) in zip(ready, ROUTES[1:4])]

    pack, probs, counts = pl.pallas_call(
        pre_kernel,
        out_shape=(
            jax.ShapeDtypeStruct((TOK, 8), F32),
            jax.ShapeDtypeStruct((TOK, EXPERTS), F32),
            jax.ShapeDtypeStruct((8, EXPERTS), F32),
        ),
        in_specs=[VMEM] * 2,
        out_specs=(VMEM,) * 3,
        compiler_params=params(8),
    )(ids, router_logits)
    wide = hidden.astype(F32)
    inv = lax.rsqrt(jnp.mean(wide * wide, axis=1, keepdims=True) + 1e-05)
    tally = [counts]
    for axis, d in (("y", 1), ("y", 2), ("z", 1), ("z", 2), ("c", 1)):
        tally.append(tally[-1] + lax.ppermute(tally[-1], AXES, xor_perm(axis, d)))
    share = tally[5][0:1].astype(BF16)
    share = jnp.concatenate([share, (tally[5][0:1] - share.astype(F32)).astype(BF16)], axis=1)
    share = jnp.broadcast_to(jnp.pad(share, ((0, 0), (0, 128 - 2 * EXPERTS))), (ROWS, 128))

    source, tally[1] = after(expert_out, tally[1])
    ready = [block(source, s, m) for s, m in ROUTES[4:]]
    ready = [jnp.concatenate([b, share], axis=1) for b in ready[:3]] + ready[3:]
    for n, (b, (s, m)) in enumerate(zip(ready, ROUTES[4:])):
        if n != 1:
            b, outs[n % 3] = after(b, outs[n % 3])
        outs.append(ring_permute(b, s, m))
    own_out = block(expert_out, 0, 0)

    source, tally[2] = after(expert_grad, tally[2])
    grads = [block(source, 0, 0)]
    for n, (s, m) in zip((3, 3, 4, 4), ROUTES[1:4] + ROUTES[7:]):
        b, outs[n] = after(block(source, s, m), outs[n])
        grads.append(ring_permute(b, s, m))
    source, tally[3] = after(expert_grad, tally[3])
    late = [ROUTES[i] for i in (6, 4, 5)]
    rest = [block(source, s, m) for s, m in late]

    small = lambda *shape: pl.BlockSpec(shape, lambda p, c: (0,) * len(shape))
    logit, partial = pl.pallas_call(
        mid_kernel,
        grid=(2, STEPS),
        out_shape=(
            jax.ShapeDtypeStruct((TOK, EXPERTS), F32),
            jax.ShapeDtypeStruct((EXPERTS, 8, 1024), F32),
        ),
        in_specs=[
            small(1, 8 * ROWS),
            small(TOK, 8),
            small(TOK, 1),
            small(TOK, 2),
            small(TOK, EXPERTS),
            small(8, EXPERTS),
            second(1),
            second(TOK),
            first(TOK),
        ]
        + [first(ROWS)] * 8
        + [pl.BlockSpec((ROWS, 128), lambda p, c: (0, D // 128))] * 3,
        out_specs=(
            small(TOK, EXPERTS),
            small(EXPERTS, 8, 1024),
        ),
        scratch_shapes=[
            pltpu.VMEM((TOK, 8 * ROWS), F32),
            pltpu.VMEM((TOK, 3 * EXPERTS), BF16),
            pltpu.VMEM((8, EXPERTS), F32),
        ],
        cost_estimate=pl.CostEstimate(flops=20_000_000_000, bytes_accessed=60_000_000, transcendentals=0),
        compiler_params=params(20),
    )(slots, pack, inv, expert_ids, probs, tally[5], gain, hidden, grad_out, own_out, *outs, *outs[3:6])
    partial = jnp.sum(lax.all_to_all(partial, "seq", 0, 0, tiled=True), axis=0)
    partial = partial + lax.ppermute(partial, AXES, xor_perm("c", 1))
    near = [lax.ppermute(partial, AXES, xor_perm("x", d)) for d in (1, 2)]
    partial, *grads[1:5] = after(partial, *grads[1:5])
    partial = (partial + near[0]) + (near[1] + lax.ppermute(partial, AXES, xor_perm("x", 3)))
    partial, *rest = after(partial, *rest)
    grads += [ring_permute(b, s, m) for b, (s, m) in zip(rest, late)]
    once = lambda rows: pl.BlockSpec((rows, WIDE), lambda c: (0, c))
    fixed = lambda *shape: pl.BlockSpec(shape, lambda c: (0,) * len(shape))
    early, last = 5 * ROWS, 3 * ROWS
    begin, partial = after(pack, partial)
    part, sums = pl.pallas_call(
        half_kernel,
        grid=(STEPS,),
        out_shape=(
            jax.ShapeDtypeStruct((TOK, D), F32),
            jax.ShapeDtypeStruct((TOK, 128), F32),
        ),
        in_specs=[
            fixed(1, early),
            fixed(TOK, 8),
            fixed(TOK, 1),
            fixed(TOK, EXPERTS),
            once(EXPERTS),
            once(1),
            once(TOK),
            once(TOK),
        ]
        + [once(ROWS)] * 5,
        out_specs=(once(TOK), fixed(TOK, 128)),
        scratch_shapes=[pltpu.VMEM((TOK, 2 * early + 6 * EXPERTS), BF16)],
        compiler_params=params(60),
        cost_estimate=pl.CostEstimate(
            flops=10_000_000_000, bytes_accessed=30_000_000, transcendentals=0
        ),
    )(early_slots, begin, inv, logit, router_weight, gain, hidden, grad_out, *grads[:5])
    partial, sums = after(partial, sums)
    router_grad = lax.all_gather(partial, "seq").reshape(EXPERTS, D)

    grad_hidden = pl.pallas_call(
        last_kernel,
        grid=(2, STEPS),
        out_shape=jax.ShapeDtypeStruct((TOK, D), BF16),
        in_specs=[
            small(1, last),
            small(TOK, 8),
            small(TOK, 1),
            small(TOK, 128),
            first(1),
            first(TOK),
            first(TOK),
        ]
        + [first(ROWS)] * 3,
        out_specs=second(TOK),
        scratch_shapes=[
            pltpu.VMEM((TOK, D), F32),
            pltpu.VMEM((TOK, D), BF16),
            pltpu.VMEM((TOK, 2 * last), BF16),
            pltpu.VMEM((TOK, 128), F32),
            pltpu.VMEM((TOK, 128), F32),
        ],
        compiler_params=params(60),
    )(late_slots, pack, inv, sums, gain, part, hidden, *grads[5:])
    return grad_hidden, router_grad


def solution(mesh):
    rows = P(("seq", "exp"), None)
    in_specs = (
        rows,
        rows,
        P(),
        rows,
        P(),
        rows,
        P("seq", "exp", None, None),
        P("seq", "exp", None, None),
    )
    return jax.shard_map(body, mesh=mesh, in_specs=in_specs, out_specs=(rows, P()), check_vma=False)
```

```python
import jax
import jax.numpy as jnp
from jax import lax
from jax.experimental import pallas as pl
from jax.experimental.pallas import tpu as pltpu
from jax.sharding import PartitionSpec as P

D = 8192
EXPERTS = 16
TOK = 128
CAP = 24
ROWS = 2 * CAP
TOKENS = 16384
AXES = ("seq", "exp")
CHUNK = 1024
F32 = jnp.float32
BF16 = jnp.bfloat16
VMEM = pl.BlockSpec(memory_space=pltpu.VMEM)

ROUTES = ((0, 0), (1, 0), (3, 0), (2, 0), (1, 1), (3, 1), (2, 1), (0, 1))


def coords():
    s, e = lax.axis_index("seq"), lax.axis_index("exp")
    return {"y": s >> 2, "z": s & 3, "x": e >> 1, "c": e & 1}


STRIDE = {"y": 32, "z": 8, "x": 2, "c": 1}
SIZE = {"y": 4, "z": 4, "x": 4, "c": 2}


def shift_perm(axis, d):
    out = []
    for i in range(128):
        a = (i // STRIDE[axis]) % SIZE[axis]
        out.append((i, i + ((a + d) % SIZE[axis] - a) * STRIDE[axis]))
    return out


def xor_perm(axis, d):
    return [(i, i ^ (d * STRIDE[axis])) for i in range(128)]


def after(*xs):
    return lax.optimization_barrier(xs)


def ring_permute(v, s, m):
    perm = [(i, (((i >> 1) + s) % 4) * 2 + ((i & 1) ^ m)) for i in range(8)]
    return lax.ppermute(v, "exp", perm)


def slot_numbers(sources):
    base = jnp.stack(sources).astype(F32) * ROWS
    return (base[:, None] + jnp.arange(ROWS, dtype=F32)[None, :]).reshape(1, len(sources) * ROWS)


def split3(v):
    a = v.astype(BF16)
    r = v - a.astype(F32)
    b = r.astype(BF16)
    c = (r - b.astype(F32)).astype(BF16)
    return a, b, c


def pre_kernel(ids_ref, logits_ref, pack_ref, probs_ref, counts_ref):
    ids = ids_ref[...]
    logits = logits_ref[...]
    labels = lax.broadcasted_iota(jnp.int32, (TOK, EXPERTS), 1)
    oh = [(ids[:, k : k + 1] == labels).astype(F32) for k in range(2)]
    both = oh[0] + oh[1]
    row = lax.broadcasted_iota(jnp.int32, (TOK, TOK), 0)
    col = lax.broadcasted_iota(jnp.int32, (TOK, TOK), 1)
    before = (row > col).astype(F32).astype(BF16)
    ranks = jnp.dot(before, both.astype(BF16), preferred_element_type=F32)
    counts_ref[...] = jnp.broadcast_to(jnp.sum(both, axis=0, keepdims=True), (8, EXPERTS))
    index = [
        jnp.sum(oh[k] * (ranks + (CAP * labels).astype(F32)), axis=1, keepdims=True)
        for k in range(2)
    ]
    chosen = [jnp.sum(oh[k] * logits, axis=1, keepdims=True) for k in range(2)]
    top = jnp.maximum(chosen[0], chosen[1])
    w = [jnp.exp(c - top) for c in chosen]
    total = w[0] + w[1]
    e = jnp.exp(logits - jnp.max(logits, axis=1, keepdims=True))
    probs_ref[...] = e / jnp.sum(e, axis=1, keepdims=True)
    lane = lax.broadcasted_iota(jnp.int32, (TOK, 8), 1)
    pack = jnp.zeros((TOK, 8), F32)
    for i, v in enumerate((w[0] / total, w[1] / total, index[0], index[1])):
        pack = jnp.where(lane == i, v, pack)
    pack_ref[...] = pack


def mid_kernel(
    slots_ref,
    pack_ref,
    inv_ref,
    ids_ref,
    probs_ref,
    counts_ref,
    gain_ref,
    hidden_ref,
    grad_ref,
    *refs,
):
    blocks, shares = refs[:8], refs[8:11]
    logit_ref, partial_ref, dots_ref, left_ref, total_ref = refs[11:]
    stage, c = pl.program_id(0), pl.program_id(1)

    @pl.when(stage == 0)
    def _():
        picked = jnp.concatenate([b[...] for b in blocks], axis=0)
        d = lax.dot_general(
            grad_ref[...], picked, (((1,), (1,)), ((), ())), preferred_element_type=F32
        )

        @pl.when(c == 0)
        def _():
            dots_ref[...] = d
            total = counts_ref[...]
            for b in shares:
                other = b[...].astype(F32)[0:8]
                total = total + other[:, :EXPERTS] + other[:, EXPERTS : 2 * EXPERTS]
            total_ref[...] = total

        @pl.when(c > 0)
        def _():
            dots_ref[...] += d

    @pl.when((stage == 1) & (c == 0))
    def _():
        pack = pack_ref[...]
        gate = [pack[:, 0:1], pack[:, 1:2]]
        slots = slots_ref[...]
        dots = dots_ref[...]
        gate_dot = [
            jnp.sum(jnp.where(slots == pack[:, 2 + k : 3 + k], dots, 0.0), axis=1, keepdims=True)
            .astype(BF16)
            .astype(F32)
            for k in range(2)
        ]
        mean = gate[0] * gate_dot[0] + gate[1] * gate_dot[1]
        ids = ids_ref[...]
        labels = lax.broadcasted_iota(jnp.int32, (TOK, EXPERTS), 1)
        direct = jnp.zeros((TOK, EXPERTS), F32)
        for k in range(2):
            chosen = gate[k] * (gate_dot[k] - mean)
            direct = direct + jnp.where(ids[:, k : k + 1] == labels, chosen, 0.0)
        probs = probs_ref[...]
        load = total_ref[0:1, :] * (EXPERTS / (2 * TOKENS))
        aux = probs * (load - jnp.sum(probs * load, axis=1, keepdims=True))
        logit = direct + aux
        logit = logit * inv_ref[...]
        logit_ref[...] = logit
        left_ref[...] = jnp.concatenate(split3(logit), axis=1)

    @pl.when(stage == 1)
    def _():
        p = lax.dot_general(
            left_ref[...], hidden_ref[...], (((0,), (0,)), ((), ())), preferred_element_type=F32
        )
        p = (p[0:16] + p[16:32] + p[32:48]) * (gain_ref[...] * (1.0 / 128.0))
        for j in range(WIDE // 1024):
            partial_ref[:, c * (WIDE // 1024) + j, :] = p[:, j * 1024 : (j + 1) * 1024]


def weights(slots, pack, inv):
    w = jnp.where(slots == pack[:, 2:3], pack[:, 0:1], 0.0)
    w = w + jnp.where(slots == pack[:, 3:4], pack[:, 1:2], 0.0)
    return split3(w * inv)[:2]


def row_sums(scaled, hidden):
    prod = scaled * hidden.astype(F32)
    total = prod[:, 0:128]
    for j in range(1, WIDE // 128):
        total = total + prod[:, j * 128 : (j + 1) * 128]
    return total


def half_kernel(
    slots_ref, pack_ref, inv_ref, logit_ref, weight_ref, gain_ref, hidden_ref, grad_ref, *refs
):
    blocks, (part_ref, sums_ref, left_ref) = refs[:-3], refs[-3:]
    c = pl.program_id(0)

    @pl.when(c == 0)
    def _():
        w_hi, w_lo = weights(slots_ref[...], pack_ref[...], inv_ref[...])
        l0, l1, l2 = split3(logit_ref[...])
        left_ref[...] = jnp.concatenate([w_hi, w_lo, l0, l0, l0, l1, l1, l2], axis=1)
        sums_ref[...] = jnp.zeros_like(sums_ref)

    r0, r1, r2 = split3(weight_ref[...])
    rows = [b[...] for b in blocks]
    right = jnp.concatenate(rows + rows + [r0, r1, r2, r0, r1, r0], axis=0)
    scaled = jnp.dot(left_ref[...], right, preferred_element_type=F32) * gain_ref[...]
    part_ref[...] = grad_ref[...].astype(F32) + scaled
    sums_ref[...] += row_sums(scaled, hidden_ref[...])


def last_kernel(
    slots_ref, pack_ref, inv_ref, sums_ref, gain_ref, part_ref, hidden_ref, *refs
):
    blocks, (out_ref, part_scr, hidden_scr, left_ref, acc_ref, factor_ref) = refs[:-6], refs[-6:]
    stage, c = pl.program_id(0), pl.program_id(1)
    cols = pl.ds(pl.multiple_of(c * WIDE, WIDE), WIDE)

    @pl.when((stage == 0) & (c == 0))
    def _():
        left_ref[...] = jnp.concatenate(
            weights(slots_ref[...], pack_ref[...], inv_ref[...]), axis=1
        )
        acc_ref[...] = sums_ref[...]

    @pl.when(stage == 0)
    def _():
        rows = [b[...] for b in blocks]
        right = jnp.concatenate(rows + rows, axis=0)
        scaled = jnp.dot(left_ref[...], right, preferred_element_type=F32) * gain_ref[...]
        part_scr[:, cols] = part_ref[...] + scaled
        hidden = hidden_ref[...]
        hidden_scr[:, cols] = hidden
        acc_ref[...] += row_sums(scaled, hidden)

    @pl.when((stage == 1) & (c == 0))
    def _():
        inv = inv_ref[...]
        mean = jnp.sum(acc_ref[...], axis=1, keepdims=True) / D
        factor_ref[...] = jnp.broadcast_to(inv * inv * mean, (TOK, 128))

    @pl.when(stage == 1)
    def _():
        normed = hidden_scr[:, cols].astype(F32) * factor_ref[:, 0:1]
        out_ref[...] = (part_scr[:, cols] - normed).astype(BF16)


STEPS = 4
WIDE = D // STEPS


def first(rows):
    return pl.BlockSpec((rows, WIDE), lambda p, c: (0, jnp.where(p == 0, c, STEPS - 1)))


def second(rows):
    return pl.BlockSpec((rows, WIDE), lambda p, c: (0, jnp.where(p == 0, 0, c)))


def params(mib):
    return pltpu.CompilerParams(vmem_limit_bytes=mib * 1024 * 1024)


def body(
    grad_out, hidden, norm_gain, router_logits, router_weight, expert_ids, expert_grad, expert_out
):
    at = coords()
    gain = norm_gain.reshape(1, D)
    sources = [((at["x"] - s) & 3) * 2 + (at["c"] ^ m) for s, m in ROUTES]
    slots = slot_numbers(sources)
    early_slots = slot_numbers([sources[i] for i in (0, 1, 2, 3, 7)])
    late_slots = slot_numbers([sources[i] for i in (6, 4, 5)])

    def block(array, s, m):
        to = ((at["x"] + s) & 3) * 2 + (at["c"] ^ m)
        return lax.dynamic_slice(array, (0, 0, to * CAP, 0), (1, 2, CAP, D)).reshape(ROWS, D)

    ready = [block(expert_out, s, m) for s, m in ROUTES[1:4]]
    ids, *ready = after(expert_ids, *ready)
    outs = [ring_permute(b, s, m) for b, (s, m) in zip(ready, ROUTES[1:4])]

    pack, probs, counts = pl.pallas_call(
        pre_kernel,
        out_shape=(
            jax.ShapeDtypeStruct((TOK, 8), F32),
            jax.ShapeDtypeStruct((TOK, EXPERTS), F32),
            jax.ShapeDtypeStruct((8, EXPERTS), F32),
        ),
        in_specs=[VMEM] * 2,
        out_specs=(VMEM,) * 3,
        compiler_params=params(8),
    )(ids, router_logits)
    wide = hidden.astype(F32)
    inv = lax.rsqrt(jnp.mean(wide * wide, axis=1, keepdims=True) + 1e-05)
    tally = [counts]
    for axis, d in (("y", 1), ("y", 2), ("z", 1), ("z", 2), ("c", 1)):
        tally.append(tally[-1] + lax.ppermute(tally[-1], AXES, xor_perm(axis, d)))
    share = tally[5][0:1].astype(BF16)
    share = jnp.concatenate([share, (tally[5][0:1] - share.astype(F32)).astype(BF16)], axis=1)
    share = jnp.broadcast_to(jnp.pad(share, ((0, 0), (0, 128 - 2 * EXPERTS))), (ROWS, 128))

    source, tally[1] = after(expert_out, tally[1])
    ready = [block(source, s, m) for s, m in ROUTES[4:]]
    ready = [jnp.concatenate([b, share], axis=1) for b in ready[:3]] + ready[3:]
    for n, (b, (s, m)) in enumerate(zip(ready, ROUTES[4:])):
        if n in (0, 3):
            b, outs[n // 3 * 2] = after(b, outs[n // 3 * 2])
        outs.append(ring_permute(b, s, m))
    own_out = block(expert_out, 0, 0)

    source, tally[2] = after(expert_grad, tally[2])
    grads = [block(source, 0, 0)]
    for n, (s, m) in zip((3, 3, 4, 4), ROUTES[1:4] + ROUTES[7:]):
        b, outs[n] = after(block(source, s, m), outs[n])
        grads.append(ring_permute(b, s, m))
    source, tally[3] = after(expert_grad, tally[3])
    late = [ROUTES[i] for i in (6, 4, 5)]
    rest = [block(source, s, m) for s, m in late]

    small = lambda *shape: pl.BlockSpec(shape, lambda p, c: (0,) * len(shape))
    logit, partial = pl.pallas_call(
        mid_kernel,
        grid=(2, STEPS),
        out_shape=(
            jax.ShapeDtypeStruct((TOK, EXPERTS), F32),
            jax.ShapeDtypeStruct((EXPERTS, 8, 1024), F32),
        ),
        in_specs=[
            small(1, 8 * ROWS),
            small(TOK, 8),
            small(TOK, 1),
            small(TOK, 2),
            small(TOK, EXPERTS),
            small(8, EXPERTS),
            second(1),
            second(TOK),
            first(TOK),
        ]
        + [first(ROWS)] * 8
        + [pl.BlockSpec((ROWS, 128), lambda p, c: (0, D // 128))] * 3,
        out_specs=(
            small(TOK, EXPERTS),
            small(EXPERTS, 8, 1024),
        ),
        scratch_shapes=[
            pltpu.VMEM((TOK, 8 * ROWS), F32),
            pltpu.VMEM((TOK, 3 * EXPERTS), BF16),
            pltpu.VMEM((8, EXPERTS), F32),
        ],
        cost_estimate=pl.CostEstimate(flops=20_000_000_000, bytes_accessed=60_000_000, transcendentals=0),
        compiler_params=params(20),
    )(slots, pack, inv, expert_ids, probs, tally[5], gain, hidden, grad_out, own_out, *outs, *outs[3:6])
    partial = jnp.sum(lax.all_to_all(partial, "seq", 0, 0, tiled=True), axis=0)
    partial = partial + lax.ppermute(partial, AXES, xor_perm("c", 1))
    near = [lax.ppermute(partial, AXES, xor_perm("x", d)) for d in (1, 2)]
    partial, *grads[1:5] = after(partial, *grads[1:5])
    partial = (partial + near[0]) + (near[1] + lax.ppermute(partial, AXES, xor_perm("x", 3)))
    partial, *rest = after(partial, *rest)
    grads += [ring_permute(b, s, m) for b, (s, m) in zip(rest, late)]
    once = lambda rows: pl.BlockSpec((rows, WIDE), lambda c: (0, c))
    fixed = lambda *shape: pl.BlockSpec(shape, lambda c: (0,) * len(shape))
    early, last = 5 * ROWS, 3 * ROWS
    begin, partial = after(pack, partial)
    part, sums = pl.pallas_call(
        half_kernel,
        grid=(STEPS,),
        out_shape=(
            jax.ShapeDtypeStruct((TOK, D), F32),
            jax.ShapeDtypeStruct((TOK, 128), F32),
        ),
        in_specs=[
            fixed(1, early),
            fixed(TOK, 8),
            fixed(TOK, 1),
            fixed(TOK, EXPERTS),
            once(EXPERTS),
            once(1),
            once(TOK),
            once(TOK),
        ]
        + [once(ROWS)] * 5,
        out_specs=(once(TOK), fixed(TOK, 128)),
        scratch_shapes=[pltpu.VMEM((TOK, 2 * early + 6 * EXPERTS), BF16)],
        compiler_params=params(60),
        cost_estimate=pl.CostEstimate(
            flops=10_000_000_000, bytes_accessed=30_000_000, transcendentals=0
        ),
    )(early_slots, begin, inv, logit, router_weight, gain, hidden, grad_out, *grads[:5])
    partial, sums = after(partial, sums)
    router_grad = lax.all_gather(partial, "seq").reshape(EXPERTS, D)

    grad_hidden = pl.pallas_call(
        last_kernel,
        grid=(2, STEPS),
        out_shape=jax.ShapeDtypeStruct((TOK, D), BF16),
        in_specs=[
            small(1, last),
            small(TOK, 8),
            small(TOK, 1),
            small(TOK, 128),
            first(1),
            first(TOK),
            first(TOK),
        ]
        + [first(ROWS)] * 3,
        out_specs=second(TOK),
        scratch_shapes=[
            pltpu.VMEM((TOK, D), F32),
            pltpu.VMEM((TOK, D), BF16),
            pltpu.VMEM((TOK, 2 * last), BF16),
            pltpu.VMEM((TOK, 128), F32),
            pltpu.VMEM((TOK, 128), F32),
        ],
        compiler_params=params(60),
    )(late_slots, pack, inv, sums, gain, part, hidden, *grads[5:])
    return grad_hidden, router_grad


def solution(mesh):
    rows = P(("seq", "exp"), None)
    in_specs = (
        rows,
        rows,
        P(),
        rows,
        P(),
        rows,
        P("seq", "exp", None, None),
        P("seq", "exp", None, None),
    )
    return jax.shard_map(body, mesh=mesh, in_specs=in_specs, out_specs=(rows, P()), check_vma=False)
```

```python
import jax
import jax.numpy as jnp
from jax import lax
from jax.experimental import pallas as pl
from jax.experimental.pallas import tpu as pltpu
from jax.sharding import PartitionSpec as P

D = 8192
EXPERTS = 16
TOK = 128
CAP = 24
ROWS = 2 * CAP
TOKENS = 16384
AXES = ("seq", "exp")
CHUNK = 1024
F32 = jnp.float32
BF16 = jnp.bfloat16
VMEM = pl.BlockSpec(memory_space=pltpu.VMEM)

ROUTES = ((0, 0), (1, 0), (3, 0), (2, 0), (1, 1), (3, 1), (2, 1), (0, 1))


def coords():
    s, e = lax.axis_index("seq"), lax.axis_index("exp")
    return {"y": s >> 2, "z": s & 3, "x": e >> 1, "c": e & 1}


STRIDE = {"y": 32, "z": 8, "x": 2, "c": 1}
SIZE = {"y": 4, "z": 4, "x": 4, "c": 2}


def shift_perm(axis, d):
    out = []
    for i in range(128):
        a = (i // STRIDE[axis]) % SIZE[axis]
        out.append((i, i + ((a + d) % SIZE[axis] - a) * STRIDE[axis]))
    return out


def xor_perm(axis, d):
    return [(i, i ^ (d * STRIDE[axis])) for i in range(128)]


def after(*xs):
    return lax.optimization_barrier(xs)


def ring_permute(v, s, m):
    perm = [(i, (((i >> 1) + s) % 4) * 2 + ((i & 1) ^ m)) for i in range(8)]
    return lax.ppermute(v, "exp", perm)


def slot_numbers(sources):
    base = jnp.stack(sources).astype(F32) * ROWS
    return (base[:, None] + jnp.arange(ROWS, dtype=F32)[None, :]).reshape(1, len(sources) * ROWS)


def split3(v):
    a = v.astype(BF16)
    r = v - a.astype(F32)
    b = r.astype(BF16)
    c = (r - b.astype(F32)).astype(BF16)
    return a, b, c


def pre_kernel(ids_ref, logits_ref, pack_ref, probs_ref, counts_ref):
    ids = ids_ref[...]
    logits = logits_ref[...]
    labels = lax.broadcasted_iota(jnp.int32, (TOK, EXPERTS), 1)
    oh = [(ids[:, k : k + 1] == labels).astype(F32) for k in range(2)]
    both = oh[0] + oh[1]
    row = lax.broadcasted_iota(jnp.int32, (TOK, TOK), 0)
    col = lax.broadcasted_iota(jnp.int32, (TOK, TOK), 1)
    before = (row > col).astype(F32).astype(BF16)
    ranks = jnp.dot(before, both.astype(BF16), preferred_element_type=F32)
    counts_ref[...] = jnp.broadcast_to(jnp.sum(both, axis=0, keepdims=True), (8, EXPERTS))
    index = [
        jnp.sum(oh[k] * (ranks + (CAP * labels).astype(F32)), axis=1, keepdims=True)
        for k in range(2)
    ]
    chosen = [jnp.sum(oh[k] * logits, axis=1, keepdims=True) for k in range(2)]
    top = jnp.maximum(chosen[0], chosen[1])
    w = [jnp.exp(c - top) for c in chosen]
    total = w[0] + w[1]
    e = jnp.exp(logits - jnp.max(logits, axis=1, keepdims=True))
    probs_ref[...] = e / jnp.sum(e, axis=1, keepdims=True)
    lane = lax.broadcasted_iota(jnp.int32, (TOK, 8), 1)
    pack = jnp.zeros((TOK, 8), F32)
    for i, v in enumerate((w[0] / total, w[1] / total, index[0], index[1])):
        pack = jnp.where(lane == i, v, pack)
    pack_ref[...] = pack


def mid_kernel(
    slots_ref,
    pack_ref,
    inv_ref,
    ids_ref,
    probs_ref,
    counts_ref,
    gain_ref,
    hidden_ref,
    grad_ref,
    *refs,
):
    blocks, shares = refs[:8], refs[8:11]
    logit_ref, partial_ref, dots_ref, left_ref, total_ref = refs[11:]
    stage, c = pl.program_id(0), pl.program_id(1)

    @pl.when(stage == 0)
    def _():
        picked = jnp.concatenate([b[...] for b in blocks], axis=0)
        d = lax.dot_general(
            grad_ref[...], picked, (((1,), (1,)), ((), ())), preferred_element_type=F32
        )

        @pl.when(c == 0)
        def _():
            dots_ref[...] = d
            total = counts_ref[...]
            for b in shares:
                other = b[...].astype(F32)[0:8]
                total = total + other[:, :EXPERTS] + other[:, EXPERTS : 2 * EXPERTS]
            total_ref[...] = total

        @pl.when(c > 0)
        def _():
            dots_ref[...] += d

    @pl.when((stage == 1) & (c == 0))
    def _():
        pack = pack_ref[...]
        gate = [pack[:, 0:1], pack[:, 1:2]]
        slots = slots_ref[...]
        dots = dots_ref[...]
        gate_dot = [
            jnp.sum(jnp.where(slots == pack[:, 2 + k : 3 + k], dots, 0.0), axis=1, keepdims=True)
            .astype(BF16)
            .astype(F32)
            for k in range(2)
        ]
        mean = gate[0] * gate_dot[0] + gate[1] * gate_dot[1]
        ids = ids_ref[...]
        labels = lax.broadcasted_iota(jnp.int32, (TOK, EXPERTS), 1)
        direct = jnp.zeros((TOK, EXPERTS), F32)
        for k in range(2):
            chosen = gate[k] * (gate_dot[k] - mean)
            direct = direct + jnp.where(ids[:, k : k + 1] == labels, chosen, 0.0)
        probs = probs_ref[...]
        load = total_ref[0:1, :] * (EXPERTS / (2 * TOKENS))
        aux = probs * (load - jnp.sum(probs * load, axis=1, keepdims=True))
        logit = direct + aux
        logit = logit * inv_ref[...]
        logit_ref[...] = logit
        left_ref[...] = jnp.concatenate(split3(logit), axis=1)

    @pl.when(stage == 1)
    def _():
        p = lax.dot_general(
            left_ref[...], hidden_ref[...], (((0,), (0,)), ((), ())), preferred_element_type=F32
        )
        p = (p[0:16] + p[16:32] + p[32:48]) * (gain_ref[...] * (1.0 / 128.0))
        for j in range(WIDE // 1024):
            partial_ref[:, c * (WIDE // 1024) + j, :] = p[:, j * 1024 : (j + 1) * 1024]


def weights(slots, pack, inv):
    w = jnp.where(slots == pack[:, 2:3], pack[:, 0:1], 0.0)
    w = w + jnp.where(slots == pack[:, 3:4], pack[:, 1:2], 0.0)
    return split3(w * inv)[:2]


def row_sums(scaled, hidden):
    prod = scaled * hidden.astype(F32)
    total = prod[:, 0:128]
    for j in range(1, WIDE // 128):
        total = total + prod[:, j * 128 : (j + 1) * 128]
    return total


def half_kernel(
    slots_ref, pack_ref, inv_ref, logit_ref, weight_ref, gain_ref, hidden_ref, grad_ref, *refs
):
    blocks, (part_ref, sums_ref, left_ref) = refs[:-3], refs[-3:]
    c = pl.program_id(0)

    @pl.when(c == 0)
    def _():
        w_hi, w_lo = weights(slots_ref[...], pack_ref[...], inv_ref[...])
        l0, l1, l2 = split3(logit_ref[...])
        left_ref[...] = jnp.concatenate([w_hi, w_lo, l0, l0, l0, l1, l1, l2], axis=1)
        sums_ref[...] = jnp.zeros_like(sums_ref)

    r0, r1, r2 = split3(weight_ref[...])
    rows = [b[...] for b in blocks]
    right = jnp.concatenate(rows + rows + [r0, r1, r2, r0, r1, r0], axis=0)
    scaled = jnp.dot(left_ref[...], right, preferred_element_type=F32) * gain_ref[...]
    part_ref[...] = grad_ref[...].astype(F32) + scaled
    sums_ref[...] += row_sums(scaled, hidden_ref[...])


def last_kernel(
    slots_ref, pack_ref, inv_ref, sums_ref, gain_ref, part_ref, hidden_ref, *refs
):
    blocks, (out_ref, part_scr, hidden_scr, left_ref, acc_ref, factor_ref) = refs[:-6], refs[-6:]
    stage, c = pl.program_id(0), pl.program_id(1)
    cols = pl.ds(pl.multiple_of(c * WIDE, WIDE), WIDE)

    @pl.when((stage == 0) & (c == 0))
    def _():
        left_ref[...] = jnp.concatenate(
            weights(slots_ref[...], pack_ref[...], inv_ref[...]), axis=1
        )
        acc_ref[...] = sums_ref[...]

    @pl.when(stage == 0)
    def _():
        rows = [b[...] for b in blocks]
        right = jnp.concatenate(rows + rows, axis=0)
        scaled = jnp.dot(left_ref[...], right, preferred_element_type=F32) * gain_ref[...]
        part_scr[:, cols] = part_ref[...] + scaled
        hidden = hidden_ref[...]
        hidden_scr[:, cols] = hidden
        acc_ref[...] += row_sums(scaled, hidden)

    @pl.when((stage == 1) & (c == 0))
    def _():
        inv = inv_ref[...]
        mean = jnp.sum(acc_ref[...], axis=1, keepdims=True) / D
        factor_ref[...] = jnp.broadcast_to(inv * inv * mean, (TOK, 128))

    @pl.when(stage == 1)
    def _():
        normed = hidden_scr[:, cols].astype(F32) * factor_ref[:, 0:1]
        out_ref[...] = (part_scr[:, cols] - normed).astype(BF16)


STEPS = 8
WIDE = D // STEPS


def first(rows):
    return pl.BlockSpec((rows, WIDE), lambda p, c: (0, jnp.where(p == 0, c, STEPS - 1)))


def second(rows):
    return pl.BlockSpec((rows, WIDE), lambda p, c: (0, jnp.where(p == 0, 0, c)))


def params(mib):
    return pltpu.CompilerParams(vmem_limit_bytes=mib * 1024 * 1024)


def body(
    grad_out, hidden, norm_gain, router_logits, router_weight, expert_ids, expert_grad, expert_out
):
    at = coords()
    gain = norm_gain.reshape(1, D)
    sources = [((at["x"] - s) & 3) * 2 + (at["c"] ^ m) for s, m in ROUTES]
    slots = slot_numbers(sources)
    early_slots = slot_numbers([sources[i] for i in (0, 1, 2, 3, 7)])
    late_slots = slot_numbers([sources[i] for i in (6, 4, 5)])

    def block(array, s, m):
        to = ((at["x"] + s) & 3) * 2 + (at["c"] ^ m)
        return lax.dynamic_slice(array, (0, 0, to * CAP, 0), (1, 2, CAP, D)).reshape(ROWS, D)

    ready = [block(expert_out, s, m) for s, m in ROUTES[1:4]]
    ids, *ready = after(expert_ids, *ready)
    outs = [ring_permute(b, s, m) for b, (s, m) in zip(ready, ROUTES[1:4])]

    pack, probs, counts = pl.pallas_call(
        pre_kernel,
        out_shape=(
            jax.ShapeDtypeStruct((TOK, 8), F32),
            jax.ShapeDtypeStruct((TOK, EXPERTS), F32),
            jax.ShapeDtypeStruct((8, EXPERTS), F32),
        ),
        in_specs=[VMEM] * 2,
        out_specs=(VMEM,) * 3,
        compiler_params=params(8),
    )(ids, router_logits)
    wide = hidden.astype(F32)
    inv = lax.rsqrt(jnp.mean(wide * wide, axis=1, keepdims=True) + 1e-05)
    tally = [counts]
    for axis, d in (("y", 1), ("y", 2), ("z", 1), ("z", 2), ("c", 1)):
        tally.append(tally[-1] + lax.ppermute(tally[-1], AXES, xor_perm(axis, d)))
    share = tally[5][0:1].astype(BF16)
    share = jnp.concatenate([share, (tally[5][0:1] - share.astype(F32)).astype(BF16)], axis=1)
    share = jnp.broadcast_to(jnp.pad(share, ((0, 0), (0, 128 - 2 * EXPERTS))), (ROWS, 128))

    source, tally[1] = after(expert_out, tally[1])
    ready = [block(source, s, m) for s, m in ROUTES[4:]]
    ready = [jnp.concatenate([b, share], axis=1) for b in ready[:3]] + ready[3:]
    for n, (b, (s, m)) in enumerate(zip(ready, ROUTES[4:])):
        if n != 1:
            b, outs[n % 3] = after(b, outs[n % 3])
        outs.append(ring_permute(b, s, m))
    own_out = block(expert_out, 0, 0)

    source, tally[2] = after(expert_grad, tally[2])
    grads = [block(source, 0, 0)]
    for n, (s, m) in zip((3, 3, 4, 4), ROUTES[1:4] + ROUTES[7:]):
        b, outs[n] = after(block(source, s, m), outs[n])
        grads.append(ring_permute(b, s, m))
    source, tally[3] = after(expert_grad, tally[3])
    late = [ROUTES[i] for i in (6, 4, 5)]
    rest = [block(source, s, m) for s, m in late]

    small = lambda *shape: pl.BlockSpec(shape, lambda p, c: (0,) * len(shape))
    logit, partial = pl.pallas_call(
        mid_kernel,
        grid=(2, STEPS),
        out_shape=(
            jax.ShapeDtypeStruct((TOK, EXPERTS), F32),
            jax.ShapeDtypeStruct((EXPERTS, 8, 1024), F32),
        ),
        in_specs=[
            small(1, 8 * ROWS),
            small(TOK, 8),
            small(TOK, 1),
            small(TOK, 2),
            small(TOK, EXPERTS),
            small(8, EXPERTS),
            second(1),
            second(TOK),
            first(TOK),
        ]
        + [first(ROWS)] * 8
        + [pl.BlockSpec((ROWS, 128), lambda p, c: (0, D // 128))] * 3,
        out_specs=(
            small(TOK, EXPERTS),
            small(EXPERTS, 8, 1024),
        ),
        scratch_shapes=[
            pltpu.VMEM((TOK, 8 * ROWS), F32),
            pltpu.VMEM((TOK, 3 * EXPERTS), BF16),
            pltpu.VMEM((8, EXPERTS), F32),
        ],
        cost_estimate=pl.CostEstimate(flops=20_000_000_000, bytes_accessed=60_000_000, transcendentals=0),
        compiler_params=params(20),
    )(slots, pack, inv, expert_ids, probs, tally[5], gain, hidden, grad_out, own_out, *outs, *outs[3:6])
    partial = jnp.sum(lax.all_to_all(partial, "seq", 0, 0, tiled=True), axis=0)
    partial = partial + lax.ppermute(partial, AXES, xor_perm("c", 1))
    near = [lax.ppermute(partial, AXES, xor_perm("x", d)) for d in (1, 2)]
    partial, *grads[1:5] = after(partial, *grads[1:5])
    partial = (partial + near[0]) + (near[1] + lax.ppermute(partial, AXES, xor_perm("x", 3)))
    partial, *rest = after(partial, *rest)
    grads += [ring_permute(b, s, m) for b, (s, m) in zip(rest, late)]
    once = lambda rows: pl.BlockSpec((rows, WIDE), lambda c: (0, c))
    fixed = lambda *shape: pl.BlockSpec(shape, lambda c: (0,) * len(shape))
    early, last = 5 * ROWS, 3 * ROWS
    begin, partial = after(pack, partial)
    part, sums = pl.pallas_call(
        half_kernel,
        grid=(STEPS,),
        out_shape=(
            jax.ShapeDtypeStruct((TOK, D), F32),
            jax.ShapeDtypeStruct((TOK, 128), F32),
        ),
        in_specs=[
            fixed(1, early),
            fixed(TOK, 8),
            fixed(TOK, 1),
            fixed(TOK, EXPERTS),
            once(EXPERTS),
            once(1),
            once(TOK),
            once(TOK),
        ]
        + [once(ROWS)] * 5,
        out_specs=(once(TOK), fixed(TOK, 128)),
        scratch_shapes=[pltpu.VMEM((TOK, 2 * early + 6 * EXPERTS), BF16)],
        compiler_params=params(60),
        cost_estimate=pl.CostEstimate(
            flops=10_000_000_000, bytes_accessed=30_000_000, transcendentals=0
        ),
    )(early_slots, begin, inv, logit, router_weight, gain, hidden, grad_out, *grads[:5])
    partial, sums = after(partial, sums)
    router_grad = lax.all_gather(partial, "seq").reshape(EXPERTS, D)

    grad_hidden = pl.pallas_call(
        last_kernel,
        grid=(2, STEPS),
        out_shape=jax.ShapeDtypeStruct((TOK, D), BF16),
        in_specs=[
            small(1, last),
            small(TOK, 8),
            small(TOK, 1),
            small(TOK, 128),
            first(1),
            first(TOK),
            first(TOK),
        ]
        + [first(ROWS)] * 3,
        out_specs=second(TOK),
        scratch_shapes=[
            pltpu.VMEM((TOK, D), F32),
            pltpu.VMEM((TOK, D), BF16),
            pltpu.VMEM((TOK, 2 * last), BF16),
            pltpu.VMEM((TOK, 128), F32),
            pltpu.VMEM((TOK, 128), F32),
        ],
        compiler_params=params(60),
    )(late_slots, pack, inv, sums, gain, part, hidden, *grads[5:])
    return grad_hidden, router_grad


def solution(mesh):
    rows = P(("seq", "exp"), None)
    in_specs = (
        rows,
        rows,
        P(),
        rows,
        P(),
        rows,
        P("seq", "exp", None, None),
        P("seq", "exp", None, None),
    )
    return jax.shard_map(body, mesh=mesh, in_specs=in_specs, out_specs=(rows, P()), check_vma=False)
```
